32 devices in a mesh: dp: 16 (over z, y, core), blk: 2 (over x).
Axes of the slice: x: 2, y: 2, z: 4, core: 2. Of those that a mesh axis runs over, the one named last changes fastest.
Arguments:
- embedded: bfloat16 [65536, 416], P(('dp', 'blk')), may hold values from -6 to 6
- dense_features: bfloat16 [65536, 13], P(('dp', 'blk')), may hold values from -6 to 6
- labels: int32 [65536, 2], P(('dp', 'blk')), may hold values from 0 to 1
- projector: float32 [13, 96], replicated, may hold values from -1.75 to 1.75
- projector_momentum: float32 [13, 96], replicated, may hold values from -0.0012207031 to 0.0012207031
- router: float32 [512, 2], replicated, may hold values from -0.25 to 0.25
- router_momentum: float32 [512, 2], replicated, may hold values from -0.0012207031 to 0.0012207031
- task_router: float32 [2, 128, 2], replicated, may hold values from -2 to 2
- task_router_momentum: float32 [2, 128, 2], replicated, may hold values from -0.0012207031 to 0.0012207031
- expand_one: float32 [2, 512, 256], P('blk'), may hold values from -0.25 to 0.25
- expand_one_momentum: float32 [2, 512, 256], P('blk'), may hold values from -0.0012207031 to 0.0012207031
- shrink_one: float32 [2, 256, 128], P('blk'), may hold values from -0.375 to 0.375
- shrink_one_momentum: float32 [2, 256, 128], P('blk'), may hold values from -0.0012207031 to 0.0012207031
- expand_two: float32 [2, 128, 256], P('blk'), may hold values from -2 to 2
- expand_two_momentum: float32 [2, 128, 256], P('blk'), may hold values from -0.0012207031 to 0.0012207031
- shrink_two: float32 [2, 256, 128], P('blk'), may hold values from -0.375 to 0.375
- shrink_two_momentum: float32 [2, 256, 128], P('blk'), may hold values from -0.0012207031 to 0.0012207031
- tower_hidden: float32 [2, 128, 64], replicated, may hold values from -2 to 2
- tower_hidden_momentum: float32 [2, 128, 64], replicated, may hold values from -0.0012207031 to 0.0012207031
- tower_final: float32 [2, 64], replicated, may hold values from -0.75 to 0.75
- tower_final_moment: float32 [2, 64], replicated, may hold values from -0.0017089844 to 0.0017089844
- tower_final_square: float32 [2, 64], replicated, may hold values from 5.0354004e-08 to 1.9836426e-07
Outputs:
- task_logits: float32 [65536, 2], P(('dp', 'blk'))
- embedded_grad: float32 [65536, 416], P(('dp', 'blk'))
- projector_momentum_next: float32 [13, 96], replicated
- projector_next: float32 [13, 96], replicated
- router_momentum_next: float32 [512, 2], replicated
- router_next: float32 [512, 2], replicated
- task_router_momentum_next: float32 [2, 128, 2], replicated
- task_router_next: float32 [2, 128, 2], replicated
- expand_one_momentum_next: float32 [2, 512, 256], P('blk')
- expand_one_next: float32 [2, 512, 256], P('blk')
- shrink_one_momentum_next: float32 [2, 256, 128], P('blk')
- shrink_one_next: float32 [2, 256, 128], P('blk')
- expand_two_momentum_next: float32 [2, 128, 256], P('blk')
- expand_two_next: float32 [2, 128, 256], P('blk')
- shrink_two_momentum_next: float32 [2, 256, 128], P('blk')
- shrink_two_next: float32 [2, 256, 128], P('blk')
- tower_hidden_momentum_next: float32 [2, 128, 64], replicated
- tower_hidden_next: float32 [2, 128, 64], replicated
- tower_final_moment_next: float32 [2, 64], replicated
- tower_final_square_next: float32 [2, 64], replicated
- tower_final_next: float32 [2, 64], replicated
The draws below stay inside these ranges and needn't reach their ends.
All inputs are finite; a program needn't handle non-finite values.
Results may differ from the reference program's by a relative error of at most 0.0075.
The reference program's roundings to bfloat16 on the way count: a program that leaves them out, or rounds other values in their place, can miss the bound.
Values may be sent and summed in bfloat16 or wider, within the bound.
A program may use at most 128 MiB of HBM per device.

```python
import math
import jax
import jax.numpy as jnp
from jax import lax

EMB = 416
DENSE = 13
PROJ = 96
D_IN = 512
HIDDEN_ONE = 256
OUT = 128
HIDDEN_TWO = 256
TOWER = 64
TASKS = 2
EXPERTS = 2
TOKENS = 65536
STEP = 5


def set_ends(drawn, key, low, largest):
    place = [jax.random.randint(jax.random.fold_in(key, axis), (), 0, length) for axis, length in enumerate(drawn.shape)]
    widest = drawn.shape.index(max(drawn.shape))
    beside = place[:widest] + [(place[widest] + 1) % drawn.shape[widest]] + place[widest + 1:]
    return drawn.at[tuple(place)].set(low).at[tuple(beside)].set(largest)


def steps_of(rng, dims, cuts, least, largest):
    factor_of = 1.0
    for position, shards_of in cuts:
        steps = jax.random.uniform(jax.random.fold_in(jax.random.fold_in(rng, 6), position), (shards_of,), jnp.float32, least / len(cuts), largest / len(cuts))
        factor_of = factor_of * jnp.repeat(jnp.exp(steps), dims[position] // shards_of).reshape((-1,) + (1,) * (len(dims) - 1 - position))
    return factor_of


def gaussian(key, dims, width, limit, cuts=(), kind=jnp.bfloat16):
    entries = width * jax.random.normal(key, dims, jnp.float32)
    if cuts:
        entries = entries * steps_of(key, dims, cuts, -0.22, 0.18)
    return jnp.clip(entries, -limit, limit).astype(kind)


def setup_inputs(seed: int = 0) -> dict:
    arg_keys = jax.random.split(jax.random.key(seed), 23)
    return {
        "embedded": gaussian(arg_keys[0], (TOKENS, EMB), 1.0, 6.0, ((0, 32),)),
        "dense_features": gaussian(arg_keys[1], (TOKENS, DENSE), 1.0, 6.0, ((0, 32),)),
        "labels": set_ends(jax.random.randint(arg_keys[2], (TOKENS, TASKS), 0, 2), jax.random.fold_in(arg_keys[2], 1), 0, 1).astype(jnp.int32),
        "projector": gaussian(arg_keys[3], (DENSE, PROJ), DENSE ** -0.5, 1.75, (), jnp.float32),
        "projector_momentum": gaussian(arg_keys[4], (DENSE, PROJ), (0.02 / TOKENS ** 0.5), 0.0012207031, (), jnp.float32),
        "router": gaussian(arg_keys[5], (D_IN, EXPERTS), D_IN ** -0.5, 0.25, (), jnp.float32),
        "router_momentum": gaussian(arg_keys[6], (D_IN, EXPERTS), (0.02 / TOKENS ** 0.5), 0.0012207031, (), jnp.float32),
        "task_router": gaussian(arg_keys[7], (TASKS, OUT, EXPERTS), (OUT // 16) ** -0.5, 2.0, (), jnp.float32),
        "task_router_momentum": gaussian(arg_keys[8], (TASKS, OUT, EXPERTS), (0.02 / TOKENS ** 0.5), 0.0012207031, (), jnp.float32),
        "expand_one": gaussian(arg_keys[9], (EXPERTS, D_IN, HIDDEN_ONE), D_IN ** -0.5, 0.25, ((0, 2),), jnp.float32),
        "expand_one_momentum": gaussian(arg_keys[10], (EXPERTS, D_IN, HIDDEN_ONE), (0.02 / TOKENS ** 0.5), 0.0012207031, ((0, 2),), jnp.float32),
        "shrink_one": gaussian(arg_keys[11], (EXPERTS, HIDDEN_ONE, OUT), HIDDEN_ONE ** -0.5, 0.375, ((0, 2),), jnp.float32),
        "shrink_one_momentum": gaussian(arg_keys[12], (EXPERTS, HIDDEN_ONE, OUT), (0.02 / TOKENS ** 0.5), 0.0012207031, ((0, 2),), jnp.float32),
        "expand_two": gaussian(arg_keys[13], (EXPERTS, OUT, HIDDEN_TWO), (OUT // 16) ** -0.5, 2.0, ((0, 2),), jnp.float32),
        "expand_two_momentum": gaussian(arg_keys[14], (EXPERTS, OUT, HIDDEN_TWO), (0.02 / TOKENS ** 0.5), 0.0012207031, ((0, 2),), jnp.float32),
        "shrink_two": gaussian(arg_keys[15], (EXPERTS, HIDDEN_TWO, OUT), HIDDEN_TWO ** -0.5, 0.375, ((0, 2),), jnp.float32),
        "shrink_two_momentum": gaussian(arg_keys[16], (EXPERTS, HIDDEN_TWO, OUT), (0.02 / TOKENS ** 0.5), 0.0012207031, ((0, 2),), jnp.float32),
        "tower_hidden": gaussian(arg_keys[17], (TASKS, OUT, TOWER), (OUT // 16) ** -0.5, 2.0, (), jnp.float32),
        "tower_hidden_momentum": gaussian(arg_keys[18], (TASKS, OUT, TOWER), (0.02 / TOKENS ** 0.5), 0.0012207031, (), jnp.float32),
        "tower_final": gaussian(arg_keys[19], (TASKS, TOWER), TOWER ** -0.5, 0.75, (), jnp.float32),
        "tower_final_moment": gaussian(arg_keys[20], (TASKS, TOWER), (0.03 / TOKENS ** 0.5), 0.0017089844, (), jnp.float32),
        "tower_final_square": jnp.clip(jnp.exp(jax.random.uniform(arg_keys[21], (TASKS, TOWER), jnp.float32, math.log(5.035400363340159e-08), math.log(1.9836426190522616e-07))), 5.035400363340159e-08, 1.9836426190522616e-07),
    }


@jax.custom_vjp
def low(v):
    return lax.optimization_barrier(v.astype(jnp.bfloat16)).astype(jnp.float32)

@jax.custom_vjp
def low_back(v):
    return v

def low_keep(v):
    return (low(v), None)

def low_pass(kept, grad):
    return (grad,)

def back_keep(v):
    return (v, None)

def back_low(kept, grad):
    return (low(grad),)
low.defvjp(low_keep, low_pass)
low_back.defvjp(back_keep, back_low)
HIGH = lax.Precision.HIGHEST
NS_A = 3.4445
NS_B = -4.775
NS_C = 2.0315

def product(left, right):
    return jnp.dot(left, right, precision=HIGH)

def expert_apply(inputs, matrix_in, matrix_out):
    pre_act = low_back(product(inputs, low(matrix_in)))
    hidden = low(jax.nn.gelu(pre_act))
    mixed = low_back(product(hidden, low(matrix_out)))
    return jax.nn.gelu(mixed)

def forward(weights, embedded, dense_features, labels):
    projector, router, task_router, expand_one, shrink_one, expand_two, shrink_two, tower_hidden, tower_final = weights
    projected = product(dense_features, low(projector))
    layer_in = low(jnp.concatenate([embedded, projected], axis=1))
    gate_one = jax.nn.softmax(low_back(product(layer_in, low(router))), axis=-1)
    summed = jnp.zeros((layer_in.shape[0], OUT), jnp.float32)
    for expert in range(EXPERTS):
        summed = summed + gate_one[:, expert:expert + 1] * expert_apply(layer_in, expand_one[expert], shrink_one[expert])
    layer_mid = low(summed)
    second_outs = [expert_apply(layer_mid, expand_two[expert], shrink_two[expert]) for expert in range(EXPERTS)]
    total_loss = jnp.float32(0.0)
    logit_list = []
    for task in range(TASKS):
        gate_two = jax.nn.softmax(low_back(product(layer_mid, low(task_router[task]))), axis=-1)
        represent = jnp.zeros((layer_in.shape[0], OUT), jnp.float32)
        for expert in range(EXPERTS):
            represent = represent + gate_two[:, expert:expert + 1] * second_outs[expert]
        tower_pre = low_back(product(low(represent), low(tower_hidden[task])))
        activation = jax.nn.gelu(tower_pre)
        logit = product(activation, tower_final[task])
        target = labels[:, task].astype(jnp.float32)
        total_loss = total_loss + jnp.sum(jax.nn.softplus(logit) - target * logit) / TOKENS
        logit_list.append(logit)
    return (total_loss, jnp.stack(logit_list, axis=1))

def orthogonal(matrix):
    row_count, col_count = matrix.shape
    current = matrix / (jnp.sqrt(jnp.sum(matrix * matrix)) + 1e-07)
    if row_count > col_count:
        current = current.T
    for sweep_index in range(5):
        gram_matrix = jnp.dot(current, current.T, precision=HIGH)
        polynomial = NS_B * gram_matrix + NS_C * jnp.dot(gram_matrix, gram_matrix, precision=HIGH)
        current = NS_A * current + jnp.dot(polynomial, current, precision=HIGH)
    if row_count > col_count:
        current = current.T
    return current

def muon_update(weight, momentum, gradient):
    renewed = 0.5 * momentum + gradient
    if weight.ndim == 3:
        ortho = jax.vmap(orthogonal)(renewed)
    else:
        ortho = orthogonal(renewed)
    scale = 0.2 * math.sqrt(max(weight.shape[-2], weight.shape[-1]))
    return (renewed, weight * (1.0 - 0.2 * 0.1) - 0.2 * scale * ortho)

def adamw_update(weight, moment, square, gradient):
    moment_next = 0.9 * moment + 0.1 * gradient
    square_next = 0.95 * square + 0.05 * gradient * gradient
    corrected = moment_next / (1.0 - 0.9 ** STEP)
    denom = jnp.sqrt(square_next / (1.0 - 0.95 ** STEP)) + 1e-08
    return (moment_next, square_next, weight * (1.0 - 0.0005) - 0.25 * corrected / denom)

def reference(embedded, dense_features, labels, projector, projector_momentum, router, router_momentum, task_router, task_router_momentum, expand_one, expand_one_momentum, shrink_one, shrink_one_momentum, expand_two, expand_two_momentum, shrink_two, shrink_two_momentum, tower_hidden, tower_hidden_momentum, tower_final, tower_final_moment, tower_final_square):
    weights = (projector, router, task_router, expand_one, shrink_one, expand_two, shrink_two, tower_hidden, tower_final)
    block = math.gcd(TOKENS, 4096)
    count = TOKENS // block
    emb_blocks = embedded.astype(jnp.float32).reshape(count, block, EMB)
    dense_blocks = dense_features.astype(jnp.float32).reshape(count, block, DENSE)
    label_blocks = labels.reshape(count, block, TASKS)

    def block_step(totals, item):
        emb_part, dense_part, label_part = item

        def loss_of(params, emb_values):
            return forward(params, emb_values, dense_part, label_part)
        loss_value, pull, logits = jax.vjp(loss_of, weights, emb_part, has_aux=True)
        weight_grads, emb_grad = pull(jnp.float32(1.0))
        totals = jax.tree.map(lambda first, second: first + second, totals, weight_grads)
        return (totals, (emb_grad, logits))
    zeros = jax.tree.map(jnp.zeros_like, weights)
    grads, (emb_grads, logit_blocks) = lax.scan(block_step, zeros, (emb_blocks, dense_blocks, label_blocks))
    embedded_grad = emb_grads.reshape(TOKENS, EMB)
    task_logits = logit_blocks.reshape(TOKENS, TASKS)
    g_proj, g_router, g_task, g_e1, g_s1, g_e2, g_s2, g_tower, g_final = grads
    outs_proj = muon_update(projector, projector_momentum, g_proj)
    outs_router = muon_update(router, router_momentum, g_router)
    outs_task = muon_update(task_router, task_router_momentum, g_task)
    outs_e1 = muon_update(expand_one, expand_one_momentum, g_e1)
    outs_s1 = muon_update(shrink_one, shrink_one_momentum, g_s1)
    outs_e2 = muon_update(expand_two, expand_two_momentum, g_e2)
    outs_s2 = muon_update(shrink_two, shrink_two_momentum, g_s2)
    outs_tower = muon_update(tower_hidden, tower_hidden_momentum, g_tower)
    outs_final = adamw_update(tower_final, tower_final_moment, tower_final_square, g_final)
    return (task_logits, embedded_grad, outs_proj[0], outs_proj[1], outs_router[0], outs_router[1], outs_task[0], outs_task[1], outs_e1[0], outs_e1[1], outs_s1[0], outs_s1[1], outs_e2[0], outs_e2[1], outs_s2[0], outs_s2[1], outs_tower[0], outs_tower[1], outs_final[0], outs_final[1], outs_final[2])
```

```python
import functools
import math

import jax
import jax.numpy as jnp
from jax import lax
from jax.experimental import pallas as pl
from jax.experimental.pallas import tpu as pltpu
from jax.sharding import PartitionSpec as P

STEP = 5
NS_A = 3.4445
NS_B = -4.775
NS_C = 2.0315
C0 = math.sqrt(2.0 / math.pi)
C1 = C0 * 0.044715
LOW = jnp.bfloat16
F32 = jnp.float32
CODE = jnp.int16
MESH = pl.DeviceIdType.MESH
MIB = 2**20
PAD = 16
LANES = 128


def mm(a, b):
    return lax.dot_general(a, b, (((1,), (0,)), ((), ())), preferred_element_type=F32)


def mm_nt(a, b):
    return lax.dot_general(a, b, (((1,), (1,)), ((), ())), preferred_element_type=F32)


def gelu(x):
    square = x * x
    half = 0.5 * jnp.tanh(x * (C0 + C1 * square)) + 0.5
    value = x * half
    slope = half + (value - value * half) * (2.0 * C0 + 6.0 * C1 * square)
    return value, slope


def softmax_rows(logits):
    shifted = jnp.exp(logits - jnp.max(logits, axis=0, keepdims=True))
    return shifted / jnp.sum(shifted, axis=0, keepdims=True)


def stack_rows(rows, height):
    width = rows[0].shape[1]
    index = lax.broadcasted_iota(jnp.int32, (height, width), 0)
    out = jnp.zeros((height, width), F32)
    for i, row in enumerate(rows):
        out = jnp.where(index == i, row, out)
    return out


def pad_to(value, rows, columns):
    if value.shape[1] < columns:
        fill = jnp.zeros((value.shape[0], columns - value.shape[1]), F32)
        value = jnp.concatenate([value, fill], axis=1)
    if value.shape[0] < rows:
        fill = jnp.zeros((rows - value.shape[0], columns), F32)
        value = jnp.concatenate([value, fill], axis=0)
    return value


def encode(v):
    top = jnp.max(jnp.abs(v), axis=0, keepdims=True)
    power = jnp.ceil(jnp.log2(jnp.maximum(top, 1e-30)))
    whole = jnp.round(v * (16000.0 * jnp.exp2(-power))).astype(jnp.int32)
    row = lax.broadcasted_iota(jnp.int32, v.shape, 0) & 7
    bit = ((power.astype(jnp.int32) + 128) >> row) & 1
    return (2 * whole + bit).astype(CODE)


def decode(code):
    v = code.astype(jnp.int32)
    bit = v & 1
    row = lax.broadcasted_iota(jnp.int32, v.shape, 0) & 7
    power = jnp.sum((bit << row).astype(F32)[0:8], axis=0, keepdims=True) - 128.0
    return (v - bit).astype(F32) * (jnp.exp2(power) * (1.0 / 32000.0))


def weights_kernel(e1_ref, s1_ref, e2_ref, s2_ref, all_ref, send, recv, send_core, recv_core):
    blk = lax.axis_size("blk")
    dp, me = lax.axis_index("dp"), lax.axis_index("blk")
    core = lax.rem(dp, 2)
    sibling = dp + 1 - 2 * core
    rows = all_ref.shape[1]
    half = rows // 2

    barrier = pltpu.get_barrier_semaphore()
    for step in range(1, blk):
        peer = lax.rem(me + step, blk)
        pl.semaphore_signal(barrier, inc=1, device_id=(dp, peer), device_id_type=MESH)
    pl.semaphore_signal(barrier, inc=1, device_id=(sibling, me), device_id_type=MESH)
    din, out = e1_ref.shape[1], e2_ref.shape[1]
    all_ref[me, 0:din, :] = e1_ref[0].astype(LOW)
    all_ref[me, din : din + out, :] = e2_ref[0].astype(LOW)
    all_ref[me, din + out :, 0:out] = s1_ref[0].astype(LOW)
    all_ref[me, din + out :, out : 2 * out] = s2_ref[0].astype(LOW)
    pl.semaphore_wait(barrier, blk)

    mine = pl.ds(pl.multiple_of(core * half, 16), half)
    copies = []
    for step in range(1, blk):
        peer = lax.rem(me + step, blk)
        copy = pltpu.make_async_remote_copy(
            src_ref=all_ref.at[me, mine],
            dst_ref=all_ref.at[me, mine],
            send_sem=send.at[step],
            recv_sem=recv.at[step],
            device_id=(dp, peer),
            device_id_type=MESH,
        )
        copy.start()
        copies.append(copy)
    forwards = []
    for step in range(1, blk):
        source = lax.rem(me - step + blk, blk)
        copies[step - 1].wait_recv()
        copy = pltpu.make_async_remote_copy(
            src_ref=all_ref.at[source, mine],
            dst_ref=all_ref.at[source, mine],
            send_sem=send_core.at[step],
            recv_sem=recv_core.at[step],
            device_id=(sibling, me),
            device_id_type=MESH,
        )
        copy.start()
        forwards.append(copy)
    for copy in copies:
        copy.wait_send()
    for copy in forwards:
        copy.wait()


def gather_weights(blk, e1, s1, e2, s2):
    rows = e1.shape[1] + e2.shape[1] + s1.shape[1]
    return pl.pallas_call(
        weights_kernel,
        out_shape=jax.ShapeDtypeStruct((blk, rows, e1.shape[2]), LOW),
        in_specs=[pl.BlockSpec(memory_space=pltpu.VMEM)] * 4,
        out_specs=pl.BlockSpec(memory_space=pltpu.VMEM),
        scratch_shapes=[pltpu.SemaphoreType.DMA((blk,)) for _ in range(4)],
        compiler_params=pltpu.CompilerParams(
            collective_id=0, has_side_effects=True, vmem_limit_bytes=16 * MIB
        ),
    )(e1, s1, e2, s2)


def compute_kernel(
    total,
    emb_ref,
    dense_ref,
    labels_ref,
    proj_ref,
    router_ref,
    task_ref,
    tower_ref,
    final_ref,
    all_ref,
    logit_ref,
    emb_grad_ref,
    grads_ref,
    a1,
    a2,
    b1,
    b2,
    s1t,
    s2t,
    s1n,
    s2n,
    tow,
    tow_n,
    fin,
    projt,
    col1,
    col2,
    x_ref,
    d1,
    d2,
    hid1,
    hid2,
    dtp,
    acc_r,
    acc_t,
    acc_p,
    acc_tow,
    acc_f,
):
    experts, h = all_ref.shape[0], all_ref.shape[2]
    tasks, th, out = tower_ref.shape
    emb, tile = emb_ref.shape
    din = router_ref.shape[1]
    eh = experts * h
    repeat = tile // LANES
    step = pl.program_id(0)
    side = din + 3 * out

    def wide(column):
        return jnp.concatenate([column] * repeat, axis=1)

    @pl.when(step == 0)
    def _():
        for e in range(experts):
            span = slice(e * h, (e + 1) * h)
            e1 = all_ref[e, 0:din, :]
            e2 = all_ref[e, din : din + out, :]
            s1 = all_ref[e, din + out :, 0:out]
            s2 = all_ref[e, din + out :, out : 2 * out]
            a1[span, :] = e1.T
            a2[span, :] = e2.T
            b1[:, span] = e1
            b2[:, span] = e2
            s1t[e] = s1.T
            s2t[e] = s2.T
            s1n[e] = s1
            s2n[e] = s2
        router = stack_rows([router_ref[e : e + 1, :] for e in range(experts)], PAD).astype(LOW)
        a1[eh:, :] = router
        router_t = pad_to(router.astype(F32), LANES, din).T
        pairs = [task_ref[t, e : e + 1, :] for t in range(tasks) for e in range(experts)]
        task = stack_rows(pairs, PAD).astype(LOW)
        a2[eh:, :] = task
        task_t = pad_to(task.astype(F32), LANES, out).T
        for e in range(experts):
            col1[e] = jnp.broadcast_to(router_t[:, e : e + 1], (din, LANES))
        for k in range(tasks * experts):
            col2[k] = jnp.broadcast_to(task_t[:, k : k + 1], (out, LANES))
        tow_n[...] = jnp.zeros_like(tow_n)
        final_t = stack_rows([final_ref[t : t + 1, :] for t in range(tasks)], 8).T
        for t in range(tasks):
            tow[t] = tower_ref[t].astype(LOW)
            tow_n[t * out : (t + 1) * out, t * th : (t + 1) * th] = tower_ref[t].T.astype(LOW)
            fin[t] = jnp.broadcast_to(final_t[:, t : t + 1], (th, LANES))
        projt[...] = proj_ref[...].T.astype(LOW)
        grads_ref[...] = jnp.zeros_like(grads_ref)
        acc_r[...] = jnp.zeros_like(acc_r)
        acc_t[...] = jnp.zeros_like(acc_t)
        acc_p[...] = jnp.zeros_like(acc_p)
        acc_tow[...] = jnp.zeros_like(acc_tow)
        acc_f[...] = jnp.zeros_like(acc_f)

    x_ref[0:emb, :] = emb_ref[...]
    x_ref[emb:, :] = mm(projt[...], dense_ref[...]).astype(LOW)
    x = x_ref[...]
    pre1 = mm(a1[...], x)
    gate1 = softmax_rows(pre1[eh : eh + experts, :])
    mid = jnp.zeros((out, tile), F32)
    slope1, mslope1, outs1 = [], [], []
    for e in range(experts):
        value, slope = gelu(pre1[e * h : (e + 1) * h, :])
        hid1[e] = value.astype(LOW)
        slope1.append(slope)
        mixed, mslope = gelu(mm(s1t[e], hid1[e]))
        outs1.append(mixed)
        mslope1.append(mslope)
        mid = mid + gate1[e : e + 1, :] * mixed
    mid = mid.astype(LOW)

    pre2 = mm(a2[...], mid)
    gate2 = []
    for t in range(tasks):
        first = eh + t * experts
        gate2.append(softmax_rows(pre2[first : first + experts, :]))
    slope2, mslope2, outs2 = [], [], []
    rep = [jnp.zeros((out, tile), F32) for _ in range(tasks)]
    for e in range(experts):
        value, slope = gelu(pre2[e * h : (e + 1) * h, :])
        hid2[e] = value.astype(LOW)
        slope2.append(slope)
        mixed, mslope = gelu(mm(s2t[e], hid2[e]))
        outs2.append(mixed)
        mslope2.append(mslope)
        for t in range(tasks):
            rep[t] = rep[t] + gate2[t][e : e + 1, :] * mixed

    for t in range(tasks):
        rep_low = rep[t].astype(LOW)
        act, tslope = gelu(mm(tow[t], rep_low))
        weight = wide(fin[t])
        logit = jnp.sum(act * weight, axis=0, keepdims=True)
        logit_ref[t : t + 1, :] = logit
        d_logit = (jax.nn.sigmoid(logit) - labels_ref[t : t + 1, :].astype(F32)) / total
        part = act * d_logit
        lump = part[:, 0:LANES]
        for k in range(1, repeat):
            lump = lump + part[:, k * LANES : (k + 1) * LANES]
        acc_f[t] += lump
        d_tp = (tslope * (d_logit * weight)).astype(LOW)
        dtp[t * th : (t + 1) * th, :] = d_tp
        acc_tow[t] += mm_nt(d_tp, rep_low)
    d_rep = mm(tow_n[...], dtp[...])

    d_gate2 = [[None] * experts for _ in range(tasks)]
    for e in range(experts):
        d_out = jnp.zeros((out, tile), F32)
        for t in range(tasks):
            piece = d_rep[t * out : (t + 1) * out, :]
            d_out = d_out + gate2[t][e : e + 1, :] * piece
            d_gate2[t][e] = jnp.sum(outs2[e] * piece, axis=0, keepdims=True)
        d_mixed = (mslope2[e] * d_out).astype(LOW)
        grads_ref[e, :, din + 2 * out : side] += mm_nt(hid2[e], d_mixed)
        d2[e * h : (e + 1) * h, :] = (slope2[e] * mm(s2n[e], d_mixed)).astype(LOW)
    rows = []
    for t in range(tasks):
        inner = sum(gate2[t][e : e + 1, :] * d_gate2[t][e] for e in range(experts))
        for e in range(experts):
            row = gate2[t][e : e + 1, :] * (d_gate2[t][e] - inner)
            rows.append(row.astype(LOW).astype(F32))
    d2[eh:, :] = stack_rows(rows, PAD).astype(LOW)
    g2 = mm_nt(d2[...], mid)
    for e in range(experts):
        grads_ref[e, :, din + out : din + 2 * out] += g2[e * h : (e + 1) * h, :]
    acc_t[...] += g2[eh:, :]
    d_mid = mm(b2[...], d2[0:eh, :])
    for k, row in enumerate(rows):
        d_mid = d_mid + wide(col2[k]) * row

    d_gate1 = []
    for e in range(experts):
        d_gate1.append(jnp.sum(outs1[e] * d_mid, axis=0, keepdims=True))
        d_mixed = (mslope1[e] * (gate1[e : e + 1, :] * d_mid)).astype(LOW)
        grads_ref[e, :, din : din + out] += mm_nt(hid1[e], d_mixed)
        d1[e * h : (e + 1) * h, :] = (slope1[e] * mm(s1n[e], d_mixed)).astype(LOW)
    inner = sum(gate1[e : e + 1, :] * d_gate1[e] for e in range(experts))
    rows = []
    for e in range(experts):
        row = gate1[e : e + 1, :] * (d_gate1[e] - inner)
        rows.append(row.astype(LOW).astype(F32))
    d1[eh:, :] = stack_rows(rows, PAD).astype(LOW)
    g1 = mm_nt(d1[...], x)
    for e in range(experts):
        grads_ref[e, :, 0:din] += g1[e * h : (e + 1) * h, :]
    acc_r[...] += g1[eh:, :]
    d_in = mm(b1[...], d1[0:eh, :])
    for e in range(experts):
        d_in = d_in + wide(col1[e]) * rows[e]
    emb_grad_ref[...] = d_in[:emb, :]
    tail = d_in[emb:, :]
    high = tail.astype(LOW)
    rest = (tail - high.astype(F32)).astype(LOW)
    acc_p[...] += mm_nt(dense_ref[...], high) + mm_nt(dense_ref[...], rest)

    @pl.when(step == pl.num_programs(0) - 1)
    def _():
        finals = [jnp.sum(acc_f[t].T, axis=0, keepdims=True) for t in range(tasks)]
        pieces = [acc_tow[t] for t in range(tasks)]
        pieces += [acc_r[:, k * out : (k + 1) * out] for k in range(din // out)]
        pieces += [acc_t[...], pad_to(acc_p[...], PAD, out)]
        pieces += [pad_to(stack_rows(finals, PAD), PAD, out)]
        at = 0
        for piece in pieces:
            for e in range(experts):
                grads_ref[e, at : at + piece.shape[0], side:] = piece
            at += piece.shape[0]


def compute(total, emb, dense, labels, proj, router, task, tower, final, everything):
    experts, _, h = everything.shape
    tasks, th, out = tower.shape
    width, rows = emb.shape
    din = router.shape[1]
    eh = experts * h
    tile = min(rows, max(LANES, 2048 // experts))

    def full(a):
        return pl.BlockSpec(a.shape, lambda i, n=a.ndim: (0,) * n)

    def part(height):
        return pl.BlockSpec((height, tile), lambda i: (0, i))

    scratch = [
        ((eh + PAD, din), LOW),
        ((eh + PAD, out), LOW),
        ((din, eh), LOW),
        ((out, eh), LOW),
        ((experts, out, h), LOW),
        ((experts, out, h), LOW),
        ((experts, h, out), LOW),
        ((experts, h, out), LOW),
        ((tasks, th, out), LOW),
        ((tasks * out, tasks * th), LOW),
        ((tasks, th, LANES), F32),
        ((proj.shape[1], proj.shape[0]), LOW),
        ((experts, din, LANES), F32),
        ((tasks * experts, out, LANES), F32),
        ((din, tile), LOW),
        ((eh + PAD, tile), LOW),
        ((eh + PAD, tile), LOW),
        ((experts, h, tile), LOW),
        ((experts, h, tile), LOW),
        ((tasks * th, tile), LOW),
        ((PAD, din), F32),
        ((PAD, out), F32),
        (proj.shape, F32),
        ((tasks, th, out), F32),
        ((tasks, th, LANES), F32),
    ]
    small = (proj, router, task, tower, final, everything)
    return pl.pallas_call(
        functools.partial(compute_kernel, total),
        grid=(rows // tile,),
        in_specs=[part(width), part(dense.shape[0]), part(tasks)] + [full(a) for a in small],
        out_specs=[
            part(tasks),
            part(width),
            pl.BlockSpec((experts, h, din + 4 * out), lambda i: (0, 0, 0)),
        ],
        out_shape=[
            jax.ShapeDtypeStruct((tasks, rows), F32),
            jax.ShapeDtypeStruct(emb.shape, F32),
            jax.ShapeDtypeStruct((experts, h, din + 4 * out), F32),
        ],
        scratch_shapes=[pltpu.VMEM(shape, kind) for shape, kind in scratch],
        compiler_params=pltpu.CompilerParams(vmem_limit_bytes=56 * MIB),
    )(emb, dense, labels, *small)


def reduce_kernel(
    grads_ref,
    full_ref,
    pair_out,
    pair_in,
    pieces,
    landed,
    gathered,
    pair_sem,
    send,
    recv,
    spread_send,
    spread_recv,
    core_send,
    core_recv,
):
    blk, devices = lax.axis_size("blk"), lax.axis_size("dp")
    chips = devices // 2
    dp, me = lax.axis_index("dp"), lax.axis_index("blk")
    core = lax.rem(dp, 2)
    chip = lax.div(dp, 2)
    sibling = dp + 1 - 2 * core
    height, columns = pieces.shape[1:]
    half = grads_ref.shape[1] // 2
    blocks = half // height
    slots = blk * chips
    own = me * chips + chip

    def place(k):
        return (lax.rem(k, blocks) * height, lax.div(k, blocks) * columns)

    def peer(step):
        to = lax.rem(own + step, slots)
        return to, (lax.rem(to, chips) * 2 + core, lax.div(to, chips))

    def source(step):
        return lax.rem(own - step + slots, slots)

    barrier = pltpu.get_barrier_semaphore()

    def greet(step, unused):
        pl.semaphore_signal(barrier, inc=1, device_id=peer(step)[1], device_id_type=MESH)
        return unused

    lax.fori_loop(1, slots, greet, 0)
    pl.semaphore_signal(barrier, inc=1, device_id=(sibling, me), device_id_type=MESH)

    other = (1 - core) * half
    first = core * half
    for e in range(blk):

        def code(j, unused, e=e):
            at = pl.multiple_of(other + j * PAD, PAD)
            to = pl.ds(pl.multiple_of(j * PAD, PAD), PAD)
            pair_out[e, to, :] = encode(grads_ref[e, pl.ds(at, PAD), :])
            return unused

        lax.fori_loop(0, half // PAD, code, 0)
    pl.semaphore_wait(barrier, slots)

    pair = pltpu.make_async_remote_copy(
        src_ref=pair_out,
        dst_ref=pair_in,
        send_sem=pair_sem.at[0],
        recv_sem=pair_sem.at[1],
        device_id=(sibling, me),
        device_id_type=MESH,
    )
    pair.start()
    pair.wait_recv()

    def outgoing(step):
        to, device = peer(step)
        return pltpu.make_async_remote_copy(
            src_ref=pieces.at[to],
            dst_ref=landed.at[own],
            send_sem=send.at[step],
            recv_sem=recv.at[step],
            device_id=device,
            device_id_type=MESH,
        )

    def prepare(to):
        e = lax.div(to, chips)
        row, column = place(lax.rem(to, chips))
        row = pl.multiple_of(row, height)
        span = pl.ds(pl.multiple_of(column, LANES), columns)
        mine = grads_ref[e, pl.ds(pl.multiple_of(first + row, height), height), span]
        return encode(mine + decode(pair_in[e, pl.ds(row, height), span]))

    def ship(step, unused):
        to = peer(step)[0]
        pieces[to] = prepare(to)
        outgoing(step).start()
        return unused

    lax.fori_loop(1, slots, ship, 0)
    landed[own] = prepare(own)

    def arrive(step, unused):
        outgoing(step).wait_recv()
        return unused

    lax.fori_loop(1, slots, arrive, 0)

    def add(slot, partial):
        return partial + decode(landed[slot])

    summed = lax.fori_loop(0, slots, add, jnp.zeros((height, columns), F32))

    def where(k, c):
        row, column = place(k)
        row = pl.multiple_of(c * half + row, height)
        return pl.ds(row, height), pl.ds(pl.multiple_of(column, LANES), columns)

    rows_own, columns_own = where(chip, core)
    gathered[rows_own, columns_own] = encode(summed)

    def spread(step):
        to = lax.rem(chip + step, chips)
        return pltpu.make_async_remote_copy(
            src_ref=gathered.at[rows_own, columns_own],
            dst_ref=gathered.at[rows_own, columns_own],
            send_sem=spread_send.at[step],
            recv_sem=spread_recv.at[step],
            device_id=(to * 2 + core, me),
            device_id_type=MESH,
        )

    def forward(step):
        rows, span = where(lax.rem(chip - step + chips, chips), core)
        return pltpu.make_async_remote_copy(
            src_ref=gathered.at[rows, span],
            dst_ref=gathered.at[rows, span],
            send_sem=core_send.at[step],
            recv_sem=core_recv.at[step],
            device_id=(sibling, me),
            device_id_type=MESH,
        )

    def spread_start(step, unused):
        spread(step).start()
        return unused

    lax.fori_loop(1, chips, spread_start, 0)
    forward(0).start()

    def pass_on(step, unused):
        spread(step).wait_recv()
        forward(step).start()
        return unused

    lax.fori_loop(1, chips, pass_on, 0)

    def finish(step, unused):
        forward(step).wait()
        return unused

    lax.fori_loop(0, chips, finish, 0)

    def write(j, unused):
        at = pl.ds(pl.multiple_of(j * PAD, PAD), PAD)
        full_ref[at, :] = decode(gathered[at, :])
        return unused

    lax.fori_loop(0, full_ref.shape[0] // PAD, write, 0)

    pair.wait_send()

    def drain(step, unused):
        outgoing(step).wait_send()
        return unused

    lax.fori_loop(1, slots, drain, 0)

    def drain_spread(step, unused):
        spread(step).wait_send()
        return unused

    lax.fori_loop(1, chips, drain_spread, 0)


def reduce_gradients(blk, devices, grads):
    _, h, width = grads.shape
    chips = devices // 2
    blocks = h // 2 // PAD
    columns = width * blocks // chips
    slots = blk * chips
    dma = pltpu.SemaphoreType.DMA
    return pl.pallas_call(
        reduce_kernel,
        out_shape=jax.ShapeDtypeStruct((h, width), F32),
        in_specs=[pl.BlockSpec(memory_space=pltpu.VMEM)],
        out_specs=pl.BlockSpec(memory_space=pltpu.VMEM),
        scratch_shapes=[
            pltpu.VMEM((blk, h // 2, width), CODE),
            pltpu.VMEM((blk, h // 2, width), CODE),
            pltpu.VMEM((slots, PAD, columns), CODE),
            pltpu.VMEM((slots, PAD, columns), CODE),
            pltpu.VMEM((h, width), CODE),
            dma((2,)),
            dma((slots,)),
            dma((slots,)),
            dma((chips,)),
            dma((chips,)),
            dma((chips,)),
            dma((chips,)),
        ],
        compiler_params=pltpu.CompilerParams(
            collective_id=1, has_side_effects=True, vmem_limit_bytes=32 * MIB
        ),
    )(grads)


def halves(value):
    high = value.astype(LOW)
    return high, (value - high.astype(F32)).astype(LOW)


def gram(value):
    high, rest = halves(value)
    return mm_nt(
        jnp.concatenate([high, high, rest], axis=1), jnp.concatenate([high, rest, high], axis=1)
    )


def times(left, right):
    high, rest = halves(left)
    up, down = halves(right)
    return mm(jnp.concatenate([high, high, rest], axis=1), jnp.concatenate([up, down, up], axis=0))


def unit(matrix):
    return matrix / (jnp.sqrt(jnp.sum(matrix * matrix)) + 1e-07)


def orthogonal(matrices, masks):
    current = list(matrices)
    number = range(len(current))
    for _ in range(5):
        grams = [gram(x) for x in current]
        grams = [g if m is None else g * m for g, m in zip(grams, masks)]
        squares = [times(g, g) for g in grams]
        polys = [NS_B * g + NS_C * s for g, s in zip(grams, squares)]
        current = [NS_A * current[i] + times(polys[i], current[i]) for i in number]
    return current


def update_kernel(*refs):
    full_ref, refs = refs[0], refs[1:]
    weights, momenta = refs[0:8], refs[8:16]
    final, moment, square = refs[16:19]
    next_momenta, next_weights = refs[19:27], refs[27:35]
    moment_next, square_next, final_next = refs[35:38]
    proj, router, task, e1, s1, e2, s2, tower = range(8)
    din, h = weights[e1].shape[1:]
    out = weights[s1].shape[2]
    tasks, th, _ = weights[tower].shape
    experts = weights[router].shape[0]
    side = din + 3 * out

    def renew(which, at, gradient):
        value = 0.5 * momenta[which][at] + gradient
        next_momenta[which][at] = value
        return value

    def settle(which, at, ortho):
        weight = weights[which][at]
        scale = 0.2 * math.sqrt(max(weight.shape))
        next_weights[which][at] = weight * (1.0 - 0.2 * 0.1) - 0.2 * scale * ortho

    m_e1 = renew(e1, 0, full_ref[:, 0:din].T)
    m_s1 = renew(s1, 0, full_ref[:, din : din + out])
    m_e2 = renew(e2, 0, full_ref[:, din + out : din + 2 * out].T)
    m_s2 = renew(s2, 0, full_ref[:, din + 2 * out : side])

    stacked, owner = [], []
    at = 0
    for t in range(tasks):
        m_tower = renew(tower, t, full_ref[at : at + th, side:])
        stacked.append(unit(m_tower))
        owner += [th]
        at += th
    router_rows = []
    for k in range(din // out):
        router_rows.append(full_ref[at : at + PAD, side:])
        at += PAD
    m_router = renew(router, slice(None), jnp.concatenate(router_rows, axis=1)[0:experts, :])
    small = full_ref[at : at + PAD, side:]
    for t in range(tasks):
        m_task = renew(task, t, small[t * experts : (t + 1) * experts, :])
        stacked.append(pad_to(unit(m_task), 8, out))
        owner += [8]
    at += PAD
    dense, width = weights[proj].shape
    m_proj = renew(proj, slice(None), full_ref[at : at + PAD, side:][0:dense, 0:width])
    stacked.append(pad_to(unit(m_proj), PAD, out))
    owner += [PAD]
    at += PAD
    grad_final = full_ref[at : at + PAD, side:][0:tasks, 0:th]

    rows = sum(owner)
    down = lax.broadcasted_iota(jnp.int32, (rows, rows), 0)
    across = lax.broadcasted_iota(jnp.int32, (rows, rows), 1)
    mask = jnp.zeros((rows, rows), F32)
    at = 0
    for count in owner:
        inside = (down >= at) & (down < at + count) & (across >= at) & (across < at + count)
        mask = jnp.where(inside, 1.0, mask)
        at += count

    x_e1, x_s1, x_e2, x_s2, x_small, x_router = orthogonal(
        [
            unit(m_e1).T,
            unit(m_s1).T,
            unit(m_e2),
            unit(m_s2).T,
            jnp.concatenate(stacked, axis=0),
            pad_to(unit(m_router), 8, din),
        ],
        [None, None, None, None, mask, None],
    )
    settle(e1, 0, x_e1.T)
    settle(s1, 0, x_s1.T)
    settle(e2, 0, x_e2)
    settle(s2, 0, x_s2.T)
    at = 0
    for t in range(tasks):
        settle(tower, t, x_small[at : at + th, :])
        at += th
    for t in range(tasks):
        settle(task, t, x_small[at : at + experts, :])
        at += 8
    settle(proj, slice(None), x_small[at : at + dense, 0:width])
    settle(router, slice(None), x_router[0:experts, :])

    moment_now = 0.9 * moment[...] + 0.1 * grad_final
    square_now = 0.95 * square[...] + 0.05 * grad_final * grad_final
    corrected = moment_now / (1.0 - 0.9**STEP)
    denom = jnp.sqrt(square_now / (1.0 - 0.95**STEP)) + 1e-08
    moment_next[...] = moment_now
    square_next[...] = square_now
    final_next[...] = final[...] * (1.0 - 0.0005) - 0.25 * corrected / denom


def update(full, weights, momenta, final, moment, square):
    like = [*momenta, *weights, moment, square, final]
    return pl.pallas_call(
        update_kernel,
        out_shape=[jax.ShapeDtypeStruct(a.shape, F32) for a in like],
        compiler_params=pltpu.CompilerParams(vmem_limit_bytes=40 * MIB),
    )(full, *weights, *momenta, final, moment, square)


def on_device(
    embedded,
    dense_features,
    labels,
    projector,
    projector_momentum,
    router,
    router_momentum,
    task_router,
    task_router_momentum,
    expand_one,
    expand_one_momentum,
    shrink_one,
    shrink_one_momentum,
    expand_two,
    expand_two_momentum,
    shrink_two,
    shrink_two_momentum,
    tower_hidden,
    tower_hidden_momentum,
    tower_final,
    tower_final_moment,
    tower_final_square,
):
    devices, blk = lax.axis_size("dp"), lax.axis_size("blk")
    total = embedded.shape[0] * devices * blk

    def turn(a):
        return jnp.swapaxes(a, -1, -2)

    everything = gather_weights(blk, expand_one, shrink_one, expand_two, shrink_two)
    router_t, task_t, tower_t = turn(router), turn(task_router), turn(tower_hidden)
    logits, embedded_grad, grads = compute(
        float(total),
        turn(embedded),
        turn(dense_features),
        turn(labels),
        projector,
        router_t,
        task_t,
        tower_t,
        tower_final,
        everything,
    )
    full = reduce_gradients(blk, devices, grads)
    results = update(
        full,
        [projector, router_t, task_t, expand_one, shrink_one, expand_two, shrink_two, tower_t],
        [
            projector_momentum,
            turn(router_momentum),
            turn(task_router_momentum),
            expand_one_momentum,
            shrink_one_momentum,
            expand_two_momentum,
            shrink_two_momentum,
            turn(tower_hidden_momentum),
        ],
        tower_final,
        tower_final_moment,
        tower_final_square,
    )
    pairs = []
    for which in range(8):
        for value in (results[which], results[8 + which]):
            pairs.append(turn(value) if which in (1, 2, 7) else value)
    return (turn(logits), turn(embedded_grad), *pairs, *results[16:19])


def solution(mesh):
    rows, owned, whole = P(("dp", "blk"), None), P("blk", None, None), P()
    return jax.shard_map(
        on_device,
        mesh=mesh,
        in_specs=(rows,) * 3 + (whole,) * 6 + (owned,) * 8 + (whole,) * 5,
        out_specs=(rows,) * 2 + (whole,) * 6 + (owned,) * 8 + (whole,) * 5,
        check_vma=False,
    )
```

```python
import functools
import math
import types

import jax
import jax.numpy as jnp
from jax import lax
from jax.experimental import pallas as pl
from jax.experimental.pallas import tpu as pltpu
from jax.sharding import PartitionSpec as P

STEP = 5
NS_A = 3.4445
NS_B = -4.775
NS_C = 2.0315
C0 = math.sqrt(2.0 / math.pi)
C1 = C0 * 0.044715
LOW = jnp.bfloat16
F32 = jnp.float32
CODE = jnp.int16
MESH = pl.DeviceIdType.MESH
MIB = 2**20
PAD = 16
LANES = 128


def mm(a, b):
    return lax.dot_general(a, b, (((1,), (0,)), ((), ())), preferred_element_type=F32)


def mm_nt(a, b):
    return lax.dot_general(a, b, (((1,), (1,)), ((), ())), preferred_element_type=F32)


def gelu(x):
    square = x * x
    half = 0.5 * jnp.tanh(x * (C0 + C1 * square)) + 0.5
    value = x * half
    slope = half + (value - value * half) * (2.0 * C0 + 6.0 * C1 * square)
    return value, slope


def softmax_rows(logits):
    shifted = jnp.exp(logits - jnp.max(logits, axis=0, keepdims=True))
    return shifted / jnp.sum(shifted, axis=0, keepdims=True)


def stack_rows(rows, height):
    width = rows[0].shape[1]
    index = lax.broadcasted_iota(jnp.int32, (height, width), 0)
    out = jnp.zeros((height, width), F32)
    for i, row in enumerate(rows):
        out = jnp.where(index == i, row, out)
    return out


def pad_to(value, rows, columns):
    if value.shape[1] < columns:
        fill = jnp.zeros((value.shape[0], columns - value.shape[1]), F32)
        value = jnp.concatenate([value, fill], axis=1)
    if value.shape[0] < rows:
        fill = jnp.zeros((rows - value.shape[0], columns), F32)
        value = jnp.concatenate([value, fill], axis=0)
    return value


def encode(v):
    top = jnp.max(jnp.abs(v), axis=0, keepdims=True)
    power = jnp.ceil(jnp.log2(jnp.maximum(top, 1e-30)))
    whole = jnp.round(v * (16000.0 * jnp.exp2(-power))).astype(jnp.int32)
    row = lax.broadcasted_iota(jnp.int32, v.shape, 0) & 7
    bit = ((power.astype(jnp.int32) + 128) >> row) & 1
    return (2 * whole + bit).astype(CODE)


def decode(code):
    v = code.astype(jnp.int32)
    bit = v & 1
    row = lax.broadcasted_iota(jnp.int32, v.shape, 0) & 7
    power = jnp.sum((bit << row).astype(F32)[0:8], axis=0, keepdims=True) - 128.0
    return (v - bit).astype(F32) * (jnp.exp2(power) * (1.0 / 32000.0))


def weights_kernel(e1_ref, s1_ref, e2_ref, s2_ref, all_ref, send, recv, send_core, recv_core):
    blk = lax.axis_size("blk")
    dp, me = lax.axis_index("dp"), lax.axis_index("blk")
    core = lax.rem(dp, 2)
    sibling = dp + 1 - 2 * core
    rows = all_ref.shape[1]
    half = rows // 2

    barrier = pltpu.get_barrier_semaphore()
    for step in range(1, blk):
        peer = lax.rem(me + step, blk)
        pl.semaphore_signal(barrier, inc=1, device_id=(dp, peer), device_id_type=MESH)
    pl.semaphore_signal(barrier, inc=1, device_id=(sibling, me), device_id_type=MESH)
    din, out = e1_ref.shape[1], e2_ref.shape[1]
    all_ref[me, 0:din, :] = e1_ref[0].astype(LOW)
    all_ref[me, din : din + out, :] = e2_ref[0].astype(LOW)
    all_ref[me, din + out :, 0:out] = s1_ref[0].astype(LOW)
    all_ref[me, din + out :, out : 2 * out] = s2_ref[0].astype(LOW)
    pl.semaphore_wait(barrier, blk)

    mine = pl.ds(pl.multiple_of(core * half, 16), half)
    copies = []
    for step in range(1, blk):
        peer = lax.rem(me + step, blk)
        copy = pltpu.make_async_remote_copy(
            src_ref=all_ref.at[me, mine],
            dst_ref=all_ref.at[me, mine],
            send_sem=send.at[step],
            recv_sem=recv.at[step],
            device_id=(dp, peer),
            device_id_type=MESH,
        )
        copy.start()
        copies.append(copy)
    forwards = []
    for step in range(1, blk):
        source = lax.rem(me - step + blk, blk)
        copies[step - 1].wait_recv()
        copy = pltpu.make_async_remote_copy(
            src_ref=all_ref.at[source, mine],
            dst_ref=all_ref.at[source, mine],
            send_sem=send_core.at[step],
            recv_sem=recv_core.at[step],
            device_id=(sibling, me),
            device_id_type=MESH,
        )
        copy.start()
        forwards.append(copy)
    for copy in copies:
        copy.wait_send()
    for copy in forwards:
        copy.wait()


def gather_weights(blk, e1, s1, e2, s2):
    rows = e1.shape[1] + e2.shape[1] + s1.shape[1]
    return pl.pallas_call(
        weights_kernel,
        out_shape=jax.ShapeDtypeStruct((blk, rows, e1.shape[2]), LOW),
        in_specs=[pl.BlockSpec(memory_space=pltpu.VMEM)] * 4,
        out_specs=pl.BlockSpec(memory_space=pltpu.VMEM),
        scratch_shapes=[pltpu.SemaphoreType.DMA((blk,)) for _ in range(4)],
        compiler_params=pltpu.CompilerParams(
            collective_id=0, has_side_effects=True, vmem_limit_bytes=16 * MIB
        ),
    )(e1, s1, e2, s2)


def compute_kernel(
    total,
    emb_ref,
    dense_ref,
    labels_ref,
    proj_ref,
    router_ref,
    task_ref,
    tower_ref,
    final_ref,
    all_ref,
    logit_ref,
    emb_grad_ref,
    grads_ref,
    a1,
    a2,
    b1,
    b2,
    s1t,
    s2t,
    s1n,
    s2n,
    tow,
    tow_n,
    fin,
    projt,
    col1,
    col2,
    x_ref,
    d1,
    d2,
    hid1,
    hid2,
    dtp,
    acc_r,
    acc_t,
    acc_p,
    acc_tow,
    acc_f,
):
    experts, h = all_ref.shape[0], all_ref.shape[2]
    tasks, th, out = tower_ref.shape
    emb, tile = emb_ref.shape
    din = router_ref.shape[1]
    eh = experts * h
    repeat = tile // LANES
    step = pl.program_id(0)
    side = din + 3 * out

    def wide(column):
        return jnp.concatenate([column] * repeat, axis=1)

    @pl.when(step == 0)
    def _():
        for e in range(experts):
            span = slice(e * h, (e + 1) * h)
            e1 = all_ref[e, 0:din, :]
            e2 = all_ref[e, din : din + out, :]
            s1 = all_ref[e, din + out :, 0:out]
            s2 = all_ref[e, din + out :, out : 2 * out]
            a1[span, :] = e1.T
            a2[span, :] = e2.T
            b1[:, span] = e1
            b2[:, span] = e2
            s1t[e] = s1.T
            s2t[e] = s2.T
            s1n[e] = s1
            s2n[e] = s2
        router = stack_rows([router_ref[e : e + 1, :] for e in range(experts)], PAD).astype(LOW)
        a1[eh:, :] = router
        router_t = pad_to(router.astype(F32), LANES, din).T
        pairs = [task_ref[t, e : e + 1, :] for t in range(tasks) for e in range(experts)]
        task = stack_rows(pairs, PAD).astype(LOW)
        a2[eh:, :] = task
        task_t = pad_to(task.astype(F32), LANES, out).T
        for e in range(experts):
            col1[e] = jnp.broadcast_to(router_t[:, e : e + 1], (din, LANES))
        for k in range(tasks * experts):
            col2[k] = jnp.broadcast_to(task_t[:, k : k + 1], (out, LANES))
        tow_n[...] = jnp.zeros_like(tow_n)
        final_t = stack_rows([final_ref[t : t + 1, :] for t in range(tasks)], 8).T
        for t in range(tasks):
            tow[t] = tower_ref[t].astype(LOW)
            tow_n[t * out : (t + 1) * out, t * th : (t + 1) * th] = tower_ref[t].T.astype(LOW)
            fin[t] = jnp.broadcast_to(final_t[:, t : t + 1], (th, LANES))
        projt[...] = proj_ref[...].T.astype(LOW)
        grads_ref[...] = jnp.zeros_like(grads_ref)
        acc_r[...] = jnp.zeros_like(acc_r)
        acc_t[...] = jnp.zeros_like(acc_t)
        acc_p[...] = jnp.zeros_like(acc_p)
        acc_tow[...] = jnp.zeros_like(acc_tow)
        acc_f[...] = jnp.zeros_like(acc_f)

    x_ref[0:emb, :] = emb_ref[...]
    x_ref[emb:, :] = mm(projt[...], dense_ref[...]).astype(LOW)
    x = x_ref[...]
    pre1 = mm(a1[...], x)
    gate1 = softmax_rows(pre1[eh : eh + experts, :])
    mid = jnp.zeros((out, tile), F32)
    slope1, mslope1, outs1 = [], [], []
    for e in range(experts):
        value, slope = gelu(pre1[e * h : (e + 1) * h, :])
        hid1[e] = value.astype(LOW)
        slope1.append(slope)
        mixed, mslope = gelu(mm(s1t[e], hid1[e]))
        outs1.append(mixed)
        mslope1.append(mslope)
        mid = mid + gate1[e : e + 1, :] * mixed
    mid = mid.astype(LOW)

    pre2 = mm(a2[...], mid)
    gate2 = []
    for t in range(tasks):
        first = eh + t * experts
        gate2.append(softmax_rows(pre2[first : first + experts, :]))
    slope2, mslope2, outs2 = [], [], []
    rep = [jnp.zeros((out, tile), F32) for _ in range(tasks)]
    for e in range(experts):
        value, slope = gelu(pre2[e * h : (e + 1) * h, :])
        hid2[e] = value.astype(LOW)
        slope2.append(slope)
        mixed, mslope = gelu(mm(s2t[e], hid2[e]))
        outs2.append(mixed)
        mslope2.append(mslope)
        for t in range(tasks):
            rep[t] = rep[t] + gate2[t][e : e + 1, :] * mixed

    for t in range(tasks):
        rep_low = rep[t].astype(LOW)
        act, tslope = gelu(mm(tow[t], rep_low))
        weight = wide(fin[t])
        logit = jnp.sum(act * weight, axis=0, keepdims=True)
        logit_ref[t : t + 1, :] = logit
        d_logit = (jax.nn.sigmoid(logit) - labels_ref[t : t + 1, :].astype(F32)) / total
        part = act * d_logit
        lump = part[:, 0:LANES]
        for k in range(1, repeat):
            lump = lump + part[:, k * LANES : (k + 1) * LANES]
        acc_f[t] += lump
        d_tp = (tslope * (d_logit * weight)).astype(LOW)
        dtp[t * th : (t + 1) * th, :] = d_tp
        acc_tow[t] += mm_nt(d_tp, rep_low)
    d_rep = mm(tow_n[...], dtp[...])

    d_gate2 = [[None] * experts for _ in range(tasks)]
    for e in range(experts):
        d_out = jnp.zeros((out, tile), F32)
        for t in range(tasks):
            piece = d_rep[t * out : (t + 1) * out, :]
            d_out = d_out + gate2[t][e : e + 1, :] * piece
            d_gate2[t][e] = jnp.sum(outs2[e] * piece, axis=0, keepdims=True)
        d_mixed = (mslope2[e] * d_out).astype(LOW)
        grads_ref[e, :, din + 2 * out : side] += mm_nt(hid2[e], d_mixed)
        d2[e * h : (e + 1) * h, :] = (slope2[e] * mm(s2n[e], d_mixed)).astype(LOW)
    rows = []
    for t in range(tasks):
        inner = sum(gate2[t][e : e + 1, :] * d_gate2[t][e] for e in range(experts))
        for e in range(experts):
            row = gate2[t][e : e + 1, :] * (d_gate2[t][e] - inner)
            rows.append(row.astype(LOW).astype(F32))
    d2[eh:, :] = stack_rows(rows, PAD).astype(LOW)
    g2 = mm_nt(d2[...], mid)
    for e in range(experts):
        grads_ref[e, :, din + out : din + 2 * out] += g2[e * h : (e + 1) * h, :]
    acc_t[...] += g2[eh:, :]
    d_mid = mm(b2[...], d2[0:eh, :])
    for k, row in enumerate(rows):
        d_mid = d_mid + wide(col2[k]) * row

    d_gate1 = []
    for e in range(experts):
        d_gate1.append(jnp.sum(outs1[e] * d_mid, axis=0, keepdims=True))
        d_mixed = (mslope1[e] * (gate1[e : e + 1, :] * d_mid)).astype(LOW)
        grads_ref[e, :, din : din + out] += mm_nt(hid1[e], d_mixed)
        d1[e * h : (e + 1) * h, :] = (slope1[e] * mm(s1n[e], d_mixed)).astype(LOW)
    inner = sum(gate1[e : e + 1, :] * d_gate1[e] for e in range(experts))
    rows = []
    for e in range(experts):
        row = gate1[e : e + 1, :] * (d_gate1[e] - inner)
        rows.append(row.astype(LOW).astype(F32))
    d1[eh:, :] = stack_rows(rows, PAD).astype(LOW)
    g1 = mm_nt(d1[...], x)
    for e in range(experts):
        grads_ref[e, :, 0:din] += g1[e * h : (e + 1) * h, :]
    acc_r[...] += g1[eh:, :]
    d_in = mm(b1[...], d1[0:eh, :])
    for e in range(experts):
        d_in = d_in + wide(col1[e]) * rows[e]
    emb_grad_ref[...] = d_in[:emb, :]
    tail = d_in[emb:, :]
    high = tail.astype(LOW)
    rest = (tail - high.astype(F32)).astype(LOW)
    acc_p[...] += mm_nt(dense_ref[...], high) + mm_nt(dense_ref[...], rest)

    @pl.when(step == pl.num_programs(0) - 1)
    def _():
        finals = [jnp.sum(acc_f[t].T, axis=0, keepdims=True) for t in range(tasks)]
        pieces = [acc_tow[t] for t in range(tasks)]
        pieces += [acc_r[:, k * out : (k + 1) * out] for k in range(din // out)]
        pieces += [acc_t[...], pad_to(acc_p[...], PAD, out)]
        pieces += [pad_to(stack_rows(finals, PAD), PAD, out)]
        at = 0
        for piece in pieces:
            for e in range(experts):
                grads_ref[e, at : at + piece.shape[0], side:] = piece
            at += piece.shape[0]


def compute(total, emb, dense, labels, proj, router, task, tower, final, everything):
    experts, _, h = everything.shape
    tasks, th, out = tower.shape
    width, rows = emb.shape
    din = router.shape[1]
    eh = experts * h
    tile = min(rows, max(LANES, 2048 // experts))

    def full(a):
        return pl.BlockSpec(a.shape, lambda i, n=a.ndim: (0,) * n)

    def part(height):
        return pl.BlockSpec((height, tile), lambda i: (0, i))

    scratch = [
        ((eh + PAD, din), LOW),
        ((eh + PAD, out), LOW),
        ((din, eh), LOW),
        ((out, eh), LOW),
        ((experts, out, h), LOW),
        ((experts, out, h), LOW),
        ((experts, h, out), LOW),
        ((experts, h, out), LOW),
        ((tasks, th, out), LOW),
        ((tasks * out, tasks * th), LOW),
        ((tasks, th, LANES), F32),
        ((proj.shape[1], proj.shape[0]), LOW),
        ((experts, din, LANES), F32),
        ((tasks * experts, out, LANES), F32),
        ((din, tile), LOW),
        ((eh + PAD, tile), LOW),
        ((eh + PAD, tile), LOW),
        ((experts, h, tile), LOW),
        ((experts, h, tile), LOW),
        ((tasks * th, tile), LOW),
        ((PAD, din), F32),
        ((PAD, out), F32),
        (proj.shape, F32),
        ((tasks, th, out), F32),
        ((tasks, th, LANES), F32),
    ]
    small = (proj, router, task, tower, final, everything)
    return pl.pallas_call(
        functools.partial(compute_kernel, total),
        grid=(rows // tile,),
        in_specs=[part(width), part(dense.shape[0]), part(tasks)] + [full(a) for a in small],
        out_specs=[
            part(tasks),
            part(width),
            pl.BlockSpec((experts, h, din + 4 * out), lambda i: (0, 0, 0)),
        ],
        out_shape=[
            jax.ShapeDtypeStruct((tasks, rows), F32),
            jax.ShapeDtypeStruct(emb.shape, F32),
            jax.ShapeDtypeStruct((experts, h, din + 4 * out), F32),
        ],
        scratch_shapes=[pltpu.VMEM(shape, kind) for shape, kind in scratch],
        compiler_params=pltpu.CompilerParams(vmem_limit_bytes=56 * MIB),
    )(emb, dense, labels, *small)


def reduce_kernel(
    grads_ref,
    full_ref,
    pair_out,
    pair_in,
    pieces,
    landed,
    gathered,
    pair_sem,
    send,
    recv,
    spread_send,
    spread_recv,
    core_send,
    core_recv,
):
    blk, devices = lax.axis_size("blk"), lax.axis_size("dp")
    chips = devices // 2
    dp, me = lax.axis_index("dp"), lax.axis_index("blk")
    core = lax.rem(dp, 2)
    chip = lax.div(dp, 2)
    sibling = dp + 1 - 2 * core
    height, columns = pieces.shape[1:]
    half = grads_ref.shape[1] // 2
    blocks = half // height
    slots = blk * chips
    own = me * chips + chip

    def place(k):
        return (lax.rem(k, blocks) * height, lax.div(k, blocks) * columns)

    def peer(step):
        to = lax.rem(own + step, slots)
        return to, (lax.rem(to, chips) * 2 + core, lax.div(to, chips))

    def source(step):
        return lax.rem(own - step + slots, slots)

    barrier = pltpu.get_barrier_semaphore()

    def greet(step, unused):
        pl.semaphore_signal(barrier, inc=1, device_id=peer(step)[1], device_id_type=MESH)
        return unused

    lax.fori_loop(1, slots, greet, 0)
    pl.semaphore_signal(barrier, inc=1, device_id=(sibling, me), device_id_type=MESH)

    other = (1 - core) * half
    first = core * half
    for e in range(blk):

        def code(j, unused, e=e):
            at = pl.multiple_of(other + j * PAD, PAD)
            to = pl.ds(pl.multiple_of(j * PAD, PAD), PAD)
            pair_out[e, to, :] = encode(grads_ref[e, pl.ds(at, PAD), :])
            return unused

        lax.fori_loop(0, half // PAD, code, 0)
    pl.semaphore_wait(barrier, slots)

    pair = pltpu.make_async_remote_copy(
        src_ref=pair_out,
        dst_ref=pair_in,
        send_sem=pair_sem.at[0],
        recv_sem=pair_sem.at[1],
        device_id=(sibling, me),
        device_id_type=MESH,
    )
    pair.start()
    pair.wait_recv()

    def outgoing(step):
        to, device = peer(step)
        return pltpu.make_async_remote_copy(
            src_ref=pieces.at[to],
            dst_ref=landed.at[own],
            send_sem=send.at[step],
            recv_sem=recv.at[step],
            device_id=device,
            device_id_type=MESH,
        )

    def prepare(to):
        e = lax.div(to, chips)
        row, column = place(lax.rem(to, chips))
        row = pl.multiple_of(row, height)
        span = pl.ds(pl.multiple_of(column, LANES), columns)
        mine = grads_ref[e, pl.ds(pl.multiple_of(first + row, height), height), span]
        return encode(mine + decode(pair_in[e, pl.ds(row, height), span]))

    def ship(step, unused):
        to = peer(step)[0]
        pieces[to] = prepare(to)
        outgoing(step).start()
        return unused

    lax.fori_loop(1, slots, ship, 0)
    landed[own] = prepare(own)

    def arrive(step, unused):
        outgoing(step).wait_recv()
        return unused

    lax.fori_loop(1, slots, arrive, 0)

    def add(slot, partial):
        return partial + decode(landed[slot])

    summed = lax.fori_loop(0, slots, add, jnp.zeros((height, columns), F32))

    def where(k, c):
        row, column = place(k)
        row = pl.multiple_of(c * half + row, height)
        return pl.ds(row, height), pl.ds(pl.multiple_of(column, LANES), columns)

    rows_own, columns_own = where(chip, core)
    gathered[rows_own, columns_own] = encode(summed)

    def spread(step):
        to = lax.rem(chip + step, chips)
        return pltpu.make_async_remote_copy(
            src_ref=gathered.at[rows_own, columns_own],
            dst_ref=gathered.at[rows_own, columns_own],
            send_sem=spread_send.at[step],
            recv_sem=spread_recv.at[step],
            device_id=(to * 2 + core, me),
            device_id_type=MESH,
        )

    def forward(step):
        rows, span = where(lax.rem(chip - step + chips, chips), core)
        return pltpu.make_async_remote_copy(
            src_ref=gathered.at[rows, span],
            dst_ref=gathered.at[rows, span],
            send_sem=core_send.at[step],
            recv_sem=core_recv.at[step],
            device_id=(sibling, me),
            device_id_type=MESH,
        )

    def spread_start(step, unused):
        spread(step).start()
        return unused

    lax.fori_loop(1, chips, spread_start, 0)
    forward(0).start()

    def pass_on(step, unused):
        spread(step).wait_recv()
        forward(step).start()
        return unused

    lax.fori_loop(1, chips, pass_on, 0)

    def finish(step, unused):
        forward(step).wait()
        return unused

    lax.fori_loop(0, chips, finish, 0)

    def write(j, unused):
        at = pl.ds(pl.multiple_of(j * PAD, PAD), PAD)
        full_ref[at, :] = decode(gathered[at, :])
        return unused

    lax.fori_loop(0, full_ref.shape[0] // PAD, write, 0)

    pair.wait_send()

    def drain(step, unused):
        outgoing(step).wait_send()
        return unused

    lax.fori_loop(1, slots, drain, 0)

    def drain_spread(step, unused):
        spread(step).wait_send()
        return unused

    lax.fori_loop(1, chips, drain_spread, 0)


def reduce_gradients(blk, devices, grads):
    _, h, width = grads.shape
    chips = devices // 2
    blocks = h // 2 // PAD
    columns = width * blocks // chips
    slots = blk * chips
    dma = pltpu.SemaphoreType.DMA
    return pl.pallas_call(
        reduce_kernel,
        out_shape=jax.ShapeDtypeStruct((h, width), F32),
        in_specs=[pl.BlockSpec(memory_space=pltpu.VMEM)],
        out_specs=pl.BlockSpec(memory_space=pltpu.VMEM),
        scratch_shapes=[
            pltpu.VMEM((blk, h // 2, width), CODE),
            pltpu.VMEM((blk, h // 2, width), CODE),
            pltpu.VMEM((slots, PAD, columns), CODE),
            pltpu.VMEM((slots, PAD, columns), CODE),
            pltpu.VMEM((h, width), CODE),
            dma((2,)),
            dma((slots,)),
            dma((slots,)),
            dma((chips,)),
            dma((chips,)),
            dma((chips,)),
            dma((chips,)),
        ],
        compiler_params=pltpu.CompilerParams(
            collective_id=1, has_side_effects=True, vmem_limit_bytes=32 * MIB
        ),
    )(grads)


def drive(steps, skew):
    live = [[one, k * skew] for k, one in enumerate(steps)]
    while live:
        for item in list(live):
            if item[1] > 0:
                item[1] -= 1
                continue
            try:
                next(item[0])
            except StopIteration:
                live.remove(item)


def put(ref, at, value, first):
    if first:
        ref[at] = value
    else:
        ref[at] += value


EARLY, LATE, SMALL = range(3)


def fused_kernel(total, names, *refs):
    table = dict(zip(names, refs))
    r = types.SimpleNamespace(**table)
    blk, devices = lax.axis_size("blk"), lax.axis_size("dp")
    chips = devices // 2
    dp, me = lax.axis_index("dp"), lax.axis_index("blk")
    core, chip = lax.rem(dp, 2), lax.div(dp, 2)
    sibling = dp + 1 - 2 * core
    experts = blk
    w1, w2 = r.w1, r.w2
    din, h = w1.shape[1:]
    tasks, th, out = r.tower.shape
    width, rows = r.emb_hbm.shape
    eh = experts * h
    tile = TILE
    count = rows // tile
    half = h // 2
    slots = blk * chips
    own = me * chips + chip

    def wide(column):
        return jnp.concatenate([column] * (tile // LANES), axis=1)

    def owner(s):
        return lax.rem(me + s, blk)

    def order(s):
        return (s + experts - 1) % experts * h

    def remote(src, dst, send, recv, device):
        return pltpu.make_async_remote_copy(
            src_ref=src,
            dst_ref=dst,
            send_sem=send,
            recv_sem=recv,
            device_id=device,
            device_id_type=MESH,
        )

    barrier = pltpu.get_barrier_semaphore()

    def greet(step, unused):
        to = lax.rem(own + step, slots)
        device = (lax.rem(to, chips) * 2 + core, lax.div(to, chips))
        pl.semaphore_signal(barrier, inc=1, device_id=device, device_id_type=MESH)
        return unused

    pl.semaphore_signal(barrier, inc=1, device_id=(sibling, me), device_id_type=MESH)
    lax.fori_loop(1, slots, greet, 0)

    loads = {}
    for k, name in enumerate(LOADED):
        loads[name] = pltpu.make_async_copy(table[name + "_hbm"], table[name], r.load_sem.at[k])
        loads[name].start()
    emb_loads = []
    for i in range(count):
        span = slice(i * tile, (i + 1) * tile)
        copy = pltpu.make_async_copy(
            r.emb_hbm.at[:, span], r.x.at[0:width, span], r.emb_sem.at[i]
        )
        copy.start()
        emb_loads.append(copy)

    for name in ("e1", "s1", "e2", "s2"):
        loads[name].wait()
    w1[0] = r.e1[0].astype(LOW)
    w2[0, 0:out, :] = r.e2[0].astype(LOW)
    w2[0, out:, 0:out] = r.s1[0].astype(LOW)
    w2[0, out:, out : 2 * out] = r.s2[0].astype(LOW)

    a1, a2, b1, b2 = r.a1, r.a2, r.b1, r.b2

    def set_first(s):
        e1 = w1[s]
        a1[s * h : (s + 1) * h, :] = e1.T
        b1[:, order(s) : order(s) + h] = e1

    def set_rest(s):
        e2 = w2[s, 0:out, :]
        s1, s2 = w2[s, out:, 0:out], w2[s, out:, out : 2 * out]
        a2[s * h : (s + 1) * h, :] = e2.T
        b2[:, s * h : (s + 1) * h] = e2
        r.s1t[s], r.s2t[s] = s1.T, s2.T
        r.s1n[s], r.s2n[s] = s1, s2

    pl.semaphore_wait(barrier, slots)

    def weight_copy(s, part):
        ref = (w1, w2)[part]
        size = ref.shape[1] // 2
        mine = pl.ds(pl.multiple_of(core * size, PAD), size)
        return remote(
            ref.at[0, mine],
            ref.at[blk - s, mine],
            r.w_send.at[s, part],
            r.w_recv.at[s, part],
            (dp, owner(s)),
        )

    def weight_forward(s, part):
        ref = (w1, w2)[part]
        size = ref.shape[1] // 2
        mine = pl.ds(pl.multiple_of(core * size, PAD), size)
        return remote(
            ref.at[s, mine],
            ref.at[s, mine],
            r.wc_send.at[s, part],
            r.wc_recv.at[s, part],
            (sibling, me),
        )

    for part in range(2):
        for s in range(1, blk):
            weight_copy(s, part).start()

    set_first(0)
    set_rest(0)
    for name in LOADED[4:]:
        loads[name].wait()
    router = stack_rows([r.router[pl.ds(owner(s), 1), :] for s in range(experts)], PAD)
    router = router.astype(LOW)
    a1[eh:, :] = router
    router_t = pad_to(router.astype(F32), LANES, din).T
    pairs = [r.task[t, pl.ds(owner(s), 1), :] for t in range(tasks) for s in range(experts)]
    task = stack_rows(pairs, PAD).astype(LOW)
    a2[eh:, :] = task
    task_t = pad_to(task.astype(F32), LANES, out).T
    for s in range(experts):
        r.col1[s] = jnp.broadcast_to(router_t[:, s : s + 1], (din, LANES))
    for k in range(tasks * experts):
        r.col2[k] = jnp.broadcast_to(task_t[:, k : k + 1], (out, LANES))
    r.tow_n[...] = jnp.zeros_like(r.tow_n)
    final_t = stack_rows([r.final[t : t + 1, :] for t in range(tasks)], 8).T
    for t in range(tasks):
        r.tow[t] = r.tower[t].astype(LOW)
        r.tow_n[t * out : (t + 1) * out, t * th : (t + 1) * th] = r.tower[t].T.astype(LOW)
        r.fin[t] = jnp.broadcast_to(final_t[:, t : t + 1], (th, LANES))
    r.projt[...] = r.proj[...].T.astype(LOW)

    x, d1, d2, hid1, hid2 = r.x, r.d1, r.d2, r.hid1, r.hid2
    sl1, out1, msl1, dmid, gate1_ref = r.sl1, r.out1, r.msl1, r.dmid, r.gate1
    g_late, g_early, g_small = r.g_late, r.g_early, r.g_small

    def layer_one(i, s):
        w = slice(i * tile, (i + 1) * tile)
        if s == 0:
            emb_loads[i].wait()
            x[width:, w] = mm(r.projt[...], r.dense[:, w]).astype(LOW)
            both = mm(a1[0:h, :], x[:, w])
            gate1_ref[:, w] = softmax_rows(mm(a1[eh:, :], x[:, w])[0:experts, :])
        else:
            both = mm(a1[s * h : (s + 1) * h, :], x[:, w])
        yield
        value, slope = gelu(both)
        hid1[s, :, w] = value.astype(LOW)
        sl1[s, :, w] = slope
        yield

    def layer_one_out(i, s):
        w = slice(i * tile, (i + 1) * tile)
        mixed = mm(r.s1t[s], hid1[s, :, w])
        yield
        mixed, slope = gelu(mixed)
        out1[s, :, w] = mixed
        msl1[s, :, w] = slope
        yield

    def layer_two(i):
        w = slice(i * tile, (i + 1) * tile)
        gate1 = gate1_ref[:, w]
        mid = jnp.zeros((out, tile), F32)
        for s in range(experts):
            mid = mid + gate1[s : s + 1, :] * out1[s, :, w]
        mid = mid.astype(LOW)
        yield
        pre2 = mm(a2[...], mid)
        yield
        gate2 = []
        for t in range(tasks):
            first = eh + t * experts
            gate2.append(softmax_rows(pre2[first : first + experts, :]))
        slope2, mslope2, outs2 = [], [], []
        for s in range(experts):
            value, slope = gelu(pre2[s * h : (s + 1) * h, :])
            hid2[s, :, w] = value.astype(LOW)
            slope2.append(slope)
        yield
        mix = [mm(r.s2t[s], hid2[s, :, w]) for s in range(experts)]
        yield
        rep = [jnp.zeros((out, tile), F32) for _ in range(tasks)]
        for s in range(experts):
            mixed, slope = gelu(mix[s])
            outs2.append(mixed)
            mslope2.append(slope)
            for t in range(tasks):
                rep[t] = rep[t] + gate2[t][s : s + 1, :] * mixed
        rep = [value.astype(LOW) for value in rep]
        yield
        pres = [mm(r.tow[t], rep[t]) for t in range(tasks)]
        yield
        for t in range(tasks):
            act, slope = gelu(pres[t])
            weight = wide(r.fin[t])
            logit = jnp.sum(act * weight, axis=0, keepdims=True)
            r.logit[t : t + 1, w] = logit
            label = r.labels[t : t + 1, w].astype(F32)
            d_logit = (jax.nn.sigmoid(logit) - label) / total
            part = act * d_logit
            lump = part[:, 0:LANES]
            for k in range(1, tile // LANES):
                lump = lump + part[:, k * LANES : (k + 1) * LANES]
            put(r.acc_f, t, lump, i == 0)
            r.dtp[t * th : (t + 1) * th, w] = (slope * (d_logit * weight)).astype(LOW)
        yield
        d_rep = mm(r.tow_n[...], r.dtp[:, w])
        for t in range(tasks):
            span = slice(t * th, (t + 1) * th)
            put(g_small, span, mm_nt(r.dtp[span, w], rep[t]), i == 0)
        yield
        d_gate2 = [[None] * experts for _ in range(tasks)]
        d_mixed = []
        for s in range(experts):
            d_out = jnp.zeros((out, tile), F32)
            for t in range(tasks):
                piece = d_rep[t * out : (t + 1) * out, :]
                d_out = d_out + gate2[t][s : s + 1, :] * piece
                d_gate2[t][s] = jnp.sum(outs2[s] * piece, axis=0, keepdims=True)
            d_mixed.append((mslope2[s] * d_out).astype(LOW))
        yield
        d_hidden = [mm(r.s2n[s], d_mixed[s]) for s in range(experts)]
        yield
        for s in range(experts):
            d2[s * h : (s + 1) * h, w] = (slope2[s] * d_hidden[s]).astype(LOW)
        lines = []
        for t in range(tasks):
            inner = sum(gate2[t][s : s + 1, :] * d_gate2[t][s] for s in range(experts))
            for s in range(experts):
                line = gate2[t][s : s + 1, :] * (d_gate2[t][s] - inner)
                lines.append(line.astype(LOW).astype(F32))
        d2[eh:, w] = stack_rows(lines, PAD).astype(LOW)
        yield
        for s in range(experts):
            at = (s, slice(None), slice(out, 2 * out))
            put(g_early, at, mm_nt(hid2[s, :, w], d_mixed[s]), i == 0)
        both = mm_nt(d2[:, w], mid)
        for s in range(experts):
            put(g_early, (s, slice(None), slice(0, out)), both[s * h : (s + 1) * h, :], i == 0)
        put(r.acc_t, Ellipsis, both[eh:, :], i == 0)
        d_mid = mm(b2[...], d2[0:eh, w])
        yield
        for k, line in enumerate(lines):
            d_mid = d_mid + wide(r.col2[k]) * line
        dmid[:, w] = d_mid
        yield

    def back_one(i, s):
        w = slice(i * tile, (i + 1) * tile)
        d_mid, gate = dmid[:, w], gate1_ref[s : s + 1, w]
        r.dgate1[s : s + 1, w] = jnp.sum(out1[s, :, w] * d_mid, axis=0, keepdims=True)
        d_mixed = (msl1[s, :, w] * (gate * d_mid)).astype(LOW)
        yield
        d_hidden = mm(r.s1n[s], d_mixed)
        put(g_late, (s, slice(None), slice(din, din + out)), mm_nt(hid1[s, :, w], d_mixed), i == 0)
        yield
        d1[order(s) : order(s) + h, w] = (sl1[s, :, w] * d_hidden).astype(LOW)
        if s == 0:
            gates, d_gates = gate1_ref[:, w], r.dgate1[:, w]
            inner = jnp.sum(gates * d_gates, axis=0, keepdims=True)
            d1[eh:, w] = pad_to(gates * (d_gates - inner), PAD, tile).astype(LOW)
        yield

    def input_grad(i):
        w = slice(i * tile, (i + 1) * tile)
        d_in = mm(b1[...], d1[0:eh, w])
        yield
        lines = d1[eh:, w].astype(F32)
        for s in range(experts):
            d_in = d_in + wide(r.col1[s]) * lines[s : s + 1, :]
        r.eg[:, w] = d_in[:width, :]
        copy = pltpu.make_async_copy(
            r.eg.at[:, w], r.emb_grad_hbm.at[:, w], r.eg_sem.at[i]
        )
        copy.start()
        stores.append(copy)
        tail = d_in[width:, :]
        high = tail.astype(LOW)
        rest = (tail - high.astype(F32)).astype(LOW)
        dense = r.dense[:, w]
        put(r.acc_p, Ellipsis, mm_nt(dense, high) + mm_nt(dense, rest), i == 0)
        yield

    stores = []
    tiles = range(count)


    mine = pl.multiple_of(core * half, half)
    other = pl.multiple_of((1 - core) * half, half)
    staged, landed = (r.st_early, r.st_late, r.st_small), (r.ld_early, r.ld_late, r.ld_small)
    gathered = (r.ga_early, r.ga_late, r.ga_small)

    def pair(k):
        src, dst = (
            (g_early.at[:, pl.ds(other, half)], r.in_early),
            (g_late.at[pl.ds(1, blk - 1), pl.ds(other, half)], r.in_late.at[pl.ds(1, blk - 1)]),
            (g_late.at[0, pl.ds(other, half)], r.in_late.at[0]),
            (g_small.at[pl.ds(other, half)], r.in_small),
        )[k]
        return remote(src, dst, r.pair_send.at[k], r.pair_recv.at[k], (sibling, me))

    def stage(kind, s):
        def one(j, unused):
            at = pl.ds(pl.multiple_of(j * PAD, PAD), PAD)
            here = pl.ds(pl.multiple_of(mine + j * PAD, PAD), PAD)
            if kind == SMALL:
                staged[kind][at, :] = encode(g_small[here, :] + r.in_small[at, :])
            elif kind == LATE:
                staged[kind][s, at, :] = encode(g_late[s, here, :] + r.in_late[s, at, :])
            else:
                staged[kind][s, at, :] = encode(g_early[s, here, :] + r.in_early[s, at, :])
            return unused

        lax.fori_loop(0, half // PAD, one, 0)

    def scatter(kind, s, j):
        to = lax.rem(chip + j, chips)
        at = pl.ds(pl.multiple_of(to * PAD, PAD), PAD)
        src = staged[kind].at[at] if kind == SMALL else staged[kind].at[s, at]
        return remote(
            src,
            landed[kind].at[own],
            r.rs_send.at[kind, s, j],
            r.rs_recv.at[kind, s, j],
            (to * 2 + core, owner(s)),
        )

    def scatter_start(kind, s):
        def one(j, unused):
            scatter(kind, s, j).start()
            return unused

        lax.fori_loop(1 if s == 0 else 0, chips, one, 0)

    def collect(kind):
        for s in range(experts):

            def one(j, unused, s=s):
                scatter(kind, s, j).wait_recv()
                return unused

            lax.fori_loop(1 if s == 0 else 0, chips, one, 0)
        at = pl.ds(pl.multiple_of(chip * PAD, PAD), PAD)
        landed[kind][own] = staged[kind][at, :] if kind == SMALL else staged[kind][0, at, :]
        summed = decode(landed[kind][0])
        for k in range(1, slots):
            summed = summed + decode(landed[kind][k])
        here = pl.ds(pl.multiple_of(mine + chip * PAD, PAD), PAD)
        gathered[kind][here, :] = encode(summed)

    def piece(kind, k):
        at = pl.ds(pl.multiple_of(mine + k * PAD, PAD), PAD)
        return gathered[kind].at[at]

    def spread(kind, j):
        to = lax.rem(chip + j, chips)
        return remote(
            piece(kind, chip),
            piece(kind, chip),
            r.ag_send.at[kind, j],
            r.ag_recv.at[kind, j],
            (to * 2 + core, me),
        )

    def forward(kind, j):
        ref = piece(kind, lax.rem(chip - j + chips, chips))
        return remote(
            ref, ref, r.fw_send.at[kind, j], r.fw_recv.at[kind, j], (sibling, me)
        )

    def spread_start(kind):
        def one(j, unused):
            spread(kind, j).start()
            return unused

        lax.fori_loop(1, chips, one, 0)
        forward(kind, 0).start()

    def pass_on(kind):
        def one(j, unused):
            spread(kind, j).wait_recv()
            forward(kind, j).start()
            return unused

        lax.fori_loop(1, chips, one, 0)

    def finish(kind):
        def one(j, unused):
            forward(kind, j).wait_recv()
            return unused

        lax.fori_loop(0, chips, one, 0)
        out_ref = (r.early_hbm, r.late_hbm, r.small_hbm)[kind]
        copy = pltpu.make_async_copy(gathered[kind], out_ref, r.ga_sem.at[kind])
        copy.start()
        stores.append(copy)


    drive([layer_one(i, 0) for i in tiles], 1)
    drive([layer_one_out(i, 0) for i in tiles], 1)
    for s in range(1, experts):
        weight_copy(blk - s, 0).wait_recv()
        weight_forward(s, 0).start()
    for s in range(1, experts):
        weight_forward(s, 0).wait_recv()
        set_first(s)
        drive([layer_one(i, s) for i in tiles], 1)
    for s in range(1, experts):
        weight_copy(blk - s, 1).wait_recv()
        weight_forward(s, 1).start()
    for s in range(1, experts):
        weight_forward(s, 1).wait_recv()
        set_rest(s)
        drive([layer_one_out(i, s) for i in tiles], 1)
    drive([layer_two(i) for i in tiles], 1)
    pair(0).start()
    copy = pltpu.make_async_copy(r.logit, r.logit_hbm, r.eg_sem.at[count])
    copy.start()
    stores.append(copy)

    for s in range(1, experts):
        drive([back_one(i, s) for i in tiles], 1)
        g_late[s, :, 0:din] = mm_nt(d1[order(s) : order(s) + h, :], x[...])
    pair(1).start()
    pair(0).wait_recv()
    for s in range(experts):
        stage(EARLY, s)
        scatter_start(EARLY, s)

    drive([back_one(i, 0) for i in tiles], 1)
    both = mm_nt(d1[order(0) :, :], x[...])
    g_late[0, :, 0:din] = both[0:h, :]
    pair(2).start()
    pair(1).wait_recv()
    for s in range(1, experts):
        stage(LATE, s)
        scatter_start(LATE, s)
    at = tasks * th
    for k in range(din // out):
        part = both[h:, k * out : (k + 1) * out]
        lines = [part[s : s + 1, :] for s in range(experts)]
        g_small[at : at + PAD, :] = stack_at(lines, [owner(s) for s in range(experts)], PAD)
        at += PAD
    lines = [r.acc_t[k : k + 1, :] for k in range(tasks * experts)]
    to = [t * experts + owner(s) for t in range(tasks) for s in range(experts)]
    g_small[at : at + PAD, :] = stack_at(lines, to, PAD)
    at += PAD
    pair(2).wait_recv()
    stage(LATE, 0)
    scatter_start(LATE, 0)

    drive([input_grad(i) for i in tiles], 1)
    g_small[at : at + PAD, :] = pad_to(r.acc_p[...], PAD, out)
    at += PAD
    finals = [jnp.sum(r.acc_f[t].T, axis=0, keepdims=True) for t in range(tasks)]
    g_small[at : at + PAD, :] = pad_to(stack_rows(finals, PAD), PAD, out)
    at += PAD
    g_small[at:, :] = jnp.zeros((h - at, out), F32)
    pair(3).start()
    pair(3).wait_recv()
    stage(SMALL, 0)
    for s in range(experts):
        scatter_start(SMALL, s)

    collect(EARLY)
    spread_start(EARLY)
    collect(LATE)
    spread_start(LATE)
    collect(SMALL)
    spread_start(SMALL)
    pass_on(EARLY)
    finish(EARLY)
    pass_on(LATE)
    pass_on(SMALL)
    finish(LATE)
    finish(SMALL)

    for s in range(1, experts):
        for part in range(2):
            weight_copy(s, part).wait_send()
            weight_forward(s, part).wait_send()
    for k in range(4):
        pair(k).wait_send()
    for kind in range(3):
        for s in range(experts):

            def left(j, unused, kind=kind, s=s):
                scatter(kind, s, j).wait_send()
                return unused

            lax.fori_loop(1 if s == 0 else 0, chips, left, 0)

        def gone(j, unused, kind=kind):
            spread(kind, j).wait_send()
            return unused

        lax.fori_loop(1, chips, gone, 0)

        def passed(j, unused, kind=kind):
            forward(kind, j).wait_send()
            return unused

        lax.fori_loop(0, chips, passed, 0)
    for copy in stores:
        copy.wait()


def stack_at(lines, places, height):
    width = lines[0].shape[1]
    index = lax.broadcasted_iota(jnp.int32, (height, width), 0)
    value = jnp.zeros((height, width), F32)
    for line, place in zip(lines, places):
        value = jnp.where(index == place, line, value)
    return value


TILE = 512
LOADED = ("e1", "s1", "e2", "s2", "dense", "labels", "proj", "router", "task", "tower", "final")


def fused(blk, devices, total, emb, arrays):
    table = dict(zip(LOADED, arrays))
    by = types.SimpleNamespace(**table)
    experts, chips = blk, devices // 2
    din, h = by.e1.shape[1:]
    tasks, th, out = by.tower.shape
    width, rows = emb.shape
    eh = experts * h
    half = h // 2
    slots = blk * chips
    side = din + out
    shapes = {name: (a.shape, a.dtype) for name, a in table.items()}
    shapes |= dict(
        w1=((experts, din, h), LOW),
        w2=((experts, out + h, 2 * out), LOW),
        a1=((eh + PAD, din), LOW),
        a2=((eh + PAD, out), LOW),
        b1=((din, eh), LOW),
        b2=((out, eh), LOW),
        s1t=((experts, out, h), LOW),
        s2t=((experts, out, h), LOW),
        s1n=((experts, h, out), LOW),
        s2n=((experts, h, out), LOW),
        tow=((tasks, th, out), LOW),
        tow_n=((tasks * out, tasks * th), LOW),
        fin=((tasks, th, LANES), F32),
        projt=(by.proj.shape[::-1], LOW),
        col1=((experts, din, LANES), F32),
        col2=((tasks * experts, out, LANES), F32),
        x=((din, rows), LOW),
        d1=((eh + PAD, rows), LOW),
        d2=((eh + PAD, rows), LOW),
        hid1=((experts, h, rows), LOW),
        hid2=((experts, h, rows), LOW),
        dtp=((tasks * th, rows), LOW),
        sl1=((experts, h, rows), F32),
        out1=((experts, out, rows), F32),
        msl1=((experts, out, rows), F32),
        dmid=((out, rows), F32),
        gate1=((experts, rows), F32),
        dgate1=((experts, rows), F32),
        logit=((tasks, rows), F32),
        eg=((width, rows), F32),
        acc_t=((PAD, out), F32),
        acc_p=(by.proj.shape, F32),
        acc_f=((tasks, th, LANES), F32),
        g_early=((experts, h, 2 * out), F32),
        g_late=((experts, h, side), F32),
        g_small=((h, out), F32),
        in_early=((experts, half, 2 * out), F32),
        in_late=((experts, half, side), F32),
        in_small=((half, out), F32),
        st_early=((experts, half, 2 * out), CODE),
        st_late=((experts, half, side), CODE),
        st_small=((half, out), CODE),
        ld_early=((slots, PAD, 2 * out), CODE),
        ld_late=((slots, PAD, side), CODE),
        ld_small=((slots, PAD, out), CODE),
        ga_early=((h, 2 * out), CODE),
        ga_late=((h, side), CODE),
        ga_small=((h, out), CODE),    )
    count = rows // TILE
    semaphores = dict(
        load_sem=(len(LOADED),),
        emb_sem=(count,),
        eg_sem=(count + 1,),
        ga_sem=(3,),
        w_send=(experts, 2),
        w_recv=(experts, 2),
        wc_send=(experts, 2),
        wc_recv=(experts, 2),
        pair_send=(4,),
        pair_recv=(4,),
        rs_send=(3, experts, chips),
        rs_recv=(3, experts, chips),
        ag_send=(3, chips),
        ag_recv=(3, chips),
        fw_send=(3, chips),
        fw_recv=(3, chips),    )
    names = [name + "_hbm" for name in LOADED] + ["emb_hbm", "logit_hbm", "emb_grad_hbm", "early_hbm", "late_hbm", "small_hbm"]
    names += [*shapes, *semaphores]
    anywhere = pl.BlockSpec(memory_space=pl.ANY)
    return pl.pallas_call(
        functools.partial(fused_kernel, total, names),
        in_specs=[anywhere] * (len(LOADED) + 1),
        out_specs=[anywhere] * 5,
        out_shape=[
            jax.ShapeDtypeStruct((tasks, rows), F32),
            jax.ShapeDtypeStruct((width, rows), F32),
            jax.ShapeDtypeStruct((h, 2 * out), CODE),
            jax.ShapeDtypeStruct((h, side), CODE),
            jax.ShapeDtypeStruct((h, out), CODE),
        ],
        scratch_shapes=[pltpu.VMEM(shape, kind) for shape, kind in shapes.values()]
        + [pltpu.SemaphoreType.DMA(shape) for shape in semaphores.values()],
        compiler_params=pltpu.CompilerParams(
            collective_id=2, has_side_effects=True, vmem_limit_bytes=60 * MIB
        ),
    )(*arrays, emb)


def halves(value):
    high = value.astype(LOW)
    return high, (value - high.astype(F32)).astype(LOW)


def gram(value):
    high, rest = halves(value)
    return mm_nt(
        jnp.concatenate([high, high, rest], axis=1), jnp.concatenate([high, rest, high], axis=1)
    )


def times(left, right):
    high, rest = halves(left)
    up, down = halves(right)
    return mm(jnp.concatenate([high, high, rest], axis=1), jnp.concatenate([up, down, up], axis=0))


def unit(matrix):
    return matrix / (jnp.sqrt(jnp.sum(matrix * matrix)) + 1e-07)


def sweep(current, masks):
    number = range(len(current))
    grams = [gram(x) for x in current]
    grams = [g if m is None else g * m for g, m in zip(grams, masks)]
    squares = [times(g, g) for g in grams]
    polys = [NS_B * g + NS_C * s for g, s in zip(grams, squares)]
    return [NS_A * current[i] + times(polys[i], current[i]) for i in number]


MUON = ("proj", "router", "task", "e1", "s1", "e2", "s2", "tower")
CHUNKS = 4


def update_kernel(coded, moved, names, *refs):
    table = dict(zip(names, refs))
    r = types.SimpleNamespace(**table)
    din, h = r.e1.shape[1:]
    out = r.s1.shape[2]
    tasks, th, _ = r.tower.shape
    experts = r.router.shape[0]
    ready = {}
    stores = []

    def load(name, k):
        ready[name] = pltpu.make_async_copy(table[name + "_hbm"], table[name], r.load_sem.at[k])
        ready[name].start()

    def store(name):
        to = r.store_sem.at[len(stores)]
        copy = pltpu.make_async_copy(table[name + "_next"], table[name + "_next_hbm"], to)
        copy.start()
        stores.append(copy)

    for k, name in enumerate(coded):
        load(name, k)
    for k, name in enumerate(MUON):
        load(name + "_m", len(coded) + k)
    passing = []
    for name in moved:
        size = table[name].shape[0] // CHUNKS if table[name].shape[0] % (8 * CHUNKS) == 0 else table[name].shape[0]
        for at in range(0, table[name].shape[0], size):
            rows = pl.ds(at, size)
            sem = r.pass_sem.at[len(passing)]
            copy = pltpu.make_async_copy(table[name + "_hbm"].at[rows], table[name].at[rows], sem)
            copy.start()
            back = pltpu.make_async_copy(table[name].at[rows], table[name + "_next_hbm"].at[rows], sem)
            passing.append((copy, back))
    rest = (*MUON, "final", "moment", "square")
    for k, name in enumerate(rest):
        load(name, len(coded) + len(MUON) + k)

    for name in coded:
        ready[name].wait()
    for name in MUON:
        ready[name + "_m"].wait()

    if len(coded) == 1:
        grads = r.full
        early, late = grads[:, din + out : din + 3 * out], grads[:, 0 : din + out]
        small = grads[:, din + 3 * out :]
    else:
        early, late, small = [
            jnp.concatenate(
                [decode(table[name][j * PAD : (j + 1) * PAD, :]) for j in range(h // PAD)], axis=0
            )
            for name in coded
        ]

    def renew(name, at, gradient):
        value = 0.5 * table[name + "_m"][at] + gradient
        table[name + "_m_next"][at] = value
        return value

    def settle(name, at, ortho):
        weight = table[name][at]
        scale = 0.2 * math.sqrt(max(weight.shape))
        table[name + "_next"][at] = weight * (1.0 - 0.2 * 0.1) - 0.2 * scale * ortho

    m_e1 = renew("e1", 0, late[:, 0:din].T)
    m_s1 = renew("s1", 0, late[:, din:])
    m_e2 = renew("e2", 0, early[:, 0:out].T)
    m_s2 = renew("s2", 0, early[:, out:])

    stacked, owner = [], []
    at = 0
    for t in range(tasks):
        stacked.append(unit(renew("tower", t, small[at : at + th, :])))
        owner += [th]
        at += th
    router_rows = []
    for k in range(din // out):
        router_rows.append(small[at : at + PAD, :])
        at += PAD
    every = slice(None)
    m_router = renew("router", every, jnp.concatenate(router_rows, axis=1)[0:experts, :])
    for t in range(tasks):
        m_task = renew("task", t, small[at + t * experts : at + (t + 1) * experts, :])
        stacked.append(pad_to(unit(m_task), 8, out))
        owner += [8]
    at += PAD
    dense, width = r.proj.shape
    m_proj = renew("proj", every, small[at : at + PAD, :][0:dense, 0:width])
    stacked.append(pad_to(unit(m_proj), PAD, out))
    owner += [PAD]
    at += PAD
    grad_final = small[at : at + PAD, :][0:tasks, 0:th]
    for name in MUON:
        store(name + "_m")

    rows = sum(owner)
    down = lax.broadcasted_iota(jnp.int32, (rows, rows), 0)
    across = lax.broadcasted_iota(jnp.int32, (rows, rows), 1)
    mask = jnp.zeros((rows, rows), F32)
    at = 0
    for length in owner:
        inside = (down >= at) & (down < at + length) & (across >= at) & (across < at + length)
        mask = jnp.where(inside, 1.0, mask)
        at += length

    current = [
        unit(m_e1).T,
        unit(m_s1).T,
        unit(m_e2),
        unit(m_s2).T,
        jnp.concatenate(stacked, axis=0),
        pad_to(unit(m_router), 8, din),
    ]
    masks = [None, None, None, None, mask, None]
    for number in range(5):
        current = sweep(current, masks)
        if number == 0:
            for copy, back in passing:
                copy.wait()
                back.start()
    x_e1, x_s1, x_e2, x_s2, x_small, x_router = current

    for name in rest:
        ready[name].wait()
    settle("e1", 0, x_e1.T)
    store("e1")
    settle("s1", 0, x_s1.T)
    settle("e2", 0, x_e2)
    settle("s2", 0, x_s2.T)
    at = 0
    for t in range(tasks):
        settle("tower", t, x_small[at : at + th, :])
        at += th
    for t in range(tasks):
        settle("task", t, x_small[at : at + experts, :])
        at += 8
    settle("proj", every, x_small[at : at + dense, 0:width])
    settle("router", every, x_router[0:experts, :])

    moment_now = 0.9 * r.moment[...] + 0.1 * grad_final
    square_now = 0.95 * r.square[...] + 0.05 * grad_final * grad_final
    corrected = moment_now / (1.0 - 0.9**STEP)
    denom = jnp.sqrt(square_now / (1.0 - 0.95**STEP)) + 1e-08
    r.moment_next[...] = moment_now
    r.square_next[...] = square_now
    r.final_next[...] = r.final[...] * (1.0 - 0.0005) - 0.25 * corrected / denom
    for name in rest:
        if name != "e1":
            store(name)
    for copy in stores:
        copy.wait()
    for copy, back in passing:
        back.wait()


def update(sums, weights, momenta, final, passed):
    taken = dict(sums)
    taken |= {name + "_m": a for name, a in zip(MUON, momenta)}
    taken |= passed
    taken |= {name: a for name, a in zip((*MUON, "final", "moment", "square"), (*weights, *final))}
    given = [name + "_m" for name in MUON] + [*MUON, "final", "moment", "square"]
    outs = [*given, *passed]
    scratch = {name: (a.shape, a.dtype) for name, a in taken.items()}
    scratch |= {name + "_next": (taken[name].shape, F32) for name in given}
    semaphores = dict(
        load_sem=(len(taken),),
        pass_sem=(CHUNKS * len(passed) + 1,),
        store_sem=(len(given),),    )
    names = [name + "_hbm" for name in taken] + [name + "_next_hbm" for name in outs]
    names += [*scratch, *semaphores]
    anywhere = pl.BlockSpec(memory_space=pl.ANY)
    results = pl.pallas_call(
        functools.partial(update_kernel, tuple(sums), tuple(passed), names),
        in_specs=[anywhere] * len(taken),
        out_specs=[anywhere] * len(outs),
        out_shape=[jax.ShapeDtypeStruct(taken[name].shape, F32) for name in outs],
        scratch_shapes=[pltpu.VMEM(shape, kind) for shape, kind in scratch.values()]
        + [pltpu.SemaphoreType.DMA(shape) for shape in semaphores.values()],
        compiler_params=pltpu.CompilerParams(vmem_limit_bytes=60 * MIB),
    )(*taken.values())
    return dict(zip(outs, results))


def on_device(
    embedded,
    dense_features,
    labels,
    projector,
    projector_momentum,
    router,
    router_momentum,
    task_router,
    task_router_momentum,
    expand_one,
    expand_one_momentum,
    shrink_one,
    shrink_one_momentum,
    expand_two,
    expand_two_momentum,
    shrink_two,
    shrink_two_momentum,
    tower_hidden,
    tower_hidden_momentum,
    tower_final,
    tower_final_moment,
    tower_final_square,
):
    devices, blk = lax.axis_size("dp"), lax.axis_size("blk")
    total = embedded.shape[0] * devices * blk

    def turn(a):
        return jnp.swapaxes(a, -1, -2)

    router_t, task_t, tower_t = turn(router), turn(task_router), turn(tower_hidden)
    examples = (turn(embedded), turn(dense_features), turn(labels))
    matrices = (expand_one, shrink_one, expand_two, shrink_two)
    small = (projector, router_t, task_t, tower_t, tower_final)
    whole = blk <= 2 and devices // 2 * PAD == expand_one.shape[2] // 2
    if whole:
        logits, embedded_grad, early, late, sums = fused(
            blk, devices, float(total), examples[0], (*matrices, *examples[1:], *small)
        )
        sums = dict(early=early, late=late, small=sums)
        passed = dict(emb_grad=embedded_grad, logit=logits)
    else:
        everything = gather_weights(blk, *matrices)
        logits, embedded_grad, grads = compute(float(total), *examples, *small, everything)
        sums = dict(full=reduce_gradients(blk, devices, grads))
        passed = {}
    results = update(
        sums,
        [projector, router_t, task_t, expand_one, shrink_one, expand_two, shrink_two, tower_t],
        [
            projector_momentum,
            turn(router_momentum),
            turn(task_router_momentum),
            expand_one_momentum,
            shrink_one_momentum,
            expand_two_momentum,
            shrink_two_momentum,
            turn(tower_hidden_momentum),
        ],
        [tower_final, tower_final_moment, tower_final_square],
        passed,
    )
    if whole:
        embedded_grad, logits = results["emb_grad"], results["logit"]
    pairs = []
    for name in MUON:
        for value in (results[name + "_m"], results[name]):
            pairs.append(turn(value) if name in ("router", "task", "tower") else value)
    last = [results[name] for name in ("moment", "square", "final")]
    return (turn(logits), turn(embedded_grad), *pairs, *last)


def solution(mesh):
    rows, owned, whole = P(("dp", "blk"), None), P("blk", None, None), P()
    return jax.shard_map(
        on_device,
        mesh=mesh,
        in_specs=(rows,) * 3 + (whole,) * 6 + (owned,) * 8 + (whole,) * 5,
        out_specs=(rows,) * 2 + (whole,) * 6 + (owned,) * 8 + (whole,) * 5,
        check_vma=False,
    )
```

```python
import functools
import math
import types

import jax
import jax.numpy as jnp
from jax import lax
from jax.experimental import pallas as pl
from jax.experimental.pallas import tpu as pltpu
from jax.sharding import PartitionSpec as P

STEP = 5
NS_A = 3.4445
NS_B = -4.775
NS_C = 2.0315
C0 = math.sqrt(2.0 / math.pi)
C1 = C0 * 0.044715
LOW = jnp.bfloat16
F32 = jnp.float32
CODE = jnp.int16
MESH = pl.DeviceIdType.MESH
MIB = 2**20
PAD = 16
LANES = 128


def mm(a, b):
    return lax.dot_general(a, b, (((1,), (0,)), ((), ())), preferred_element_type=F32)


def mm_nt(a, b):
    return lax.dot_general(a, b, (((1,), (1,)), ((), ())), preferred_element_type=F32)


def gelu(x):
    square = x * x
    half = 0.5 * jnp.tanh(x * (C0 + C1 * square)) + 0.5
    value = x * half
    slope = half + (value - value * half) * (2.0 * C0 + 6.0 * C1 * square)
    return value, slope


def softmax_rows(logits):
    shifted = jnp.exp(logits - jnp.max(logits, axis=0, keepdims=True))
    return shifted / jnp.sum(shifted, axis=0, keepdims=True)


def stack_rows(rows, height):
    width = rows[0].shape[1]
    index = lax.broadcasted_iota(jnp.int32, (height, width), 0)
    out = jnp.zeros((height, width), F32)
    for i, row in enumerate(rows):
        out = jnp.where(index == i, row, out)
    return out


def pad_to(value, rows, columns):
    if value.shape[1] < columns:
        fill = jnp.zeros((value.shape[0], columns - value.shape[1]), F32)
        value = jnp.concatenate([value, fill], axis=1)
    if value.shape[0] < rows:
        fill = jnp.zeros((rows - value.shape[0], columns), F32)
        value = jnp.concatenate([value, fill], axis=0)
    return value


def encode(v):
    top = jnp.max(jnp.abs(v), axis=0, keepdims=True)
    power = jnp.ceil(jnp.log2(jnp.maximum(top, 1e-30)))
    whole = jnp.round(v * (16000.0 * jnp.exp2(-power))).astype(jnp.int32)
    row = lax.broadcasted_iota(jnp.int32, v.shape, 0) & 7
    bit = ((power.astype(jnp.int32) + 128) >> row) & 1
    return (2 * whole + bit).astype(CODE)


def decode(code):
    v = code.astype(jnp.int32)
    bit = v & 1
    row = lax.broadcasted_iota(jnp.int32, v.shape, 0) & 7
    power = jnp.sum((bit << row).astype(F32)[0:8], axis=0, keepdims=True) - 128.0
    return (v - bit).astype(F32) * (jnp.exp2(power) * (1.0 / 32000.0))


def weights_kernel(e1_ref, s1_ref, e2_ref, s2_ref, all_ref, send, recv, send_core, recv_core):
    blk = lax.axis_size("blk")
    dp, me = lax.axis_index("dp"), lax.axis_index("blk")
    core = lax.rem(dp, 2)
    sibling = dp + 1 - 2 * core
    rows = all_ref.shape[1]
    half = rows // 2

    barrier = pltpu.get_barrier_semaphore()
    for step in range(1, blk):
        peer = lax.rem(me + step, blk)
        pl.semaphore_signal(barrier, inc=1, device_id=(dp, peer), device_id_type=MESH)
    pl.semaphore_signal(barrier, inc=1, device_id=(sibling, me), device_id_type=MESH)
    din, out = e1_ref.shape[1], e2_ref.shape[1]
    all_ref[me, 0:din, :] = e1_ref[0].astype(LOW)
    all_ref[me, din : din + out, :] = e2_ref[0].astype(LOW)
    all_ref[me, din + out :, 0:out] = s1_ref[0].astype(LOW)
    all_ref[me, din + out :, out : 2 * out] = s2_ref[0].astype(LOW)
    pl.semaphore_wait(barrier, blk)

    mine = pl.ds(pl.multiple_of(core * half, 16), half)
    copies = []
    for step in range(1, blk):
        peer = lax.rem(me + step, blk)
        copy = pltpu.make_async_remote_copy(
            src_ref=all_ref.at[me, mine],
            dst_ref=all_ref.at[me, mine],
            send_sem=send.at[step],
            recv_sem=recv.at[step],
            device_id=(dp, peer),
            device_id_type=MESH,
        )
        copy.start()
        copies.append(copy)
    forwards = []
    for step in range(1, blk):
        source = lax.rem(me - step + blk, blk)
        copies[step - 1].wait_recv()
        copy = pltpu.make_async_remote_copy(
            src_ref=all_ref.at[source, mine],
            dst_ref=all_ref.at[source, mine],
            send_sem=send_core.at[step],
            recv_sem=recv_core.at[step],
            device_id=(sibling, me),
            device_id_type=MESH,
        )
        copy.start()
        forwards.append(copy)
    for copy in copies:
        copy.wait_send()
    for copy in forwards:
        copy.wait()


def gather_weights(blk, e1, s1, e2, s2):
    rows = e1.shape[1] + e2.shape[1] + s1.shape[1]
    return pl.pallas_call(
        weights_kernel,
        out_shape=jax.ShapeDtypeStruct((blk, rows, e1.shape[2]), LOW),
        in_specs=[pl.BlockSpec(memory_space=pltpu.VMEM)] * 4,
        out_specs=pl.BlockSpec(memory_space=pltpu.VMEM),
        scratch_shapes=[pltpu.SemaphoreType.DMA((blk,)) for _ in range(4)],
        compiler_params=pltpu.CompilerParams(
            collective_id=0, has_side_effects=True, vmem_limit_bytes=16 * MIB
        ),
    )(e1, s1, e2, s2)


def compute_kernel(
    total,
    emb_ref,
    dense_ref,
    labels_ref,
    proj_ref,
    router_ref,
    task_ref,
    tower_ref,
    final_ref,
    all_ref,
    logit_ref,
    emb_grad_ref,
    grads_ref,
    a1,
    a2,
    b1,
    b2,
    s1t,
    s2t,
    s1n,
    s2n,
    tow,
    tow_n,
    fin,
    projt,
    col1,
    col2,
    x_ref,
    d1,
    d2,
    hid1,
    hid2,
    dtp,
    acc_r,
    acc_t,
    acc_p,
    acc_tow,
    acc_f,
):
    experts, h = all_ref.shape[0], all_ref.shape[2]
    tasks, th, out = tower_ref.shape
    emb, tile = emb_ref.shape
    din = router_ref.shape[1]
    eh = experts * h
    repeat = tile // LANES
    step = pl.program_id(0)
    side = din + 3 * out

    def wide(column):
        return jnp.concatenate([column] * repeat, axis=1)

    @pl.when(step == 0)
    def _():
        for e in range(experts):
            span = slice(e * h, (e + 1) * h)
            e1 = all_ref[e, 0:din, :]
            e2 = all_ref[e, din : din + out, :]
            s1 = all_ref[e, din + out :, 0:out]
            s2 = all_ref[e, din + out :, out : 2 * out]
            a1[span, :] = e1.T
            a2[span, :] = e2.T
            b1[:, span] = e1
            b2[:, span] = e2
            s1t[e] = s1.T
            s2t[e] = s2.T
            s1n[e] = s1
            s2n[e] = s2
        router = stack_rows([router_ref[e : e + 1, :] for e in range(experts)], PAD).astype(LOW)
        a1[eh:, :] = router
        router_t = pad_to(router.astype(F32), LANES, din).T
        pairs = [task_ref[t, e : e + 1, :] for t in range(tasks) for e in range(experts)]
        task = stack_rows(pairs, PAD).astype(LOW)
        a2[eh:, :] = task
        task_t = pad_to(task.astype(F32), LANES, out).T
        for e in range(experts):
            col1[e] = jnp.broadcast_to(router_t[:, e : e + 1], (din, LANES))
        for k in range(tasks * experts):
            col2[k] = jnp.broadcast_to(task_t[:, k : k + 1], (out, LANES))
        tow_n[...] = jnp.zeros_like(tow_n)
        final_t = stack_rows([final_ref[t : t + 1, :] for t in range(tasks)], 8).T
        for t in range(tasks):
            tow[t] = tower_ref[t].astype(LOW)
            tow_n[t * out : (t + 1) * out, t * th : (t + 1) * th] = tower_ref[t].T.astype(LOW)
            fin[t] = jnp.broadcast_to(final_t[:, t : t + 1], (th, LANES))
        projt[...] = proj_ref[...].T.astype(LOW)
        grads_ref[...] = jnp.zeros_like(grads_ref)
        acc_r[...] = jnp.zeros_like(acc_r)
        acc_t[...] = jnp.zeros_like(acc_t)
        acc_p[...] = jnp.zeros_like(acc_p)
        acc_tow[...] = jnp.zeros_like(acc_tow)
        acc_f[...] = jnp.zeros_like(acc_f)

    x_ref[0:emb, :] = emb_ref[...]
    x_ref[emb:, :] = mm(projt[...], dense_ref[...]).astype(LOW)
    x = x_ref[...]
    pre1 = mm(a1[...], x)
    gate1 = softmax_rows(pre1[eh : eh + experts, :])
    mid = jnp.zeros((out, tile), F32)
    slope1, mslope1, outs1 = [], [], []
    for e in range(experts):
        value, slope = gelu(pre1[e * h : (e + 1) * h, :])
        hid1[e] = value.astype(LOW)
        slope1.append(slope)
        mixed, mslope = gelu(mm(s1t[e], hid1[e]))
        outs1.append(mixed)
        mslope1.append(mslope)
        mid = mid + gate1[e : e + 1, :] * mixed
    mid = mid.astype(LOW)

    pre2 = mm(a2[...], mid)
    gate2 = []
    for t in range(tasks):
        first = eh + t * experts
        gate2.append(softmax_rows(pre2[first : first + experts, :]))
    slope2, mslope2, outs2 = [], [], []
    rep = [jnp.zeros((out, tile), F32) for _ in range(tasks)]
    for e in range(experts):
        value, slope = gelu(pre2[e * h : (e + 1) * h, :])
        hid2[e] = value.astype(LOW)
        slope2.append(slope)
        mixed, mslope = gelu(mm(s2t[e], hid2[e]))
        outs2.append(mixed)
        mslope2.append(mslope)
        for t in range(tasks):
            rep[t] = rep[t] + gate2[t][e : e + 1, :] * mixed

    for t in range(tasks):
        rep_low = rep[t].astype(LOW)
        act, tslope = gelu(mm(tow[t], rep_low))
        weight = wide(fin[t])
        logit = jnp.sum(act * weight, axis=0, keepdims=True)
        logit_ref[t : t + 1, :] = logit
        d_logit = (jax.nn.sigmoid(logit) - labels_ref[t : t + 1, :].astype(F32)) / total
        part = act * d_logit
        lump = part[:, 0:LANES]
        for k in range(1, repeat):
            lump = lump + part[:, k * LANES : (k + 1) * LANES]
        acc_f[t] += lump
        d_tp = (tslope * (d_logit * weight)).astype(LOW)
        dtp[t * th : (t + 1) * th, :] = d_tp
        acc_tow[t] += mm_nt(d_tp, rep_low)
    d_rep = mm(tow_n[...], dtp[...])

    d_gate2 = [[None] * experts for _ in range(tasks)]
    for e in range(experts):
        d_out = jnp.zeros((out, tile), F32)
        for t in range(tasks):
            piece = d_rep[t * out : (t + 1) * out, :]
            d_out = d_out + gate2[t][e : e + 1, :] * piece
            d_gate2[t][e] = jnp.sum(outs2[e] * piece, axis=0, keepdims=True)
        d_mixed = (mslope2[e] * d_out).astype(LOW)
        grads_ref[e, :, din + 2 * out : side] += mm_nt(hid2[e], d_mixed)
        d2[e * h : (e + 1) * h, :] = (slope2[e] * mm(s2n[e], d_mixed)).astype(LOW)
    rows = []
    for t in range(tasks):
        inner = sum(gate2[t][e : e + 1, :] * d_gate2[t][e] for e in range(experts))
        for e in range(experts):
            row = gate2[t][e : e + 1, :] * (d_gate2[t][e] - inner)
            rows.append(row.astype(LOW).astype(F32))
    d2[eh:, :] = stack_rows(rows, PAD).astype(LOW)
    g2 = mm_nt(d2[...], mid)
    for e in range(experts):
        grads_ref[e, :, din + out : din + 2 * out] += g2[e * h : (e + 1) * h, :]
    acc_t[...] += g2[eh:, :]
    d_mid = mm(b2[...], d2[0:eh, :])
    for k, row in enumerate(rows):
        d_mid = d_mid + wide(col2[k]) * row

    d_gate1 = []
    for e in range(experts):
        d_gate1.append(jnp.sum(outs1[e] * d_mid, axis=0, keepdims=True))
        d_mixed = (mslope1[e] * (gate1[e : e + 1, :] * d_mid)).astype(LOW)
        grads_ref[e, :, din : din + out] += mm_nt(hid1[e], d_mixed)
        d1[e * h : (e + 1) * h, :] = (slope1[e] * mm(s1n[e], d_mixed)).astype(LOW)
    inner = sum(gate1[e : e + 1, :] * d_gate1[e] for e in range(experts))
    rows = []
    for e in range(experts):
        row = gate1[e : e + 1, :] * (d_gate1[e] - inner)
        rows.append(row.astype(LOW).astype(F32))
    d1[eh:, :] = stack_rows(rows, PAD).astype(LOW)
    g1 = mm_nt(d1[...], x)
    for e in range(experts):
        grads_ref[e, :, 0:din] += g1[e * h : (e + 1) * h, :]
    acc_r[...] += g1[eh:, :]
    d_in = mm(b1[...], d1[0:eh, :])
    for e in range(experts):
        d_in = d_in + wide(col1[e]) * rows[e]
    emb_grad_ref[...] = d_in[:emb, :]
    tail = d_in[emb:, :]
    high = tail.astype(LOW)
    rest = (tail - high.astype(F32)).astype(LOW)
    acc_p[...] += mm_nt(dense_ref[...], high) + mm_nt(dense_ref[...], rest)

    @pl.when(step == pl.num_programs(0) - 1)
    def _():
        finals = [jnp.sum(acc_f[t].T, axis=0, keepdims=True) for t in range(tasks)]
        pieces = [acc_tow[t] for t in range(tasks)]
        pieces += [acc_r[:, k * out : (k + 1) * out] for k in range(din // out)]
        pieces += [acc_t[...], pad_to(acc_p[...], PAD, out)]
        pieces += [pad_to(stack_rows(finals, PAD), PAD, out)]
        at = 0
        for piece in pieces:
            for e in range(experts):
                grads_ref[e, at : at + piece.shape[0], side:] = piece
            at += piece.shape[0]


def compute(total, emb, dense, labels, proj, router, task, tower, final, everything):
    experts, _, h = everything.shape
    tasks, th, out = tower.shape
    width, rows = emb.shape
    din = router.shape[1]
    eh = experts * h
    tile = min(rows, max(LANES, 2048 // experts))

    def full(a):
        return pl.BlockSpec(a.shape, lambda i, n=a.ndim: (0,) * n)

    def part(height):
        return pl.BlockSpec((height, tile), lambda i: (0, i))

    scratch = [
        ((eh + PAD, din), LOW),
        ((eh + PAD, out), LOW),
        ((din, eh), LOW),
        ((out, eh), LOW),
        ((experts, out, h), LOW),
        ((experts, out, h), LOW),
        ((experts, h, out), LOW),
        ((experts, h, out), LOW),
        ((tasks, th, out), LOW),
        ((tasks * out, tasks * th), LOW),
        ((tasks, th, LANES), F32),
        ((proj.shape[1], proj.shape[0]), LOW),
        ((experts, din, LANES), F32),
        ((tasks * experts, out, LANES), F32),
        ((din, tile), LOW),
        ((eh + PAD, tile), LOW),
        ((eh + PAD, tile), LOW),
        ((experts, h, tile), LOW),
        ((experts, h, tile), LOW),
        ((tasks * th, tile), LOW),
        ((PAD, din), F32),
        ((PAD, out), F32),
        (proj.shape, F32),
        ((tasks, th, out), F32),
        ((tasks, th, LANES), F32),
    ]
    small = (proj, router, task, tower, final, everything)
    return pl.pallas_call(
        functools.partial(compute_kernel, total),
        grid=(rows // tile,),
        in_specs=[part(width), part(dense.shape[0]), part(tasks)] + [full(a) for a in small],
        out_specs=[
            part(tasks),
            part(width),
            pl.BlockSpec((experts, h, din + 4 * out), lambda i: (0, 0, 0)),
        ],
        out_shape=[
            jax.ShapeDtypeStruct((tasks, rows), F32),
            jax.ShapeDtypeStruct(emb.shape, F32),
            jax.ShapeDtypeStruct((experts, h, din + 4 * out), F32),
        ],
        scratch_shapes=[pltpu.VMEM(shape, kind) for shape, kind in scratch],
        compiler_params=pltpu.CompilerParams(vmem_limit_bytes=56 * MIB),
    )(emb, dense, labels, *small)


def reduce_kernel(
    grads_ref,
    full_ref,
    pair_out,
    pair_in,
    pieces,
    landed,
    gathered,
    pair_sem,
    send,
    recv,
    spread_send,
    spread_recv,
    core_send,
    core_recv,
):
    blk, devices = lax.axis_size("blk"), lax.axis_size("dp")
    chips = devices // 2
    dp, me = lax.axis_index("dp"), lax.axis_index("blk")
    core = lax.rem(dp, 2)
    chip = lax.div(dp, 2)
    sibling = dp + 1 - 2 * core
    height, columns = pieces.shape[1:]
    half = grads_ref.shape[1] // 2
    blocks = half // height
    slots = blk * chips
    own = me * chips + chip

    def place(k):
        return (lax.rem(k, blocks) * height, lax.div(k, blocks) * columns)

    def peer(step):
        to = lax.rem(own + step, slots)
        return to, (lax.rem(to, chips) * 2 + core, lax.div(to, chips))

    def source(step):
        return lax.rem(own - step + slots, slots)

    barrier = pltpu.get_barrier_semaphore()

    def greet(step, unused):
        pl.semaphore_signal(barrier, inc=1, device_id=peer(step)[1], device_id_type=MESH)
        return unused

    lax.fori_loop(1, slots, greet, 0)
    pl.semaphore_signal(barrier, inc=1, device_id=(sibling, me), device_id_type=MESH)

    other = (1 - core) * half
    first = core * half
    for e in range(blk):

        def code(j, unused, e=e):
            at = pl.multiple_of(other + j * PAD, PAD)
            to = pl.ds(pl.multiple_of(j * PAD, PAD), PAD)
            pair_out[e, to, :] = encode(grads_ref[e, pl.ds(at, PAD), :])
            return unused

        lax.fori_loop(0, half // PAD, code, 0)
    pl.semaphore_wait(barrier, slots)

    pair = pltpu.make_async_remote_copy(
        src_ref=pair_out,
        dst_ref=pair_in,
        send_sem=pair_sem.at[0],
        recv_sem=pair_sem.at[1],
        device_id=(sibling, me),
        device_id_type=MESH,
    )
    pair.start()
    pair.wait_recv()

    def outgoing(step):
        to, device = peer(step)
        return pltpu.make_async_remote_copy(
            src_ref=pieces.at[to],
            dst_ref=landed.at[own],
            send_sem=send.at[step],
            recv_sem=recv.at[step],
            device_id=device,
            device_id_type=MESH,
        )

    def prepare(to):
        e = lax.div(to, chips)
        row, column = place(lax.rem(to, chips))
        row = pl.multiple_of(row, height)
        span = pl.ds(pl.multiple_of(column, LANES), columns)
        mine = grads_ref[e, pl.ds(pl.multiple_of(first + row, height), height), span]
        return encode(mine + decode(pair_in[e, pl.ds(row, height), span]))

    def ship(step, unused):
        to = peer(step)[0]
        pieces[to] = prepare(to)
        outgoing(step).start()
        return unused

    lax.fori_loop(1, slots, ship, 0)
    landed[own] = prepare(own)

    def arrive(step, unused):
        outgoing(step).wait_recv()
        return unused

    lax.fori_loop(1, slots, arrive, 0)

    def add(slot, partial):
        return partial + decode(landed[slot])

    summed = lax.fori_loop(0, slots, add, jnp.zeros((height, columns), F32))

    def where(k, c):
        row, column = place(k)
        row = pl.multiple_of(c * half + row, height)
        return pl.ds(row, height), pl.ds(pl.multiple_of(column, LANES), columns)

    rows_own, columns_own = where(chip, core)
    gathered[rows_own, columns_own] = encode(summed)

    def spread(step):
        to = lax.rem(chip + step, chips)
        return pltpu.make_async_remote_copy(
            src_ref=gathered.at[rows_own, columns_own],
            dst_ref=gathered.at[rows_own, columns_own],
            send_sem=spread_send.at[step],
            recv_sem=spread_recv.at[step],
            device_id=(to * 2 + core, me),
            device_id_type=MESH,
        )

    def forward(step):
        rows, span = where(lax.rem(chip - step + chips, chips), core)
        return pltpu.make_async_remote_copy(
            src_ref=gathered.at[rows, span],
            dst_ref=gathered.at[rows, span],
            send_sem=core_send.at[step],
            recv_sem=core_recv.at[step],
            device_id=(sibling, me),
            device_id_type=MESH,
        )

    def spread_start(step, unused):
        spread(step).start()
        return unused

    lax.fori_loop(1, chips, spread_start, 0)
    forward(0).start()

    def pass_on(step, unused):
        spread(step).wait_recv()
        forward(step).start()
        return unused

    lax.fori_loop(1, chips, pass_on, 0)

    def finish(step, unused):
        forward(step).wait()
        return unused

    lax.fori_loop(0, chips, finish, 0)

    def write(j, unused):
        at = pl.ds(pl.multiple_of(j * PAD, PAD), PAD)
        full_ref[at, :] = decode(gathered[at, :])
        return unused

    lax.fori_loop(0, full_ref.shape[0] // PAD, write, 0)

    pair.wait_send()

    def drain(step, unused):
        outgoing(step).wait_send()
        return unused

    lax.fori_loop(1, slots, drain, 0)

    def drain_spread(step, unused):
        spread(step).wait_send()
        return unused

    lax.fori_loop(1, chips, drain_spread, 0)


def reduce_gradients(blk, devices, grads):
    _, h, width = grads.shape
    chips = devices // 2
    blocks = h // 2 // PAD
    columns = width * blocks // chips
    slots = blk * chips
    dma = pltpu.SemaphoreType.DMA
    return pl.pallas_call(
        reduce_kernel,
        out_shape=jax.ShapeDtypeStruct((h, width), F32),
        in_specs=[pl.BlockSpec(memory_space=pltpu.VMEM)],
        out_specs=pl.BlockSpec(memory_space=pltpu.VMEM),
        scratch_shapes=[
            pltpu.VMEM((blk, h // 2, width), CODE),
            pltpu.VMEM((blk, h // 2, width), CODE),
            pltpu.VMEM((slots, PAD, columns), CODE),
            pltpu.VMEM((slots, PAD, columns), CODE),
            pltpu.VMEM((h, width), CODE),
            dma((2,)),
            dma((slots,)),
            dma((slots,)),
            dma((chips,)),
            dma((chips,)),
            dma((chips,)),
            dma((chips,)),
        ],
        compiler_params=pltpu.CompilerParams(
            collective_id=1, has_side_effects=True, vmem_limit_bytes=32 * MIB
        ),
    )(grads)


MATRIX, VECTOR = range(2)


def drive(steps):
    live = [[one, next(one), k] for k, one in enumerate(steps)]
    while live:
        due = [item for item in live if item[2] == 0]
        for item in live:
            item[2] = max(0, item[2] - 1)
        for kind in (VECTOR, MATRIX):
            for item in [item for item in due if item[1] == kind]:
                item[1] = next(item[0], None)
                due.remove(item)
        live = [item for item in live if item[1] is not None]


def put(ref, at, value, first):
    if first:
        ref[at] = value
    else:
        ref[at] += value


EARLY, LATE, SMALL = range(3)


def fused_kernel(total, names, *refs):
    table = dict(zip(names, refs))
    r = types.SimpleNamespace(**table)
    blk, devices = lax.axis_size("blk"), lax.axis_size("dp")
    chips = devices // 2
    dp, me = lax.axis_index("dp"), lax.axis_index("blk")
    core, chip = lax.rem(dp, 2), lax.div(dp, 2)
    sibling = dp + 1 - 2 * core
    experts = blk
    w1, w2 = r.w1, r.w2
    din, h = w1.shape[1:]
    tasks, th, out = r.tower.shape
    width, rows = r.emb_hbm.shape
    eh = experts * h
    tile = TILE
    count = rows // tile
    half = h // 2
    tiles = range(count)

    def owner(s):
        return lax.rem(me + s, blk)

    line, b = lax.div(chip, 2), lax.rem(chip, 2)
    lines = chips // 2
    plane_rows = half // 2
    others = [(s, bb) for s in range(blk) for bb in (1, 0) if s or bb]

    def at_chip(line, b):
        return (line * 2 + b) * 2 + core

    def order(s):
        return (s + experts - 1) % experts * h

    def remote(src, dst, send, recv, device):
        return pltpu.make_async_remote_copy(
            src_ref=src,
            dst_ref=dst,
            send_sem=send,
            recv_sem=recv,
            device_id=device,
            device_id_type=MESH,
        )

    barrier = pltpu.get_barrier_semaphore()
    met = [(sibling, me), (at_chip(line ^ 1, b), me), (at_chip(line ^ 2, b), me)]
    met += [(at_chip(line, b ^ bb), owner(s)) for s, bb in others]
    for device in met:
        pl.semaphore_signal(barrier, inc=1, device_id=device, device_id_type=MESH)

    x, d1, d2, hid2, mid, reps, dtp, dm1, dm2, hid1 = [
        [table[name + str(i)] for i in range(count * (experts if name == HID1 else 1))]
        for name in (*TILED, HID1)
    ]
    loads = {}
    for k, name in enumerate(LOADED):
        loads[name] = pltpu.make_async_copy(table[name + "_hbm"], table[name], r.load_sem.at[k])
        loads[name].start()
    emb_loads = []
    for i in range(count):
        span = slice(i * tile, (i + 1) * tile)
        copy = pltpu.make_async_copy(
            r.emb_hbm.at[:, span], x[i].at[0:width], r.emb_sem.at[i]
        )
        copy.start()
        emb_loads.append(copy)

    for name in ("e1", "s1", "e2", "s2"):
        loads[name].wait()
    w1[0] = r.e1[0].astype(LOW)
    w2[0, 0:out, :] = r.e2[0].astype(LOW)
    w2[0, out:, 0:out] = r.s1[0].astype(LOW)
    w2[0, out:, out : 2 * out] = r.s2[0].astype(LOW)

    a1, a2, b1, b2 = r.a1, r.a2, r.b1, r.b2

    def set_first(s):
        e1 = w1[s]
        a1[s * h : (s + 1) * h, :] = e1.T
        b1[:, order(s) : order(s) + h] = e1

    def set_rest(s):
        e2 = w2[s, 0:out, :]
        s1, s2 = w2[s, out:, 0:out], w2[s, out:, out : 2 * out]
        a2[s * h : (s + 1) * h, :] = e2.T
        b2[:, s * h : (s + 1) * h] = e2
        r.s1t[s], r.s2t[s] = s1.T, s2.T
        r.s1n[s], r.s2n[s] = s1, s2

    pl.semaphore_wait(barrier, len(met))
    pl.semaphore_signal(r.relay, inc=1, device_id=met[1], device_id_type=MESH)

    def weight_copy(s, part):
        ref = (w1, w2)[part]
        size = ref.shape[1] // 2
        mine = pl.ds(pl.multiple_of(core * size, PAD), size)
        return remote(
            ref.at[0, mine],
            ref.at[blk - s, mine],
            r.w_send.at[s, part],
            r.w_recv.at[s, part],
            (dp, owner(s)),
        )

    def weight_forward(s, part):
        ref = (w1, w2)[part]
        size = ref.shape[1] // 2
        mine = pl.ds(pl.multiple_of(core * size, PAD), size)
        return remote(
            ref.at[s, mine],
            ref.at[s, mine],
            r.wc_send.at[s, part],
            r.wc_recv.at[s, part],
            (sibling, me),
        )

    for part in range(2):
        for s in range(1, blk):
            weight_copy(s, part).start()

    set_first(0)
    set_rest(0)
    for name in LOADED[4:]:
        loads[name].wait()
    router = stack_rows([r.router[pl.ds(owner(s), 1), :] for s in range(experts)], PAD)
    router = router.astype(LOW)
    a1[eh:, :] = router
    router_t = pad_to(router.astype(F32), LANES, din).T
    r.gate_tail[...] = router_t[width:, 0:PAD].astype(LOW)
    pairs = [r.task[t, pl.ds(owner(s), 1), :] for t in range(tasks) for s in range(experts)]
    task = stack_rows(pairs, PAD).astype(LOW)
    a2[eh:, :] = task
    task_t = pad_to(task.astype(F32), LANES, out).T
    for s in range(experts):
        r.col1[s] = jnp.broadcast_to(router_t[0:width, s : s + 1], (width, LANES))
    for k in range(tasks * experts):
        r.col2[k] = jnp.broadcast_to(task_t[:, k : k + 1], (out, LANES))
    r.tow_n[...] = jnp.zeros_like(r.tow_n)
    final_t = stack_rows([r.final[t : t + 1, :] for t in range(tasks)], 8).T
    for t in range(tasks):
        r.tow[t] = r.tower[t].astype(LOW)
        r.tow_n[t * out : (t + 1) * out, t * th : (t + 1) * th] = r.tower[t].T.astype(LOW)
        r.fin[t] = jnp.broadcast_to(final_t[:, t : t + 1], (th, LANES))
    r.projt[...] = r.proj[...].T.astype(LOW)

    sl1, out1, msl1, dmid, gate1_ref = r.sl1, r.out1, r.msl1, r.dmid, r.gate1
    p2, q2, ms2, gate2, tp, dr, dh = r.p2, r.q2, r.ms2, r.gate2, r.tp, r.dr, r.dh
    eg, lines1, lines2 = r.eg, r.lines1, r.lines2
    g_late, g_early, g_small = r.g_late, r.g_early, r.g_small
    stores = []

    def chunked(height, w, step, body):
        for left in range(w.start, w.stop, step):
            columns = slice(left, left + step)
            for top in range(0, height, PAD):
                body(slice(top, top + PAD), columns)

    def local(columns):
        left = columns.start % tile
        return slice(left, left + columns.stop - columns.start)

    def narrow(column, step):
        return jnp.concatenate([column] * (step // LANES), axis=1)

    def layer_one(i, s):
        w = slice(i * tile, (i + 1) * tile)
        yield MATRIX
        if s == 0:
            emb_loads[i].wait()
            x[i][width:, :] = mm(r.projt[...], r.dense[:, w]).astype(LOW)
            sl1[s, :, w] = mm(a1[0:h, :], x[i][...])
            gate1_ref[:, w] = softmax_rows(mm(a1[eh:, :], x[i][...])[0:experts, :])
        else:
            sl1[s, :, w] = mm(a1[s * h : (s + 1) * h, :], x[i][...])
        yield VECTOR

        def hidden(rows, columns):
            value, slope = gelu(sl1[s, rows, columns])
            hid1[s * count + i][rows, local(columns)] = value.astype(LOW)
            sl1[s, rows, columns] = slope

        chunked(h, w, STEP_COLUMNS, hidden)

    def layer_one_out(i, s):
        w = slice(i * tile, (i + 1) * tile)
        yield MATRIX
        out1[s, :, w] = mm(r.s1t[s], hid1[s * count + i][...])
        yield VECTOR

        def mixed(rows, columns):
            value, slope = gelu(out1[s, rows, columns])
            out1[s, rows, columns] = value
            msl1[s, rows, columns] = slope
            if s == experts - 1:
                total_out = gate1_ref[s : s + 1, columns] * value
                for other in range(experts - 1):
                    gate = gate1_ref[other : other + 1, columns]
                    total_out = total_out + gate * out1[other, rows, columns]
                mid[i][rows, local(columns)] = total_out.astype(LOW)

        chunked(out, w, STEP_COLUMNS, mixed)

    def layer_two(i):
        w = slice(i * tile, (i + 1) * tile)
        first = i == 0
        pairs_of = [(t, s) for t in range(tasks) for s in range(experts)]
        yield MATRIX
        p2[:, w] = mm(a2[...], mid[i][...])
        yield VECTOR
        for t in range(tasks):
            at = eh + t * experts
            gate2[t * experts : (t + 1) * experts, w] = softmax_rows(p2[at : at + experts, w])

        def hidden(rows, columns):
            value, slope = gelu(p2[rows, columns])
            hid2[i][rows, local(columns)] = value.astype(LOW)
            p2[rows, columns] = slope

        chunked(eh, w, STEP_COLUMNS, hidden)
        yield MATRIX
        for s in range(experts):
            q2[s, :, w] = mm(r.s2t[s], hid2[i][s * h : (s + 1) * h, :])
        yield VECTOR

        def mixed(rows, columns):
            rep = [None] * tasks
            for s in range(experts):
                value, slope = gelu(q2[s, rows, columns])
                q2[s, rows, columns] = value
                ms2[s, rows, columns] = slope
                for t in range(tasks):
                    k = t * experts + s
                    term = gate2[k : k + 1, columns] * value
                    rep[t] = term if s == 0 else rep[t] + term
            for t in range(tasks):
                reps[i][t, rows, local(columns)] = rep[t].astype(LOW)

        chunked(out, w, STEP_COLUMNS, mixed)
        yield MATRIX
        for t in range(tasks):
            tp[t * th : (t + 1) * th, w] = mm(r.tow[t], reps[i][t])
        yield VECTOR
        lumps = [None] * tasks
        for left in range(w.start, w.stop, STEP_COLUMNS):
            columns = slice(left, left + STEP_COLUMNS)
            for t in range(tasks):
                at = slice(t * th, (t + 1) * th)
                weight = narrow(r.fin[t], STEP_COLUMNS)
                act, slope = gelu(tp[at, columns])
                logit = jnp.sum(act * weight, axis=0, keepdims=True)
                r.logit[t : t + 1, columns] = logit
                label = r.labels[t : t + 1, columns].astype(F32)
                d_logit = (jax.nn.sigmoid(logit) - label) / total
                dtp[i][at, local(columns)] = (slope * weight * d_logit).astype(LOW)
                part = act * d_logit
                for k in range(0, STEP_COLUMNS, LANES):
                    piece = part[:, k : k + LANES]
                    lumps[t] = piece if lumps[t] is None else lumps[t] + piece
        for t in range(tasks):
            put(r.acc_f, t, lumps[t], first)
        yield MATRIX
        dr[:, w] = mm(r.tow_n[...], dtp[i][...])
        for t in range(tasks):
            span = slice(t * th, (t + 1) * th)
            put(g_small, span, mm_nt(dtp[i][span, :], reps[i][t]), first)
        yield VECTOR
        for left in range(w.start, w.stop, STEP_COLUMNS):
            columns = slice(left, left + STEP_COLUMNS)
            sums = [None] * (tasks * experts)
            for top in range(0, out, PAD):
                rows = slice(top, top + PAD)
                piece = [dr[t * out + top : t * out + top + PAD, columns] for t in range(tasks)]
                for s in range(experts):
                    value = q2[s, rows, columns]
                    d_out = None
                    for t in range(tasks):
                        k = t * experts + s
                        term = gate2[k : k + 1, columns] * piece[t]
                        d_out = term if t == 0 else d_out + term
                        part = value * piece[t]
                        sums[k] = part if top == 0 else sums[k] + part
                    slope = ms2[s, rows, columns]
                    dm2[i][s, rows, local(columns)] = (slope * d_out).astype(LOW)
            d_gate = [jnp.sum(part, axis=0, keepdims=True) for part in sums]
            lines = []
            for t in range(tasks):
                gates = [
                    gate2[t * experts + s : t * experts + s + 1, columns] for s in range(experts)
                ]
                inner = sum(gates[s] * d_gate[t * experts + s] for s in range(experts))
                for s in range(experts):
                    lines.append(gates[s] * (d_gate[t * experts + s] - inner))
            lines = stack_rows(lines, PAD).astype(LOW)
            d2[i][eh:, local(columns)] = lines
            lines2[:, columns] = lines.astype(F32)
        yield MATRIX
        for s in range(experts):
            dh[s, :, w] = mm(r.s2n[s], dm2[i][s])
        yield VECTOR

        def before(rows, columns):
            s, top = divmod(rows.start, h)
            d_hidden = dh[s, top : top + PAD, columns]
            d2[i][rows, local(columns)] = (p2[rows, columns] * d_hidden).astype(LOW)

        chunked(eh, w, STEP_COLUMNS, before)
        yield MATRIX
        for s in range(experts):
            at = (s, slice(None), slice(out, 2 * out))
            put(g_early, at, mm_nt(hid2[i][s * h : (s + 1) * h, :], dm2[i][s]), first)
        both = mm_nt(d2[i][...], mid[i][...])
        for s in range(experts):
            put(g_early, (s, slice(None), slice(0, out)), both[s * h : (s + 1) * h, :], first)
        put(r.acc_t, Ellipsis, both[eh:, :], first)
        dmid[:, w] = mm(b2[...], d2[i][0:eh, :])
        yield VECTOR

        def gates_too(rows, columns):
            value = dmid[rows, columns]
            for k in range(tasks * experts):
                line = lines2[k : k + 1, columns]
                value = value + narrow(r.col2[k, rows, :], STEP_COLUMNS) * line
            dmid[rows, columns] = value

        chunked(out, w, STEP_COLUMNS, gates_too)

    def matrix_grad(first, last):
        left = jnp.concatenate([d1[i][first:last, :] for i in tiles], axis=1)
        return mm_nt(left, jnp.concatenate([x[i][...] for i in tiles], axis=1))

    def back_one(i, s):
        w = slice(i * tile, (i + 1) * tile)
        yield VECTOR
        for left in range(w.start, w.stop, STEP_COLUMNS):
            columns = slice(left, left + STEP_COLUMNS)
            gate = gate1_ref[s : s + 1, columns]
            sums = None
            for top in range(0, out, PAD):
                rows = slice(top, top + PAD)
                d_out = dmid[rows, columns]
                part = out1[s, rows, columns] * d_out
                sums = part if top == 0 else sums + part
                slope = msl1[s, rows, columns]
                dm1[i][rows, local(columns)] = (slope * (gate * d_out)).astype(LOW)
            r.dgate1[s : s + 1, columns] = jnp.sum(sums, axis=0, keepdims=True)
            if s == 0:
                gates, d_gates = gate1_ref[:, columns], r.dgate1[:, columns]
                inner = jnp.sum(gates * d_gates, axis=0, keepdims=True)
                lines = pad_to(gates * (d_gates - inner), PAD, STEP_COLUMNS).astype(LOW)
                d1[i][eh:, local(columns)] = lines
                lines1[:, columns] = lines.astype(F32)
        yield MATRIX
        dh[s, :, w] = mm(r.s1n[s], dm1[i][...])
        at = (s, slice(None), slice(din, din + out))
        put(g_late, at, mm_nt(hid1[s * count + i][...], dm1[i][...]), i == 0)
        yield VECTOR

        def before(rows, columns):
            at = order(s) + rows.start
            d_hidden = dh[s, rows, columns]
            d_pre = (sl1[s, rows, columns] * d_hidden).astype(LOW)
            d1[i][at : at + PAD, local(columns)] = d_pre

        chunked(h, w, STEP_COLUMNS, before)

    def input_grad(i):
        w = slice(i * tile, (i + 1) * tile)
        yield MATRIX
        eg[:, w] = mm(b1[0:width, :], d1[i][0:eh, :])
        yield VECTOR

        def gates_too(rows, columns):
            value = eg[rows, columns]
            for s in range(experts):
                gate = lines1[s : s + 1, columns]
                value = value + narrow(r.col1[s, rows, :], STEP_COLUMNS) * gate
            eg[rows, columns] = value

        chunked(width, w, STEP_COLUMNS, gates_too)
        copy = pltpu.make_async_copy(eg.at[:, w], r.emb_grad_hbm.at[:, w], r.eg_sem.at[i])
        copy.start()
        stores.append(copy)

    def projector_grad():
        left = jnp.concatenate([d1[i][...] for i in tiles], axis=1)
        summed = mm_nt(r.dense[...], left)
        high = summed.astype(LOW)
        rest = (summed - high.astype(F32)).astype(LOW)
        value = jnp.zeros(r.proj.shape, F32)
        for piece in (high, rest):
            value = value + mm_nt(piece[:, 0:eh], b1[width:, :])
            value = value + mm_nt(piece[:, eh:], r.gate_tail[...])
        return value


    mine = pl.multiple_of(core * half, half)
    other = pl.multiple_of((1 - core) * half, half)
    staged = (r.st_early, r.st_late, r.st_small)
    plane_in, line_out = (r.pi_early, r.pi_late, r.pi_small), (r.lo_early, r.lo_late, r.lo_small)
    line_in, gathered = (r.li_early, r.li_late, r.li_small), (r.ga_early, r.ga_late, r.ga_small)

    def pair(k):
        src, dst = (
            (g_early.at[:, pl.ds(other, half)], r.in_early),
            (g_late.at[pl.ds(1, blk - 1), pl.ds(other, half)], r.in_late.at[pl.ds(1, blk - 1)]),
            (g_late.at[0, pl.ds(other, half)], r.in_late.at[0]),
            (g_small.at[pl.ds(other, half)], r.in_small),
        )[k]
        return remote(src, dst, r.pair_send.at[k], r.pair_recv.at[k], (sibling, me))

    def stage(kind, s):
        for top in range(0, half, PAD):
            at = slice(top, top + PAD)
            here = pl.ds(pl.multiple_of(mine + top, PAD), PAD)
            if kind == SMALL:
                staged[kind][at, :] = encode(g_small[here, :] + r.in_small[at, :])
            elif kind == LATE:
                staged[kind][s, at, :] = encode(g_late[s, here, :] + r.in_late[s, at, :])
            else:
                staged[kind][s, at, :] = encode(g_early[s, here, :] + r.in_early[s, at, :])

    def plane(kind, s, bb):
        at = pl.ds(pl.multiple_of((b ^ bb) * plane_rows, PAD), plane_rows)
        src = staged[kind].at[at] if kind == SMALL else staged[kind].at[s, at]
        return remote(
            src,
            plane_in[kind].at[me * 2 + b],
            r.pl_send.at[kind, s, bb],
            r.pl_recv.at[kind, s, bb],
            (at_chip(line, b ^ bb), owner(s)),
        )

    def plane_start(kind, s):
        for slot, bb in others:
            if slot == s:
                plane(kind, s, bb).start()

    def along(kind, j):
        to = lax.rem(line + j, lines)
        at = pl.ds(pl.multiple_of(to * PAD, PAD), PAD)
        return remote(
            line_out[kind].at[at],
            line_in[kind].at[line],
            r.ln_send.at[kind, j],
            r.ln_recv.at[kind, j],
            (at_chip(to, b), me),
        )

    def line_start(kind):
        for s, bb in others:
            plane(kind, s, bb).wait_recv()
        at = pl.ds(pl.multiple_of(b * plane_rows, PAD), plane_rows)
        plane_in[kind][me * 2 + b] = staged[kind][at, :] if kind == SMALL else staged[kind][0, at, :]

        for top in range(0, plane_rows, PAD):
            here = slice(top, top + PAD)
            summed = decode(plane_in[kind][0, here, :])
            for k in range(1, 2 * blk):
                summed = summed + decode(plane_in[kind][k, here, :])
            line_out[kind][here, :] = encode(summed)
        for j in range(1, lines):
            along(kind, j).start()

    def collect(kind):
        for j in range(1, lines):
            along(kind, j).wait_recv()
        line_in[kind][line] = line_out[kind][pl.ds(pl.multiple_of(line * PAD, PAD), PAD), :]
        summed = decode(line_in[kind][0])
        for k in range(1, lines):
            summed = summed + decode(line_in[kind][k])
        gathered[kind][rows_of(chip), :] = encode(summed)

    def rows_of(k):
        at = mine + lax.rem(k, 2) * plane_rows + lax.div(k, 2) * PAD
        return pl.ds(pl.multiple_of(at, PAD), PAD)

    def piece(kind, k):
        return gathered[kind].at[rows_of(k)]

    def spread(kind, j):
        to = lax.rem(chip + j, chips)
        return remote(
            piece(kind, chip),
            piece(kind, chip),
            r.ag_send.at[kind, j],
            r.ag_recv.at[kind, j],
            (to * 2 + core, me),
        )

    def forward(kind, j):
        ref = piece(kind, lax.rem(chip - j + chips, chips))
        return remote(
            ref, ref, r.fw_send.at[kind, j], r.fw_recv.at[kind, j], (sibling, me)
        )

    def spread_start(kind):
        def one(j, unused):
            spread(kind, j).start()
            return unused

        lax.fori_loop(1, chips, one, 0)
        forward(kind, 0).start()

    def pass_on(kind):
        def one(j, unused):
            spread(kind, j).wait_recv()
            forward(kind, j).start()
            return unused

        lax.fori_loop(1, chips, one, 0)

    def finish(kind):
        def one(j, unused):
            forward(kind, j).wait_recv()
            return unused

        lax.fori_loop(0, chips, one, 0)
        out_ref = (r.early_hbm, r.late_hbm, r.small_hbm)[kind]
        copy = pltpu.make_async_copy(gathered[kind], out_ref, r.ga_sem.at[kind])
        copy.start()
        stores.append(copy)


    drive([layer_one(i, 0) for i in tiles])
    drive([layer_one_out(i, 0) for i in tiles])
    for s in range(1, experts):
        weight_copy(blk - s, 0).wait_recv()
        weight_forward(s, 0).start()
    for s in range(1, experts):
        weight_forward(s, 0).wait_recv()
        set_first(s)
        drive([layer_one(i, s) for i in tiles])
    for s in range(1, experts):
        weight_copy(blk - s, 1).wait_recv()
        weight_forward(s, 1).start()
    for s in range(1, experts):
        weight_forward(s, 1).wait_recv()
        set_rest(s)
        drive([layer_one_out(i, s) for i in tiles])
    drive([layer_two(i) for i in tiles])
    pair(0).start()
    copy = pltpu.make_async_copy(r.logit, r.logit_hbm, r.eg_sem.at[count])
    copy.start()
    stores.append(copy)

    for s in range(1, experts):
        drive([back_one(i, s) for i in tiles])
    pair(0).wait_recv()
    for s in range(experts):
        stage(EARLY, s)
        plane_start(EARLY, s)
    for s in range(1, experts):
        g_late[s, :, 0:din] = matrix_grad(order(s), order(s) + h)
    pair(1).start()
    drive([back_one(i, 0) for i in tiles])
    pair(1).wait_recv()
    for s in range(1, experts):
        stage(LATE, s)
        plane_start(LATE, s)
    both = matrix_grad(order(0), eh + PAD)
    g_late[0, :, 0:din] = both[0:h, :]
    pair(2).start()
    at = tasks * th
    for k in range(din // out):
        value = both[h:, k * out : (k + 1) * out]
        parts = [value[s : s + 1, :] for s in range(experts)]
        g_small[at : at + PAD, :] = stack_at(parts, [owner(s) for s in range(experts)], PAD)
        at += PAD
    parts = [r.acc_t[k : k + 1, :] for k in range(tasks * experts)]
    to = [t * experts + owner(s) for t in range(tasks) for s in range(experts)]
    g_small[at : at + PAD, :] = stack_at(parts, to, PAD)
    at += PAD
    finals = [jnp.sum(r.acc_f[t].T, axis=0, keepdims=True) for t in range(tasks)]
    g_small[at + PAD : at + 2 * PAD, :] = pad_to(stack_rows(finals, PAD), PAD, out)
    g_small[at + 2 * PAD :, :] = jnp.zeros((h - at - 2 * PAD, out), F32)
    g_small[at : at + PAD, :] = pad_to(projector_grad(), PAD, out)
    pair(3).start()
    pair(2).wait_recv()
    stage(LATE, 0)
    plane_start(LATE, 0)
    pair(3).wait_recv()
    stage(SMALL, 0)
    for s in range(experts):
        plane_start(SMALL, s)
    pl.semaphore_wait(r.relay, 1)
    line_start(EARLY)
    drive([input_grad(i) for i in tiles])
    line_start(LATE)
    line_start(SMALL)
    collect(EARLY)
    spread_start(EARLY)
    collect(LATE)
    spread_start(LATE)
    collect(SMALL)
    spread_start(SMALL)
    pass_on(EARLY)
    finish(EARLY)
    pass_on(LATE)
    pass_on(SMALL)
    finish(LATE)
    finish(SMALL)

    for s in range(1, experts):
        for part in range(2):
            weight_copy(s, part).wait_send()
            weight_forward(s, part).wait_send()
    for k in range(4):
        pair(k).wait_send()
    for kind in range(3):
        for s, bb in others:
            plane(kind, s, bb).wait_send()
        for j in range(1, lines):
            along(kind, j).wait_send()

        def gone(j, unused, kind=kind):
            spread(kind, j).wait_send()
            return unused

        lax.fori_loop(1, chips, gone, 0)

        def passed(j, unused, kind=kind):
            forward(kind, j).wait_send()
            return unused

        lax.fori_loop(0, chips, passed, 0)
    for copy in stores:
        copy.wait()


def stack_at(lines, places, height):
    width = lines[0].shape[1]
    index = lax.broadcasted_iota(jnp.int32, (height, width), 0)
    value = jnp.zeros((height, width), F32)
    for line, place in zip(lines, places):
        value = jnp.where(index == place, line, value)
    return value


TILE = 512
STEP_COLUMNS = 256
HID1 = "hid1"
TILED = ("x", "d1", "d2", "hid2", "mid", "reps", "dtp", "dm1", "dm2")
LOADED = ("e1", "s1", "e2", "s2", "dense", "labels", "proj", "router", "task", "tower", "final")


def fused(blk, devices, total, emb, arrays):
    table = dict(zip(LOADED, arrays))
    by = types.SimpleNamespace(**table)
    experts, chips = blk, devices // 2
    din, h = by.e1.shape[1:]
    tasks, th, out = by.tower.shape
    width, rows = emb.shape
    eh = experts * h
    half = h // 2
    side = din + out
    shapes = {name: (a.shape, a.dtype) for name, a in table.items()}
    shapes |= dict(
        w1=((experts, din, h), LOW),
        w2=((experts, out + h, 2 * out), LOW),
        a1=((eh + PAD, din), LOW),
        a2=((eh + PAD, out), LOW),
        b1=((din, eh), LOW),
        b2=((out, eh), LOW),
        s1t=((experts, out, h), LOW),
        s2t=((experts, out, h), LOW),
        s1n=((experts, h, out), LOW),
        s2n=((experts, h, out), LOW),
        tow=((tasks, th, out), LOW),
        tow_n=((tasks * out, tasks * th), LOW),
        fin=((tasks, th, LANES), F32),
        projt=(by.proj.shape[::-1], LOW),
        col1=((experts, width, LANES), F32),
        gate_tail=((din - width, PAD), LOW),
        col2=((tasks * experts, out, LANES), F32),
        sl1=((experts, h, rows), F32),
        out1=((experts, out, rows), F32),
        msl1=((experts, out, rows), F32),
        dmid=((out, rows), F32),
        gate1=((experts, rows), F32),
        dgate1=((experts, rows), F32),
        logit=((tasks, rows), F32),
        eg=((width, rows), F32),
        lines1=((PAD, rows), F32),
        lines2=((PAD, rows), F32),
        p2=((eh + PAD, rows), F32),
        q2=((experts, out, rows), F32),
        ms2=((experts, out, rows), F32),
        gate2=((tasks * experts, rows), F32),
        tp=((tasks * th, rows), F32),
        dr=((tasks * out, rows), F32),
        dh=((experts, h, rows), F32),
        acc_t=((PAD, out), F32),
        acc_f=((tasks, th, LANES), F32),
        g_early=((experts, h, 2 * out), F32),
        g_late=((experts, h, side), F32),
        g_small=((h, out), F32),
        in_early=((experts, half, 2 * out), F32),
        in_late=((experts, half, side), F32),
        in_small=((half, out), F32),
        st_early=((experts, half, 2 * out), CODE),
        st_late=((experts, half, side), CODE),
        st_small=((half, out), CODE),
        pi_early=((2 * blk, half // 2, 2 * out), CODE),
        pi_late=((2 * blk, half // 2, side), CODE),
        pi_small=((2 * blk, half // 2, out), CODE),
        lo_early=((half // 2, 2 * out), CODE),
        lo_late=((half // 2, side), CODE),
        lo_small=((half // 2, out), CODE),
        li_early=((chips // 2, PAD, 2 * out), CODE),
        li_late=((chips // 2, PAD, side), CODE),
        li_small=((chips // 2, PAD, out), CODE),
        ga_early=((h, 2 * out), CODE),
        ga_late=((h, side), CODE),
        ga_small=((h, out), CODE),    )
    count = rows // TILE
    for name, shape in zip(
        TILED,
        (
            (din,),
            (eh + PAD,),
            (eh + PAD,),
            (eh,),
            (out,),
            (tasks, out),
            (tasks * th,),
            (out,),
            (experts, out),
        ),
    ):
        shapes |= {name + str(i): ((*shape, TILE), LOW) for i in range(count)}
    shapes |= {HID1 + str(i): ((h, TILE), LOW) for i in range(count * experts)}
    semaphores = dict(
        load_sem=(len(LOADED),),
        emb_sem=(count,),
        eg_sem=(count + 1,),
        ga_sem=(3,),
        w_send=(experts, 2),
        w_recv=(experts, 2),
        wc_send=(experts, 2),
        wc_recv=(experts, 2),
        pair_send=(4,),
        pair_recv=(4,),
        pl_send=(3, experts, 2),
        pl_recv=(3, experts, 2),
        ln_send=(3, chips // 2),
        ln_recv=(3, chips // 2),
        ag_send=(3, chips),
        ag_recv=(3, chips),
        fw_send=(3, chips),
        fw_recv=(3, chips),    )
    names = [name + "_hbm" for name in LOADED] + ["emb_hbm", "logit_hbm", "emb_grad_hbm", "early_hbm", "late_hbm", "small_hbm"]
    names += [*shapes, *semaphores, "relay"]
    anywhere = pl.BlockSpec(memory_space=pl.ANY)
    return pl.pallas_call(
        functools.partial(fused_kernel, total, names),
        in_specs=[anywhere] * (len(LOADED) + 1),
        out_specs=[anywhere] * 5,
        out_shape=[
            jax.ShapeDtypeStruct((tasks, rows), F32),
            jax.ShapeDtypeStruct((width, rows), F32),
            jax.ShapeDtypeStruct((h, 2 * out), CODE),
            jax.ShapeDtypeStruct((h, side), CODE),
            jax.ShapeDtypeStruct((h, out), CODE),
        ],
        scratch_shapes=[pltpu.VMEM(shape, kind) for shape, kind in shapes.values()]
        + [pltpu.SemaphoreType.DMA(shape) for shape in semaphores.values()]
        + [pltpu.SemaphoreType.REGULAR],
        compiler_params=pltpu.CompilerParams(
            collective_id=2, has_side_effects=True, vmem_limit_bytes=60 * MIB
        ),
    )(*arrays, emb)


def halves(value):
    high = value.astype(LOW)
    return high, (value - high.astype(F32)).astype(LOW)


def gram(value, once=False):
    high, rest = halves(value)
    if once:
        return mm_nt(high, high)
    return mm_nt(
        jnp.concatenate([high, high, rest], axis=1), jnp.concatenate([high, rest, high], axis=1)
    )


def times(left, right, once=False):
    high, rest = halves(left)
    up, down = halves(right)
    if once:
        return mm(high, up)
    return mm(jnp.concatenate([high, high, rest], axis=1), jnp.concatenate([up, down, up], axis=0))


def unit(matrix):
    return matrix / (jnp.sqrt(jnp.sum(matrix * matrix)) + 1e-07)


def sweep(current, masks, once):
    number = range(len(current))
    grams = [gram(current[i], once[i]) for i in number]
    grams = [g if m is None else g * m for g, m in zip(grams, masks)]
    squares = [times(grams[i], grams[i], once[i]) for i in number]
    polys = [NS_B * g + NS_C * s for g, s in zip(grams, squares)]
    return [NS_A * current[i] + times(polys[i], current[i], once[i]) for i in number]


MUON = ("proj", "router", "task", "e1", "s1", "e2", "s2", "tower")
CHUNKS = 4


def update_kernel(coded, moved, names, *refs):
    table = dict(zip(names, refs))
    r = types.SimpleNamespace(**table)
    din, h = r.e1.shape[1:]
    out = r.s1.shape[2]
    tasks, th, _ = r.tower.shape
    experts = r.router.shape[0]
    ready = {}
    stores = []

    def load(name, k):
        ready[name] = pltpu.make_async_copy(table[name + "_hbm"], table[name], r.load_sem.at[k])
        ready[name].start()

    def store(name):
        to = r.store_sem.at[len(stores)]
        copy = pltpu.make_async_copy(table[name + "_next"], table[name + "_next_hbm"], to)
        copy.start()
        stores.append(copy)

    for k, name in enumerate(coded):
        load(name, k)
    for k, name in enumerate(MUON):
        load(name + "_m", len(coded) + k)
    passing = []
    for name in moved:
        size = table[name].shape[0] // CHUNKS if table[name].shape[0] % (8 * CHUNKS) == 0 else table[name].shape[0]
        for at in range(0, table[name].shape[0], size):
            rows = pl.ds(at, size)
            sem = r.pass_sem.at[len(passing)]
            copy = pltpu.make_async_copy(table[name + "_hbm"].at[rows], table[name].at[rows], sem)
            copy.start()
            back = pltpu.make_async_copy(table[name].at[rows], table[name + "_next_hbm"].at[rows], sem)
            passing.append((copy, back))
    rest = (*MUON, "final", "moment", "square")
    for k, name in enumerate(rest):
        load(name, len(coded) + len(MUON) + k)

    for name in coded:
        ready[name].wait()
    for name in MUON:
        ready[name + "_m"].wait()

    if len(coded) == 1:
        grads = r.full
        early, late = grads[:, din + out : din + 3 * out], grads[:, 0 : din + out]
        small = grads[:, din + 3 * out :]
    else:
        early, late, small = [
            jnp.concatenate(
                [decode(table[name][j * PAD : (j + 1) * PAD, :]) for j in range(h // PAD)], axis=0
            )
            for name in coded
        ]

    def renew(name, at, gradient):
        value = 0.5 * table[name + "_m"][at] + gradient
        table[name + "_m_next"][at] = value
        return value

    def settle(name, at, ortho):
        weight = table[name][at]
        scale = 0.2 * math.sqrt(max(weight.shape))
        table[name + "_next"][at] = weight * (1.0 - 0.2 * 0.1) - 0.2 * scale * ortho

    m_e1 = renew("e1", 0, late[:, 0:din].T)
    m_s1 = renew("s1", 0, late[:, din:])
    m_e2 = renew("e2", 0, early[:, 0:out].T)
    m_s2 = renew("s2", 0, early[:, out:])

    stacked, owner = [], []
    at = 0
    for t in range(tasks):
        stacked.append(unit(renew("tower", t, small[at : at + th, :])))
        owner += [th]
        at += th
    router_rows = []
    for k in range(din // out):
        router_rows.append(small[at : at + PAD, :])
        at += PAD
    every = slice(None)
    m_router = renew("router", every, jnp.concatenate(router_rows, axis=1)[0:experts, :])
    for t in range(tasks):
        m_task = renew("task", t, small[at + t * experts : at + (t + 1) * experts, :])
        stacked.append(pad_to(unit(m_task), 8, out))
        owner += [8]
    at += PAD
    dense, width = r.proj.shape
    m_proj = renew("proj", every, small[at : at + PAD, :][0:dense, 0:width])
    stacked.append(pad_to(unit(m_proj), PAD, out))
    owner += [PAD]
    at += PAD
    grad_final = small[at : at + PAD, :][0:tasks, 0:th]
    for name in MUON:
        store(name + "_m")

    rows = sum(owner)
    down = lax.broadcasted_iota(jnp.int32, (rows, rows), 0)
    across = lax.broadcasted_iota(jnp.int32, (rows, rows), 1)
    mask = jnp.zeros((rows, rows), F32)
    at = 0
    for length in owner:
        inside = (down >= at) & (down < at + length) & (across >= at) & (across < at + length)
        mask = jnp.where(inside, 1.0, mask)
        at += length

    current = [
        unit(m_e1).T,
        unit(m_s1).T,
        unit(m_e2),
        unit(m_s2).T,
        jnp.concatenate(stacked, axis=0),
        pad_to(unit(m_router), 8, din),
    ]
    masks = [None, None, None, None, mask, None]
    for number in range(5):
        once = [number == 0 and x.shape[0] >= out and m is None for x, m in zip(current, masks)]
        current = sweep(current, masks, once)
        if number == 0:
            for copy, back in passing:
                copy.wait()
                back.start()
    x_e1, x_s1, x_e2, x_s2, x_small, x_router = current

    for name in rest:
        ready[name].wait()
    settle("e1", 0, x_e1.T)
    store("e1")
    settle("s1", 0, x_s1.T)
    settle("e2", 0, x_e2)
    settle("s2", 0, x_s2.T)
    at = 0
    for t in range(tasks):
        settle("tower", t, x_small[at : at + th, :])
        at += th
    for t in range(tasks):
        settle("task", t, x_small[at : at + experts, :])
        at += 8
    settle("proj", every, x_small[at : at + dense, 0:width])
    settle("router", every, x_router[0:experts, :])

    moment_now = 0.9 * r.moment[...] + 0.1 * grad_final
    square_now = 0.95 * r.square[...] + 0.05 * grad_final * grad_final
    corrected = moment_now / (1.0 - 0.9**STEP)
    denom = jnp.sqrt(square_now / (1.0 - 0.95**STEP)) + 1e-08
    r.moment_next[...] = moment_now
    r.square_next[...] = square_now
    r.final_next[...] = r.final[...] * (1.0 - 0.0005) - 0.25 * corrected / denom
    for name in rest:
        if name != "e1":
            store(name)
    for copy in stores:
        copy.wait()
    for copy, back in passing:
        back.wait()


def update(sums, weights, momenta, final, passed):
    taken = dict(sums)
    taken |= {name + "_m": a for name, a in zip(MUON, momenta)}
    taken |= passed
    taken |= {name: a for name, a in zip((*MUON, "final", "moment", "square"), (*weights, *final))}
    given = [name + "_m" for name in MUON] + [*MUON, "final", "moment", "square"]
    outs = [*given, *passed]
    scratch = {name: (a.shape, a.dtype) for name, a in taken.items()}
    scratch |= {name + "_next": (taken[name].shape, F32) for name in given}
    semaphores = dict(
        load_sem=(len(taken),),
        pass_sem=(CHUNKS * len(passed) + 1,),
        store_sem=(len(given),),    )
    names = [name + "_hbm" for name in taken] + [name + "_next_hbm" for name in outs]
    names += [*scratch, *semaphores]
    anywhere = pl.BlockSpec(memory_space=pl.ANY)
    results = pl.pallas_call(
        functools.partial(update_kernel, tuple(sums), tuple(passed), names),
        in_specs=[anywhere] * len(taken),
        out_specs=[anywhere] * len(outs),
        out_shape=[jax.ShapeDtypeStruct(taken[name].shape, F32) for name in outs],
        scratch_shapes=[pltpu.VMEM(shape, kind) for shape, kind in scratch.values()]
        + [pltpu.SemaphoreType.DMA(shape) for shape in semaphores.values()],
        compiler_params=pltpu.CompilerParams(vmem_limit_bytes=60 * MIB),
    )(*taken.values())
    return dict(zip(outs, results))


def on_device(
    embedded,
    dense_features,
    labels,
    projector,
    projector_momentum,
    router,
    router_momentum,
    task_router,
    task_router_momentum,
    expand_one,
    expand_one_momentum,
    shrink_one,
    shrink_one_momentum,
    expand_two,
    expand_two_momentum,
    shrink_two,
    shrink_two_momentum,
    tower_hidden,
    tower_hidden_momentum,
    tower_final,
    tower_final_moment,
    tower_final_square,
):
    devices, blk = lax.axis_size("dp"), lax.axis_size("blk")
    total = embedded.shape[0] * devices * blk

    def turn(a):
        return jnp.swapaxes(a, -1, -2)

    router_t, task_t, tower_t = turn(router), turn(task_router), turn(tower_hidden)
    examples = (turn(embedded), turn(dense_features), turn(labels))
    matrices = (expand_one, shrink_one, expand_two, shrink_two)
    small = (projector, router_t, task_t, tower_t, tower_final)
    whole = blk <= 2 and devices // 2 * PAD == expand_one.shape[2] // 2
    if whole:
        logits, embedded_grad, early, late, sums = fused(
            blk, devices, float(total), examples[0], (*matrices, *examples[1:], *small)
        )
        sums = dict(early=early, late=late, small=sums)
        passed = dict(emb_grad=embedded_grad, logit=logits)
    else:
        everything = gather_weights(blk, *matrices)
        logits, embedded_grad, grads = compute(float(total), *examples, *small, everything)
        sums = dict(full=reduce_gradients(blk, devices, grads))
        passed = {}
    results = update(
        sums,
        [projector, router_t, task_t, expand_one, shrink_one, expand_two, shrink_two, tower_t],
        [
            projector_momentum,
            turn(router_momentum),
            turn(task_router_momentum),
            expand_one_momentum,
            shrink_one_momentum,
            expand_two_momentum,
            shrink_two_momentum,
            turn(tower_hidden_momentum),
        ],
        [tower_final, tower_final_moment, tower_final_square],
        passed,
    )
    if whole:
        embedded_grad, logits = results["emb_grad"], results["logit"]
    pairs = []
    for name in MUON:
        for value in (results[name + "_m"], results[name]):
            pairs.append(turn(value) if name in ("router", "task", "tower") else value)
    last = [results[name] for name in ("moment", "square", "final")]
    return (turn(logits), turn(embedded_grad), *pairs, *last)


def solution(mesh):
    rows, owned, whole = P(("dp", "blk"), None), P("blk", None, None), P()
    return jax.shard_map(
        on_device,
        mesh=mesh,
        in_specs=(rows,) * 3 + (whole,) * 6 + (owned,) * 8 + (whole,) * 5,
        out_specs=(rows,) * 2 + (whole,) * 6 + (owned,) * 8 + (whole,) * 5,
        check_vma=False,
    )
```

```python
import functools
import math
import types

import jax
import jax.numpy as jnp
from jax import lax
from jax.experimental import pallas as pl
from jax.experimental.pallas import tpu as pltpu
from jax.sharding import PartitionSpec as P

STEP = 5
NS_A = 3.4445
NS_B = -4.775
NS_C = 2.0315
C0 = math.sqrt(2.0 / math.pi)
C1 = C0 * 0.044715
LOW = jnp.bfloat16
F32 = jnp.float32
CODE = jnp.int16
MESH = pl.DeviceIdType.MESH
MIB = 2**20
PAD = 16
LANES = 128


def mm(a, b):
    return lax.dot_general(a, b, (((1,), (0,)), ((), ())), preferred_element_type=F32)


def mm_nt(a, b):
    return lax.dot_general(a, b, (((1,), (1,)), ((), ())), preferred_element_type=F32)


def gelu(x):
    square = x * x
    half = 0.5 * jnp.tanh(x * (C0 + C1 * square)) + 0.5
    value = x * half
    slope = half + (value - value * half) * (2.0 * C0 + 6.0 * C1 * square)
    return value, slope


def softmax_rows(logits):
    shifted = jnp.exp(logits - jnp.max(logits, axis=0, keepdims=True))
    return shifted / jnp.sum(shifted, axis=0, keepdims=True)


def stack_rows(rows, height):
    width = rows[0].shape[1]
    index = lax.broadcasted_iota(jnp.int32, (height, width), 0)
    out = jnp.zeros((height, width), F32)
    for i, row in enumerate(rows):
        out = jnp.where(index == i, row, out)
    return out


def pad_to(value, rows, columns):
    if value.shape[1] < columns:
        fill = jnp.zeros((value.shape[0], columns - value.shape[1]), F32)
        value = jnp.concatenate([value, fill], axis=1)
    if value.shape[0] < rows:
        fill = jnp.zeros((rows - value.shape[0], columns), F32)
        value = jnp.concatenate([value, fill], axis=0)
    return value


def encode(v):
    top = jnp.max(jnp.abs(v), axis=0, keepdims=True)
    power = jnp.ceil(jnp.log2(jnp.maximum(top, 1e-30)))
    whole = jnp.round(v * (16000.0 * jnp.exp2(-power))).astype(jnp.int32)
    row = lax.broadcasted_iota(jnp.int32, v.shape, 0) & 7
    bit = ((power.astype(jnp.int32) + 128) >> row) & 1
    return (2 * whole + bit).astype(CODE)


def decode(code):
    v = code.astype(jnp.int32)
    bit = v & 1
    row = lax.broadcasted_iota(jnp.int32, v.shape, 0) & 7
    power = jnp.sum((bit << row).astype(F32)[0:8], axis=0, keepdims=True) - 128.0
    return (v - bit).astype(F32) * (jnp.exp2(power) * (1.0 / 32000.0))


def weights_kernel(e1_ref, s1_ref, e2_ref, s2_ref, all_ref, send, recv, send_core, recv_core):
    blk = lax.axis_size("blk")
    dp, me = lax.axis_index("dp"), lax.axis_index("blk")
    core = lax.rem(dp, 2)
    sibling = dp + 1 - 2 * core
    rows = all_ref.shape[1]
    half = rows // 2

    barrier = pltpu.get_barrier_semaphore()
    for step in range(1, blk):
        peer = lax.rem(me + step, blk)
        pl.semaphore_signal(barrier, inc=1, device_id=(dp, peer), device_id_type=MESH)
    pl.semaphore_signal(barrier, inc=1, device_id=(sibling, me), device_id_type=MESH)
    din, out = e1_ref.shape[1], e2_ref.shape[1]
    all_ref[me, 0:din, :] = e1_ref[0].astype(LOW)
    all_ref[me, din : din + out, :] = e2_ref[0].astype(LOW)
    all_ref[me, din + out :, 0:out] = s1_ref[0].astype(LOW)
    all_ref[me, din + out :, out : 2 * out] = s2_ref[0].astype(LOW)
    pl.semaphore_wait(barrier, blk)

    mine = pl.ds(pl.multiple_of(core * half, 16), half)
    copies = []
    for step in range(1, blk):
        peer = lax.rem(me + step, blk)
        copy = pltpu.make_async_remote_copy(
            src_ref=all_ref.at[me, mine],
            dst_ref=all_ref.at[me, mine],
            send_sem=send.at[step],
            recv_sem=recv.at[step],
            device_id=(dp, peer),
            device_id_type=MESH,
        )
        copy.start()
        copies.append(copy)
    forwards = []
    for step in range(1, blk):
        source = lax.rem(me - step + blk, blk)
        copies[step - 1].wait_recv()
        copy = pltpu.make_async_remote_copy(
            src_ref=all_ref.at[source, mine],
            dst_ref=all_ref.at[source, mine],
            send_sem=send_core.at[step],
            recv_sem=recv_core.at[step],
            device_id=(sibling, me),
            device_id_type=MESH,
        )
        copy.start()
        forwards.append(copy)
    for copy in copies:
        copy.wait_send()
    for copy in forwards:
        copy.wait()


def gather_weights(blk, e1, s1, e2, s2):
    rows = e1.shape[1] + e2.shape[1] + s1.shape[1]
    return pl.pallas_call(
        weights_kernel,
        out_shape=jax.ShapeDtypeStruct((blk, rows, e1.shape[2]), LOW),
        in_specs=[pl.BlockSpec(memory_space=pltpu.VMEM)] * 4,
        out_specs=pl.BlockSpec(memory_space=pltpu.VMEM),
        scratch_shapes=[pltpu.SemaphoreType.DMA((blk,)) for _ in range(4)],
        compiler_params=pltpu.CompilerParams(
            collective_id=0, has_side_effects=True, vmem_limit_bytes=16 * MIB
        ),
    )(e1, s1, e2, s2)


def compute_kernel(
    total,
    emb_ref,
    dense_ref,
    labels_ref,
    proj_ref,
    router_ref,
    task_ref,
    tower_ref,
    final_ref,
    all_ref,
    logit_ref,
    emb_grad_ref,
    grads_ref,
    a1,
    a2,
    b1,
    b2,
    s1t,
    s2t,
    s1n,
    s2n,
    tow,
    tow_n,
    fin,
    projt,
    col1,
    col2,
    x_ref,
    d1,
    d2,
    hid1,
    hid2,
    dtp,
    acc_r,
    acc_t,
    acc_p,
    acc_tow,
    acc_f,
):
    experts, h = all_ref.shape[0], all_ref.shape[2]
    tasks, th, out = tower_ref.shape
    emb, tile = emb_ref.shape
    din = router_ref.shape[1]
    eh = experts * h
    repeat = tile // LANES
    step = pl.program_id(0)
    side = din + 3 * out

    def wide(column):
        return jnp.concatenate([column] * repeat, axis=1)

    @pl.when(step == 0)
    def _():
        for e in range(experts):
            span = slice(e * h, (e + 1) * h)
            e1 = all_ref[e, 0:din, :]
            e2 = all_ref[e, din : din + out, :]
            s1 = all_ref[e, din + out :, 0:out]
            s2 = all_ref[e, din + out :, out : 2 * out]
            a1[span, :] = e1.T
            a2[span, :] = e2.T
            b1[:, span] = e1
            b2[:, span] = e2
            s1t[e] = s1.T
            s2t[e] = s2.T
            s1n[e] = s1
            s2n[e] = s2
        router = stack_rows([router_ref[e : e + 1, :] for e in range(experts)], PAD).astype(LOW)
        a1[eh:, :] = router
        router_t = pad_to(router.astype(F32), LANES, din).T
        pairs = [task_ref[t, e : e + 1, :] for t in range(tasks) for e in range(experts)]
        task = stack_rows(pairs, PAD).astype(LOW)
        a2[eh:, :] = task
        task_t = pad_to(task.astype(F32), LANES, out).T
        for e in range(experts):
            col1[e] = jnp.broadcast_to(router_t[:, e : e + 1], (din, LANES))
        for k in range(tasks * experts):
            col2[k] = jnp.broadcast_to(task_t[:, k : k + 1], (out, LANES))
        tow_n[...] = jnp.zeros_like(tow_n)
        final_t = stack_rows([final_ref[t : t + 1, :] for t in range(tasks)], 8).T
        for t in range(tasks):
            tow[t] = tower_ref[t].astype(LOW)
            tow_n[t * out : (t + 1) * out, t * th : (t + 1) * th] = tower_ref[t].T.astype(LOW)
            fin[t] = jnp.broadcast_to(final_t[:, t : t + 1], (th, LANES))
        projt[...] = proj_ref[...].T.astype(LOW)
        grads_ref[...] = jnp.zeros_like(grads_ref)
        acc_r[...] = jnp.zeros_like(acc_r)
        acc_t[...] = jnp.zeros_like(acc_t)
        acc_p[...] = jnp.zeros_like(acc_p)
        acc_tow[...] = jnp.zeros_like(acc_tow)
        acc_f[...] = jnp.zeros_like(acc_f)

    x_ref[0:emb, :] = emb_ref[...]
    x_ref[emb:, :] = mm(projt[...], dense_ref[...]).astype(LOW)
    x = x_ref[...]
    pre1 = mm(a1[...], x)
    gate1 = softmax_rows(pre1[eh : eh + experts, :])
    mid = jnp.zeros((out, tile), F32)
    slope1, mslope1, outs1 = [], [], []
    for e in range(experts):
        value, slope = gelu(pre1[e * h : (e + 1) * h, :])
        hid1[e] = value.astype(LOW)
        slope1.append(slope)
        mixed, mslope = gelu(mm(s1t[e], hid1[e]))
        outs1.append(mixed)
        mslope1.append(mslope)
        mid = mid + gate1[e : e + 1, :] * mixed
    mid = mid.astype(LOW)

    pre2 = mm(a2[...], mid)
    gate2 = []
    for t in range(tasks):
        first = eh + t * experts
        gate2.append(softmax_rows(pre2[first : first + experts, :]))
    slope2, mslope2, outs2 = [], [], []
    rep = [jnp.zeros((out, tile), F32) for _ in range(tasks)]
    for e in range(experts):
        value, slope = gelu(pre2[e * h : (e + 1) * h, :])
        hid2[e] = value.astype(LOW)
        slope2.append(slope)
        mixed, mslope = gelu(mm(s2t[e], hid2[e]))
        outs2.append(mixed)
        mslope2.append(mslope)
        for t in range(tasks):
            rep[t] = rep[t] + gate2[t][e : e + 1, :] * mixed

    for t in range(tasks):
        rep_low = rep[t].astype(LOW)
        act, tslope = gelu(mm(tow[t], rep_low))
        weight = wide(fin[t])
        logit = jnp.sum(act * weight, axis=0, keepdims=True)
        logit_ref[t : t + 1, :] = logit
        d_logit = (jax.nn.sigmoid(logit) - labels_ref[t : t + 1, :].astype(F32)) / total
        part = act * d_logit
        lump = part[:, 0:LANES]
        for k in range(1, repeat):
            lump = lump + part[:, k * LANES : (k + 1) * LANES]
        acc_f[t] += lump
        d_tp = (tslope * (d_logit * weight)).astype(LOW)
        dtp[t * th : (t + 1) * th, :] = d_tp
        acc_tow[t] += mm_nt(d_tp, rep_low)
    d_rep = mm(tow_n[...], dtp[...])

    d_gate2 = [[None] * experts for _ in range(tasks)]
    for e in range(experts):
        d_out = jnp.zeros((out, tile), F32)
        for t in range(tasks):
            piece = d_rep[t * out : (t + 1) * out, :]
            d_out = d_out + gate2[t][e : e + 1, :] * piece
            d_gate2[t][e] = jnp.sum(outs2[e] * piece, axis=0, keepdims=True)
        d_mixed = (mslope2[e] * d_out).astype(LOW)
        grads_ref[e, :, din + 2 * out : side] += mm_nt(hid2[e], d_mixed)
        d2[e * h : (e + 1) * h, :] = (slope2[e] * mm(s2n[e], d_mixed)).astype(LOW)
    rows = []
    for t in range(tasks):
        inner = sum(gate2[t][e : e + 1, :] * d_gate2[t][e] for e in range(experts))
        for e in range(experts):
            row = gate2[t][e : e + 1, :] * (d_gate2[t][e] - inner)
            rows.append(row.astype(LOW).astype(F32))
    d2[eh:, :] = stack_rows(rows, PAD).astype(LOW)
    g2 = mm_nt(d2[...], mid)
    for e in range(experts):
        grads_ref[e, :, din + out : din + 2 * out] += g2[e * h : (e + 1) * h, :]
    acc_t[...] += g2[eh:, :]
    d_mid = mm(b2[...], d2[0:eh, :])
    for k, row in enumerate(rows):
        d_mid = d_mid + wide(col2[k]) * row

    d_gate1 = []
    for e in range(experts):
        d_gate1.append(jnp.sum(outs1[e] * d_mid, axis=0, keepdims=True))
        d_mixed = (mslope1[e] * (gate1[e : e + 1, :] * d_mid)).astype(LOW)
        grads_ref[e, :, din : din + out] += mm_nt(hid1[e], d_mixed)
        d1[e * h : (e + 1) * h, :] = (slope1[e] * mm(s1n[e], d_mixed)).astype(LOW)
    inner = sum(gate1[e : e + 1, :] * d_gate1[e] for e in range(experts))
    rows = []
    for e in range(experts):
        row = gate1[e : e + 1, :] * (d_gate1[e] - inner)
        rows.append(row.astype(LOW).astype(F32))
    d1[eh:, :] = stack_rows(rows, PAD).astype(LOW)
    g1 = mm_nt(d1[...], x)
    for e in range(experts):
        grads_ref[e, :, 0:din] += g1[e * h : (e + 1) * h, :]
    acc_r[...] += g1[eh:, :]
    d_in = mm(b1[...], d1[0:eh, :])
    for e in range(experts):
        d_in = d_in + wide(col1[e]) * rows[e]
    emb_grad_ref[...] = d_in[:emb, :]
    tail = d_in[emb:, :]
    high = tail.astype(LOW)
    rest = (tail - high.astype(F32)).astype(LOW)
    acc_p[...] += mm_nt(dense_ref[...], high) + mm_nt(dense_ref[...], rest)

    @pl.when(step == pl.num_programs(0) - 1)
    def _():
        finals = [jnp.sum(acc_f[t].T, axis=0, keepdims=True) for t in range(tasks)]
        pieces = [acc_tow[t] for t in range(tasks)]
        pieces += [acc_r[:, k * out : (k + 1) * out] for k in range(din // out)]
        pieces += [acc_t[...], pad_to(acc_p[...], PAD, out)]
        pieces += [pad_to(stack_rows(finals, PAD), PAD, out)]
        at = 0
        for piece in pieces:
            for e in range(experts):
                grads_ref[e, at : at + piece.shape[0], side:] = piece
            at += piece.shape[0]


def compute(total, emb, dense, labels, proj, router, task, tower, final, everything):
    experts, _, h = everything.shape
    tasks, th, out = tower.shape
    width, rows = emb.shape
    din = router.shape[1]
    eh = experts * h
    tile = min(rows, max(LANES, 2048 // experts))

    def full(a):
        return pl.BlockSpec(a.shape, lambda i, n=a.ndim: (0,) * n)

    def part(height):
        return pl.BlockSpec((height, tile), lambda i: (0, i))

    scratch = [
        ((eh + PAD, din), LOW),
        ((eh + PAD, out), LOW),
        ((din, eh), LOW),
        ((out, eh), LOW),
        ((experts, out, h), LOW),
        ((experts, out, h), LOW),
        ((experts, h, out), LOW),
        ((experts, h, out), LOW),
        ((tasks, th, out), LOW),
        ((tasks * out, tasks * th), LOW),
        ((tasks, th, LANES), F32),
        ((proj.shape[1], proj.shape[0]), LOW),
        ((experts, din, LANES), F32),
        ((tasks * experts, out, LANES), F32),
        ((din, tile), LOW),
        ((eh + PAD, tile), LOW),
        ((eh + PAD, tile), LOW),
        ((experts, h, tile), LOW),
        ((experts, h, tile), LOW),
        ((tasks * th, tile), LOW),
        ((PAD, din), F32),
        ((PAD, out), F32),
        (proj.shape, F32),
        ((tasks, th, out), F32),
        ((tasks, th, LANES), F32),
    ]
    small = (proj, router, task, tower, final, everything)
    return pl.pallas_call(
        functools.partial(compute_kernel, total),
        grid=(rows // tile,),
        in_specs=[part(width), part(dense.shape[0]), part(tasks)] + [full(a) for a in small],
        out_specs=[
            part(tasks),
            part(width),
            pl.BlockSpec((experts, h, din + 4 * out), lambda i: (0, 0, 0)),
        ],
        out_shape=[
            jax.ShapeDtypeStruct((tasks, rows), F32),
            jax.ShapeDtypeStruct(emb.shape, F32),
            jax.ShapeDtypeStruct((experts, h, din + 4 * out), F32),
        ],
        scratch_shapes=[pltpu.VMEM(shape, kind) for shape, kind in scratch],
        compiler_params=pltpu.CompilerParams(vmem_limit_bytes=56 * MIB),
    )(emb, dense, labels, *small)


def reduce_kernel(
    grads_ref,
    full_ref,
    pair_out,
    pair_in,
    pieces,
    landed,
    gathered,
    pair_sem,
    send,
    recv,
    spread_send,
    spread_recv,
    core_send,
    core_recv,
):
    blk, devices = lax.axis_size("blk"), lax.axis_size("dp")
    chips = devices // 2
    dp, me = lax.axis_index("dp"), lax.axis_index("blk")
    core = lax.rem(dp, 2)
    chip = lax.div(dp, 2)
    sibling = dp + 1 - 2 * core
    height, columns = pieces.shape[1:]
    half = grads_ref.shape[1] // 2
    blocks = half // height
    slots = blk * chips
    own = me * chips + chip

    def place(k):
        return (lax.rem(k, blocks) * height, lax.div(k, blocks) * columns)

    def peer(step):
        to = lax.rem(own + step, slots)
        return to, (lax.rem(to, chips) * 2 + core, lax.div(to, chips))

    def source(step):
        return lax.rem(own - step + slots, slots)

    barrier = pltpu.get_barrier_semaphore()

    def greet(step, unused):
        pl.semaphore_signal(barrier, inc=1, device_id=peer(step)[1], device_id_type=MESH)
        return unused

    lax.fori_loop(1, slots, greet, 0)
    pl.semaphore_signal(barrier, inc=1, device_id=(sibling, me), device_id_type=MESH)

    other = (1 - core) * half
    first = core * half
    for e in range(blk):

        def code(j, unused, e=e):
            at = pl.multiple_of(other + j * PAD, PAD)
            to = pl.ds(pl.multiple_of(j * PAD, PAD), PAD)
            pair_out[e, to, :] = encode(grads_ref[e, pl.ds(at, PAD), :])
            return unused

        lax.fori_loop(0, half // PAD, code, 0)
    pl.semaphore_wait(barrier, slots)

    pair = pltpu.make_async_remote_copy(
        src_ref=pair_out,
        dst_ref=pair_in,
        send_sem=pair_sem.at[0],
        recv_sem=pair_sem.at[1],
        device_id=(sibling, me),
        device_id_type=MESH,
    )
    pair.start()
    pair.wait_recv()

    def outgoing(step):
        to, device = peer(step)
        return pltpu.make_async_remote_copy(
            src_ref=pieces.at[to],
            dst_ref=landed.at[own],
            send_sem=send.at[step],
            recv_sem=recv.at[step],
            device_id=device,
            device_id_type=MESH,
        )

    def prepare(to):
        e = lax.div(to, chips)
        row, column = place(lax.rem(to, chips))
        row = pl.multiple_of(row, height)
        span = pl.ds(pl.multiple_of(column, LANES), columns)
        mine = grads_ref[e, pl.ds(pl.multiple_of(first + row, height), height), span]
        return encode(mine + decode(pair_in[e, pl.ds(row, height), span]))

    def ship(step, unused):
        to = peer(step)[0]
        pieces[to] = prepare(to)
        outgoing(step).start()
        return unused

    lax.fori_loop(1, slots, ship, 0)
    landed[own] = prepare(own)

    def arrive(step, unused):
        outgoing(step).wait_recv()
        return unused

    lax.fori_loop(1, slots, arrive, 0)

    def add(slot, partial):
        return partial + decode(landed[slot])

    summed = lax.fori_loop(0, slots, add, jnp.zeros((height, columns), F32))

    def where(k, c):
        row, column = place(k)
        row = pl.multiple_of(c * half + row, height)
        return pl.ds(row, height), pl.ds(pl.multiple_of(column, LANES), columns)

    rows_own, columns_own = where(chip, core)
    gathered[rows_own, columns_own] = encode(summed)

    def spread(step):
        to = lax.rem(chip + step, chips)
        return pltpu.make_async_remote_copy(
            src_ref=gathered.at[rows_own, columns_own],
            dst_ref=gathered.at[rows_own, columns_own],
            send_sem=spread_send.at[step],
            recv_sem=spread_recv.at[step],
            device_id=(to * 2 + core, me),
            device_id_type=MESH,
        )

    def forward(step):
        rows, span = where(lax.rem(chip - step + chips, chips), core)
        return pltpu.make_async_remote_copy(
            src_ref=gathered.at[rows, span],
            dst_ref=gathered.at[rows, span],
            send_sem=core_send.at[step],
            recv_sem=core_recv.at[step],
            device_id=(sibling, me),
            device_id_type=MESH,
        )

    def spread_start(step, unused):
        spread(step).start()
        return unused

    lax.fori_loop(1, chips, spread_start, 0)
    forward(0).start()

    def pass_on(step, unused):
        spread(step).wait_recv()
        forward(step).start()
        return unused

    lax.fori_loop(1, chips, pass_on, 0)

    def finish(step, unused):
        forward(step).wait()
        return unused

    lax.fori_loop(0, chips, finish, 0)

    def write(j, unused):
        at = pl.ds(pl.multiple_of(j * PAD, PAD), PAD)
        full_ref[at, :] = decode(gathered[at, :])
        return unused

    lax.fori_loop(0, full_ref.shape[0] // PAD, write, 0)

    pair.wait_send()

    def drain(step, unused):
        outgoing(step).wait_send()
        return unused

    lax.fori_loop(1, slots, drain, 0)

    def drain_spread(step, unused):
        spread(step).wait_send()
        return unused

    lax.fori_loop(1, chips, drain_spread, 0)


def reduce_gradients(blk, devices, grads):
    _, h, width = grads.shape
    chips = devices // 2
    blocks = h // 2 // PAD
    columns = width * blocks // chips
    slots = blk * chips
    dma = pltpu.SemaphoreType.DMA
    return pl.pallas_call(
        reduce_kernel,
        out_shape=jax.ShapeDtypeStruct((h, width), F32),
        in_specs=[pl.BlockSpec(memory_space=pltpu.VMEM)],
        out_specs=pl.BlockSpec(memory_space=pltpu.VMEM),
        scratch_shapes=[
            pltpu.VMEM((blk, h // 2, width), CODE),
            pltpu.VMEM((blk, h // 2, width), CODE),
            pltpu.VMEM((slots, PAD, columns), CODE),
            pltpu.VMEM((slots, PAD, columns), CODE),
            pltpu.VMEM((h, width), CODE),
            dma((2,)),
            dma((slots,)),
            dma((slots,)),
            dma((chips,)),
            dma((chips,)),
            dma((chips,)),
            dma((chips,)),
        ],
        compiler_params=pltpu.CompilerParams(
            collective_id=1, has_side_effects=True, vmem_limit_bytes=32 * MIB
        ),
    )(grads)


MATRIX, VECTOR = range(2)


def drive(steps):
    live = [[one, next(one), k] for k, one in enumerate(steps)]
    while live:
        due = [item for item in live if item[2] == 0]
        for item in live:
            item[2] = max(0, item[2] - 1)
        for kind in (VECTOR, MATRIX):
            for item in [item for item in due if item[1] == kind]:
                item[1] = next(item[0], None)
                due.remove(item)
        live = [item for item in live if item[1] is not None]


def put(ref, at, value, first):
    if first:
        ref[at] = value
    else:
        ref[at] += value


EARLY, MIDDLE, LATE, SMALL = range(4)


def fused_kernel(total, names, *refs):
    table = dict(zip(names, refs))
    r = types.SimpleNamespace(**table)
    blk, devices = lax.axis_size("blk"), lax.axis_size("dp")
    chips = devices // 2
    dp, me = lax.axis_index("dp"), lax.axis_index("blk")
    core, chip = lax.rem(dp, 2), lax.div(dp, 2)
    sibling = dp + 1 - 2 * core
    experts = blk
    w1, w2 = r.w1, r.w2
    din, h = w1.shape[1:]
    tasks, th, out = r.tower.shape
    width, rows = r.emb_hbm.shape
    eh = experts * h
    tile = TILE
    count = rows // tile
    half = h // 2
    tiles = range(count)

    def owner(s):
        return lax.rem(me + s, blk)

    line, b = lax.div(chip, 2), lax.rem(chip, 2)
    lines = chips // 2
    plane_rows = half // 2
    others = [(s, bb) for s in range(blk) for bb in (1, 0) if s or bb]

    def at_chip(line, b):
        return (line * 2 + b) * 2 + core

    def order(s):
        return (s + experts - 1) % experts * h

    def remote(src, dst, send, recv, device):
        return pltpu.make_async_remote_copy(
            src_ref=src,
            dst_ref=dst,
            send_sem=send,
            recv_sem=recv,
            device_id=device,
            device_id_type=MESH,
        )

    barrier = pltpu.get_barrier_semaphore()
    met = [(sibling, me), (at_chip(line ^ 1, b), me), (at_chip(line ^ 2, b), me)]
    met += [(at_chip(line, b ^ bb), owner(s)) for s, bb in others]
    for device in met:
        pl.semaphore_signal(barrier, inc=1, device_id=device, device_id_type=MESH)

    x, d1, d2, hid2, mid, reps, dtp, dm1, dm2, hid1 = [
        [table[name + str(i)] for i in range(count * (experts if name == HID1 else 1))]
        for name in (*TILED, HID1)
    ]
    loads = {}
    for k, name in enumerate(LOADED):
        loads[name] = pltpu.make_async_copy(table[name + "_hbm"], table[name], r.load_sem.at[k])
        loads[name].start()
    emb_loads = []
    for i in range(count):
        span = slice(i * tile, (i + 1) * tile)
        copy = pltpu.make_async_copy(
            r.emb_hbm.at[:, span], x[i].at[0:width], r.emb_sem.at[i]
        )
        copy.start()
        emb_loads.append(copy)

    for name in ("e1", "s1", "e2", "s2"):
        loads[name].wait()
    w1[0] = r.e1[0].astype(LOW)
    w2[0, 0:out, :] = r.e2[0].astype(LOW)
    w2[0, out:, 0:out] = r.s1[0].astype(LOW)
    w2[0, out:, out : 2 * out] = r.s2[0].astype(LOW)

    a1, a2, b1, b2 = r.a1, r.a2, r.b1, r.b2

    def set_first(s):
        e1 = w1[s]
        a1[s * h : (s + 1) * h, :] = e1.T
        b1[:, order(s) : order(s) + h] = e1

    def set_rest(s):
        e2 = w2[s, 0:out, :]
        s1, s2 = w2[s, out:, 0:out], w2[s, out:, out : 2 * out]
        a2[s * h : (s + 1) * h, :] = e2.T
        b2[:, s * h : (s + 1) * h] = e2
        r.s1t[s], r.s2t[s] = s1.T, s2.T
        r.s1n[s], r.s2n[s] = s1, s2

    pl.semaphore_wait(barrier, len(met))
    pl.semaphore_signal(r.relay, inc=1, device_id=met[1], device_id_type=MESH)

    def weight_copy(s, part):
        ref = (w1, w2)[part]
        size = ref.shape[1] // 2
        mine = pl.ds(pl.multiple_of(core * size, PAD), size)
        return remote(
            ref.at[0, mine],
            ref.at[blk - s, mine],
            r.w_send.at[s, part],
            r.w_recv.at[s, part],
            (dp, owner(s)),
        )

    def weight_forward(s, part):
        ref = (w1, w2)[part]
        size = ref.shape[1] // 2
        mine = pl.ds(pl.multiple_of(core * size, PAD), size)
        return remote(
            ref.at[s, mine],
            ref.at[s, mine],
            r.wc_send.at[s, part],
            r.wc_recv.at[s, part],
            (sibling, me),
        )

    for part in range(2):
        for s in range(1, blk):
            weight_copy(s, part).start()

    set_first(0)
    set_rest(0)
    for name in LOADED[4:]:
        loads[name].wait()
    router = stack_rows([r.router[pl.ds(owner(s), 1), :] for s in range(experts)], PAD)
    router = router.astype(LOW)
    a1[eh:, :] = router
    router_t = pad_to(router.astype(F32), LANES, din).T
    r.gate_tail[...] = router_t[width:, 0:PAD].astype(LOW)
    pairs = [r.task[t, pl.ds(owner(s), 1), :] for t in range(tasks) for s in range(experts)]
    task = stack_rows(pairs, PAD).astype(LOW)
    a2[eh:, :] = task
    task_t = pad_to(task.astype(F32), LANES, out).T
    for s in range(experts):
        r.col1[s] = jnp.broadcast_to(router_t[0:width, s : s + 1], (width, LANES))
    for k in range(tasks * experts):
        r.col2[k] = jnp.broadcast_to(task_t[:, k : k + 1], (out, LANES))
    r.tow_n[...] = jnp.zeros_like(r.tow_n)
    final_t = stack_rows([r.final[t : t + 1, :] for t in range(tasks)], 8).T
    for t in range(tasks):
        r.tow[t] = r.tower[t].astype(LOW)
        r.tow_n[t * out : (t + 1) * out, t * th : (t + 1) * th] = r.tower[t].T.astype(LOW)
        r.fin[t] = jnp.broadcast_to(final_t[:, t : t + 1], (th, LANES))
    r.projt[...] = r.proj[...].T.astype(LOW)

    sl1, out1, msl1, dmid, gate1_ref = r.sl1, r.out1, r.msl1, r.dmid, r.gate1
    p2, q2, ms2, gate2, tp, dr, dh = r.p2, r.q2, r.ms2, r.gate2, r.tp, r.dr, r.dh
    eg, lines1, lines2 = r.eg, r.lines1, r.lines2
    g_late, g_middle, g_early, g_small = r.g_late, r.g_middle, r.g_early, r.g_small
    stores = []

    def chunked(height, w, step, body):
        for left in range(w.start, w.stop, step):
            columns = slice(left, left + step)
            for top in range(0, height, PAD):
                body(slice(top, top + PAD), columns)

    def local(columns):
        left = columns.start % tile
        return slice(left, left + columns.stop - columns.start)

    def narrow(column, step):
        return jnp.concatenate([column] * (step // LANES), axis=1)

    def layer_one(i, s):
        w = slice(i * tile, (i + 1) * tile)
        yield MATRIX
        if s == 0:
            emb_loads[i].wait()
            x[i][width:, :] = mm(r.projt[...], r.dense[:, w]).astype(LOW)
            sl1[s, :, w] = mm(a1[0:h, :], x[i][...])
            gate1_ref[:, w] = softmax_rows(mm(a1[eh:, :], x[i][...])[0:experts, :])
        else:
            sl1[s, :, w] = mm(a1[s * h : (s + 1) * h, :], x[i][...])
        yield VECTOR

        def hidden(rows, columns):
            value, slope = gelu(sl1[s, rows, columns])
            hid1[s * count + i][rows, local(columns)] = value.astype(LOW)
            sl1[s, rows, columns] = slope

        chunked(h, w, STEP_COLUMNS, hidden)

    def layer_one_out(i, s):
        w = slice(i * tile, (i + 1) * tile)
        yield MATRIX
        out1[s, :, w] = mm(r.s1t[s], hid1[s * count + i][...])
        yield VECTOR

        def mixed(rows, columns):
            value, slope = gelu(out1[s, rows, columns])
            out1[s, rows, columns] = value
            msl1[s, rows, columns] = slope
            if s == experts - 1:
                total_out = gate1_ref[s : s + 1, columns] * value
                for other in range(experts - 1):
                    gate = gate1_ref[other : other + 1, columns]
                    total_out = total_out + gate * out1[other, rows, columns]
                mid[i][rows, local(columns)] = total_out.astype(LOW)

        chunked(out, w, STEP_COLUMNS, mixed)

    def layer_two(i):
        w = slice(i * tile, (i + 1) * tile)
        first = i == 0
        pairs_of = [(t, s) for t in range(tasks) for s in range(experts)]
        yield MATRIX
        p2[:, w] = mm(a2[...], mid[i][...])
        yield VECTOR
        for t in range(tasks):
            at = eh + t * experts
            gate2[t * experts : (t + 1) * experts, w] = softmax_rows(p2[at : at + experts, w])

        def hidden(rows, columns):
            value, slope = gelu(p2[rows, columns])
            hid2[i][rows, local(columns)] = value.astype(LOW)
            p2[rows, columns] = slope

        chunked(eh, w, STEP_COLUMNS, hidden)
        yield MATRIX
        for s in range(experts):
            q2[s, :, w] = mm(r.s2t[s], hid2[i][s * h : (s + 1) * h, :])
        yield VECTOR

        def mixed(rows, columns):
            rep = [None] * tasks
            for s in range(experts):
                value, slope = gelu(q2[s, rows, columns])
                q2[s, rows, columns] = value
                ms2[s, rows, columns] = slope
                for t in range(tasks):
                    k = t * experts + s
                    term = gate2[k : k + 1, columns] * value
                    rep[t] = term if s == 0 else rep[t] + term
            for t in range(tasks):
                reps[i][t, rows, local(columns)] = rep[t].astype(LOW)

        chunked(out, w, STEP_COLUMNS, mixed)
        yield MATRIX
        for t in range(tasks):
            tp[t * th : (t + 1) * th, w] = mm(r.tow[t], reps[i][t])
        yield VECTOR
        lumps = [None] * tasks
        for left in range(w.start, w.stop, STEP_COLUMNS):
            columns = slice(left, left + STEP_COLUMNS)
            for t in range(tasks):
                at = slice(t * th, (t + 1) * th)
                weight = narrow(r.fin[t], STEP_COLUMNS)
                act, slope = gelu(tp[at, columns])
                logit = jnp.sum(act * weight, axis=0, keepdims=True)
                r.logit[t : t + 1, columns] = logit
                label = r.labels[t : t + 1, columns].astype(F32)
                d_logit = (jax.nn.sigmoid(logit) - label) / total
                dtp[i][at, local(columns)] = (slope * weight * d_logit).astype(LOW)
                part = act * d_logit
                for k in range(0, STEP_COLUMNS, LANES):
                    piece = part[:, k : k + LANES]
                    lumps[t] = piece if lumps[t] is None else lumps[t] + piece
        for t in range(tasks):
            put(r.acc_f, t, lumps[t], first)
        yield MATRIX
        dr[:, w] = mm(r.tow_n[...], dtp[i][...])
        for t in range(tasks):
            span = slice(t * th, (t + 1) * th)
            put(g_small, span, mm_nt(dtp[i][span, :], reps[i][t]), first)
        yield VECTOR
        for left in range(w.start, w.stop, STEP_COLUMNS):
            columns = slice(left, left + STEP_COLUMNS)
            sums = [None] * (tasks * experts)
            for top in range(0, out, PAD):
                rows = slice(top, top + PAD)
                piece = [dr[t * out + top : t * out + top + PAD, columns] for t in range(tasks)]
                for s in range(experts):
                    value = q2[s, rows, columns]
                    d_out = None
                    for t in range(tasks):
                        k = t * experts + s
                        term = gate2[k : k + 1, columns] * piece[t]
                        d_out = term if t == 0 else d_out + term
                        part = value * piece[t]
                        sums[k] = part if top == 0 else sums[k] + part
                    slope = ms2[s, rows, columns]
                    dm2[i][s, rows, local(columns)] = (slope * d_out).astype(LOW)
            d_gate = [jnp.sum(part, axis=0, keepdims=True) for part in sums]
            lines = []
            for t in range(tasks):
                gates = [
                    gate2[t * experts + s : t * experts + s + 1, columns] for s in range(experts)
                ]
                inner = sum(gates[s] * d_gate[t * experts + s] for s in range(experts))
                for s in range(experts):
                    lines.append(gates[s] * (d_gate[t * experts + s] - inner))
            lines = stack_rows(lines, PAD).astype(LOW)
            d2[i][eh:, local(columns)] = lines
            lines2[:, columns] = lines.astype(F32)
        yield MATRIX
        for s in range(experts):
            dh[s, :, w] = mm(r.s2n[s], dm2[i][s])
        yield VECTOR

        def before(rows, columns):
            s, top = divmod(rows.start, h)
            d_hidden = dh[s, top : top + PAD, columns]
            d2[i][rows, local(columns)] = (p2[rows, columns] * d_hidden).astype(LOW)

        chunked(eh, w, STEP_COLUMNS, before)
        yield MATRIX
        for s in range(experts):
            at = (s, slice(None), slice(out, 2 * out))
            put(g_early, at, mm_nt(hid2[i][s * h : (s + 1) * h, :], dm2[i][s]), first)
        both = mm_nt(d2[i][...], mid[i][...])
        for s in range(experts):
            put(g_early, (s, slice(None), slice(0, out)), both[s * h : (s + 1) * h, :], first)
        put(r.acc_t, Ellipsis, both[eh:, :], first)
        dmid[:, w] = mm(b2[...], d2[i][0:eh, :])
        yield VECTOR

        def gates_too(rows, columns):
            value = dmid[rows, columns]
            for k in range(tasks * experts):
                line = lines2[k : k + 1, columns]
                value = value + narrow(r.col2[k, rows, :], STEP_COLUMNS) * line
            dmid[rows, columns] = value

        chunked(out, w, STEP_COLUMNS, gates_too)

    def matrix_grad(first, last):
        left = jnp.concatenate([d1[i][first:last, :] for i in tiles], axis=1)
        return mm_nt(left, jnp.concatenate([x[i][...] for i in tiles], axis=1))

    def back_one(i, s):
        w = slice(i * tile, (i + 1) * tile)
        yield VECTOR
        for left in range(w.start, w.stop, STEP_COLUMNS):
            columns = slice(left, left + STEP_COLUMNS)
            gate = gate1_ref[s : s + 1, columns]
            sums = None
            for top in range(0, out, PAD):
                rows = slice(top, top + PAD)
                d_out = dmid[rows, columns]
                part = out1[s, rows, columns] * d_out
                sums = part if top == 0 else sums + part
                slope = msl1[s, rows, columns]
                dm1[i][rows, local(columns)] = (slope * (gate * d_out)).astype(LOW)
            r.dgate1[s : s + 1, columns] = jnp.sum(sums, axis=0, keepdims=True)
            if s == 0:
                gates, d_gates = gate1_ref[:, columns], r.dgate1[:, columns]
                inner = jnp.sum(gates * d_gates, axis=0, keepdims=True)
                lines = pad_to(gates * (d_gates - inner), PAD, STEP_COLUMNS).astype(LOW)
                d1[i][eh:, local(columns)] = lines
                lines1[:, columns] = lines.astype(F32)
        yield MATRIX
        dh[s, :, w] = mm(r.s1n[s], dm1[i][...])
        put(g_middle, s, mm_nt(hid1[s * count + i][...], dm1[i][...]), i == 0)
        yield VECTOR

        def before(rows, columns):
            at = order(s) + rows.start
            d_hidden = dh[s, rows, columns]
            d_pre = (sl1[s, rows, columns] * d_hidden).astype(LOW)
            d1[i][at : at + PAD, local(columns)] = d_pre

        chunked(h, w, STEP_COLUMNS, before)

    def input_grad(i):
        w = slice(i * tile, (i + 1) * tile)
        yield MATRIX
        eg[:, w] = mm(b1[0:width, :], d1[i][0:eh, :])
        yield VECTOR

        def gates_too(rows, columns):
            value = eg[rows, columns]
            for s in range(experts):
                gate = lines1[s : s + 1, columns]
                value = value + narrow(r.col1[s, rows, :], STEP_COLUMNS) * gate
            eg[rows, columns] = value

        chunked(width, w, STEP_COLUMNS, gates_too)
        copy = pltpu.make_async_copy(eg.at[:, w], r.emb_grad_hbm.at[:, w], r.eg_sem.at[i])
        copy.start()
        stores.append(copy)

    def projector_grad():
        left = jnp.concatenate([d1[i][...] for i in tiles], axis=1)
        summed = mm_nt(r.dense[...], left)
        high = summed.astype(LOW)
        rest = (summed - high.astype(F32)).astype(LOW)
        value = jnp.zeros(r.proj.shape, F32)
        for piece in (high, rest):
            value = value + mm_nt(piece[:, 0:eh], b1[width:, :])
            value = value + mm_nt(piece[:, eh:], r.gate_tail[...])
        return value


    mine = pl.multiple_of(core * half, half)
    other = pl.multiple_of((1 - core) * half, half)
    staged = (r.st_early, r.st_middle, r.st_late, r.st_small)
    plane_in = (r.pi_early, r.pi_middle, r.pi_late, r.pi_small)
    line_out = (r.lo_early, r.lo_middle, r.lo_late, r.lo_small)
    line_in = (r.li_early, r.li_middle, r.li_late, r.li_small)
    gathered = (r.ga_early, r.ga_middle, r.ga_late, r.ga_small)

    def pair(k):
        src, dst = (
            (g_early.at[:, pl.ds(other, half)], r.in_early),
            (g_middle.at[:, pl.ds(other, half)], r.in_middle),
            (g_late.at[pl.ds(1, blk - 1), pl.ds(other, half)], r.in_late.at[pl.ds(1, blk - 1)]),
            (g_late.at[0, pl.ds(other, half)], r.in_late.at[0]),
            (g_small.at[pl.ds(other, half)], r.in_small),
        )[k]
        return remote(src, dst, r.pair_send.at[k], r.pair_recv.at[k], (sibling, me))

    def stage(kind, s):
        for top in range(0, half, PAD):
            at = slice(top, top + PAD)
            here = pl.ds(pl.multiple_of(mine + top, PAD), PAD)
            if kind == SMALL:
                staged[kind][at, :] = encode(g_small[here, :] + r.in_small[at, :])
            else:
                sums, come = ((g_early, r.in_early), (g_middle, r.in_middle), (g_late, r.in_late))[kind]
                staged[kind][s, at, :] = encode(sums[s, here, :] + come[s, at, :])

    def plane(kind, s, bb):
        at = pl.ds(pl.multiple_of((b ^ bb) * plane_rows, PAD), plane_rows)
        src = staged[kind].at[at] if kind == SMALL else staged[kind].at[s, at]
        return remote(
            src,
            plane_in[kind].at[me * 2 + b],
            r.pl_send.at[kind, s, bb],
            r.pl_recv.at[kind, s, bb],
            (at_chip(line, b ^ bb), owner(s)),
        )

    def plane_start(kind, s):
        for slot, bb in others:
            if slot == s:
                plane(kind, s, bb).start()

    def along(kind, j):
        to = lax.rem(line + j, lines)
        at = pl.ds(pl.multiple_of(to * PAD, PAD), PAD)
        return remote(
            line_out[kind].at[at],
            line_in[kind].at[line],
            r.ln_send.at[kind, j],
            r.ln_recv.at[kind, j],
            (at_chip(to, b), me),
        )

    def line_start(kind):
        for s, bb in others:
            plane(kind, s, bb).wait_recv()
        at = pl.ds(pl.multiple_of(b * plane_rows, PAD), plane_rows)
        plane_in[kind][me * 2 + b] = staged[kind][at, :] if kind == SMALL else staged[kind][0, at, :]

        for top in range(0, plane_rows, PAD):
            here = slice(top, top + PAD)
            summed = decode(plane_in[kind][0, here, :])
            for k in range(1, 2 * blk):
                summed = summed + decode(plane_in[kind][k, here, :])
            line_out[kind][here, :] = encode(summed)
        for j in range(1, lines):
            along(kind, j).start()

    def collect(kind):
        for j in range(1, lines):
            along(kind, j).wait_recv()
        line_in[kind][line] = line_out[kind][pl.ds(pl.multiple_of(line * PAD, PAD), PAD), :]
        summed = decode(line_in[kind][0])
        for k in range(1, lines):
            summed = summed + decode(line_in[kind][k])
        gathered[kind][rows_of(chip), :] = encode(summed)

    def rows_of(k):
        at = mine + lax.rem(k, 2) * plane_rows + lax.div(k, 2) * PAD
        return pl.ds(pl.multiple_of(at, PAD), PAD)

    def piece(kind, k):
        return gathered[kind].at[rows_of(k)]

    def spread(kind, j):
        to = lax.rem(chip + j, chips)
        return remote(
            piece(kind, chip),
            piece(kind, chip),
            r.ag_send.at[kind, j],
            r.ag_recv.at[kind, j],
            (to * 2 + core, me),
        )

    def forward(kind, j):
        ref = piece(kind, lax.rem(chip - j + chips, chips))
        return remote(
            ref, ref, r.fw_send.at[kind, j], r.fw_recv.at[kind, j], (sibling, me)
        )

    def spread_start(kind):
        def one(j, unused):
            spread(kind, j).start()
            return unused

        lax.fori_loop(1, chips, one, 0)
        forward(kind, 0).start()

    def pass_on(kind):
        def one(j, unused):
            spread(kind, j).wait_recv()
            forward(kind, j).start()
            return unused

        lax.fori_loop(1, chips, one, 0)

    def finish(kind):
        def one(j, unused):
            forward(kind, j).wait_recv()
            return unused

        lax.fori_loop(0, chips, one, 0)
        out_ref = (r.early_hbm, r.middle_hbm, r.late_hbm, r.small_hbm)[kind]
        copy = pltpu.make_async_copy(gathered[kind], out_ref, r.ga_sem.at[kind])
        copy.start()
        stores.append(copy)


    drive([layer_one(i, 0) for i in tiles])
    drive([layer_one_out(i, 0) for i in tiles])
    for s in range(1, experts):
        weight_copy(blk - s, 0).wait_recv()
        weight_forward(s, 0).start()
    for s in range(1, experts):
        weight_forward(s, 0).wait_recv()
        set_first(s)
        drive([layer_one(i, s) for i in tiles])
    for s in range(1, experts):
        weight_copy(blk - s, 1).wait_recv()
        weight_forward(s, 1).start()
    for s in range(1, experts):
        weight_forward(s, 1).wait_recv()
        set_rest(s)
        drive([layer_one_out(i, s) for i in tiles])
    drive([layer_two(i) for i in tiles])
    pair(0).start()
    copy = pltpu.make_async_copy(r.logit, r.logit_hbm, r.eg_sem.at[count])
    copy.start()
    stores.append(copy)

    for s in range(1, experts):
        drive([back_one(i, s) for i in tiles])
    pair(0).wait_recv()
    for s in range(experts):
        stage(EARLY, s)
        plane_start(EARLY, s)
    for s in range(1, experts):
        g_late[s] = matrix_grad(order(s), order(s) + h)
    pair(2).start()
    drive([back_one(i, 0) for i in tiles])
    pair(1).start()
    pair(2).wait_recv()
    for s in range(1, experts):
        stage(LATE, s)
        plane_start(LATE, s)
    both = matrix_grad(order(0), eh + PAD)
    g_late[0] = both[0:h, :]
    pair(3).start()
    pair(1).wait_recv()
    for s in range(experts):
        stage(MIDDLE, s)
        plane_start(MIDDLE, s)
    at = tasks * th
    for k in range(din // out):
        value = both[h:, k * out : (k + 1) * out]
        parts = [value[s : s + 1, :] for s in range(experts)]
        g_small[at : at + PAD, :] = stack_at(parts, [owner(s) for s in range(experts)], PAD)
        at += PAD
    parts = [r.acc_t[k : k + 1, :] for k in range(tasks * experts)]
    to = [t * experts + owner(s) for t in range(tasks) for s in range(experts)]
    g_small[at : at + PAD, :] = stack_at(parts, to, PAD)
    at += PAD
    finals = [jnp.sum(r.acc_f[t].T, axis=0, keepdims=True) for t in range(tasks)]
    g_small[at + PAD : at + 2 * PAD, :] = pad_to(stack_rows(finals, PAD), PAD, out)
    g_small[at + 2 * PAD :, :] = jnp.zeros((h - at - 2 * PAD, out), F32)
    g_small[at : at + PAD, :] = pad_to(projector_grad(), PAD, out)
    pair(4).start()
    pair(3).wait_recv()
    stage(LATE, 0)
    plane_start(LATE, 0)
    pair(4).wait_recv()
    stage(SMALL, 0)
    for s in range(experts):
        plane_start(SMALL, s)
    pl.semaphore_wait(r.relay, 1)
    line_start(EARLY)
    drive([input_grad(i) for i in tiles])
    line_start(MIDDLE)
    line_start(LATE)
    line_start(SMALL)
    collect(EARLY)
    spread_start(EARLY)
    collect(MIDDLE)
    spread_start(MIDDLE)
    collect(LATE)
    spread_start(LATE)
    collect(SMALL)
    spread_start(SMALL)
    pass_on(EARLY)
    finish(EARLY)
    pass_on(MIDDLE)
    finish(MIDDLE)
    pass_on(LATE)
    pass_on(SMALL)
    finish(LATE)
    finish(SMALL)

    for s in range(1, experts):
        for part in range(2):
            weight_copy(s, part).wait_send()
            weight_forward(s, part).wait_send()
    for k in range(5):
        pair(k).wait_send()
    for kind in range(4):
        for s, bb in others:
            plane(kind, s, bb).wait_send()
        for j in range(1, lines):
            along(kind, j).wait_send()

        def gone(j, unused, kind=kind):
            spread(kind, j).wait_send()
            return unused

        lax.fori_loop(1, chips, gone, 0)

        def passed(j, unused, kind=kind):
            forward(kind, j).wait_send()
            return unused

        lax.fori_loop(0, chips, passed, 0)
    for copy in stores:
        copy.wait()


def stack_at(lines, places, height):
    width = lines[0].shape[1]
    index = lax.broadcasted_iota(jnp.int32, (height, width), 0)
    value = jnp.zeros((height, width), F32)
    for line, place in zip(lines, places):
        value = jnp.where(index == place, line, value)
    return value


TILE = 512
STEP_COLUMNS = 256
HID1 = "hid1"
TILED = ("x", "d1", "d2", "hid2", "mid", "reps", "dtp", "dm1", "dm2")
LOADED = ("e1", "s1", "e2", "s2", "dense", "labels", "proj", "router", "task", "tower", "final")


def fused(blk, devices, total, emb, arrays):
    table = dict(zip(LOADED, arrays))
    by = types.SimpleNamespace(**table)
    experts, chips = blk, devices // 2
    din, h = by.e1.shape[1:]
    tasks, th, out = by.tower.shape
    width, rows = emb.shape
    eh = experts * h
    half = h // 2
    shapes = {name: (a.shape, a.dtype) for name, a in table.items()}
    shapes |= dict(
        w1=((experts, din, h), LOW),
        w2=((experts, out + h, 2 * out), LOW),
        a1=((eh + PAD, din), LOW),
        a2=((eh + PAD, out), LOW),
        b1=((din, eh), LOW),
        b2=((out, eh), LOW),
        s1t=((experts, out, h), LOW),
        s2t=((experts, out, h), LOW),
        s1n=((experts, h, out), LOW),
        s2n=((experts, h, out), LOW),
        tow=((tasks, th, out), LOW),
        tow_n=((tasks * out, tasks * th), LOW),
        fin=((tasks, th, LANES), F32),
        projt=(by.proj.shape[::-1], LOW),
        col1=((experts, width, LANES), F32),
        gate_tail=((din - width, PAD), LOW),
        col2=((tasks * experts, out, LANES), F32),
        sl1=((experts, h, rows), F32),
        out1=((experts, out, rows), F32),
        msl1=((experts, out, rows), F32),
        dmid=((out, rows), F32),
        gate1=((experts, rows), F32),
        dgate1=((experts, rows), F32),
        logit=((tasks, rows), F32),
        eg=((width, rows), F32),
        lines1=((PAD, rows), F32),
        lines2=((PAD, rows), F32),
        p2=((eh + PAD, rows), F32),
        q2=((experts, out, rows), F32),
        ms2=((experts, out, rows), F32),
        gate2=((tasks * experts, rows), F32),
        tp=((tasks * th, rows), F32),
        dr=((tasks * out, rows), F32),
        dh=((experts, h, rows), F32),
        acc_t=((PAD, out), F32),
        acc_f=((tasks, th, LANES), F32),
        g_early=((experts, h, 2 * out), F32),
        g_middle=((experts, h, out), F32),
        g_late=((experts, h, din), F32),
        g_small=((h, out), F32),
        in_early=((experts, half, 2 * out), F32),
        in_middle=((experts, half, out), F32),
        in_late=((experts, half, din), F32),
        in_small=((half, out), F32),
        st_early=((experts, half, 2 * out), CODE),
        st_middle=((experts, half, out), CODE),
        st_late=((experts, half, din), CODE),
        st_small=((half, out), CODE),
        pi_early=((2 * blk, half // 2, 2 * out), CODE),
        pi_middle=((2 * blk, half // 2, out), CODE),
        pi_late=((2 * blk, half // 2, din), CODE),
        pi_small=((2 * blk, half // 2, out), CODE),
        lo_early=((half // 2, 2 * out), CODE),
        lo_middle=((half // 2, out), CODE),
        lo_late=((half // 2, din), CODE),
        lo_small=((half // 2, out), CODE),
        li_early=((chips // 2, PAD, 2 * out), CODE),
        li_middle=((chips // 2, PAD, out), CODE),
        li_late=((chips // 2, PAD, din), CODE),
        li_small=((chips // 2, PAD, out), CODE),
        ga_early=((h, 2 * out), CODE),
        ga_middle=((h, out), CODE),
        ga_late=((h, din), CODE),
        ga_small=((h, out), CODE),    )
    count = rows // TILE
    for name, shape in zip(
        TILED,
        (
            (din,),
            (eh + PAD,),
            (eh + PAD,),
            (eh,),
            (out,),
            (tasks, out),
            (tasks * th,),
            (out,),
            (experts, out),
        ),
    ):
        shapes |= {name + str(i): ((*shape, TILE), LOW) for i in range(count)}
    shapes |= {HID1 + str(i): ((h, TILE), LOW) for i in range(count * experts)}
    semaphores = dict(
        load_sem=(len(LOADED),),
        emb_sem=(count,),
        eg_sem=(count + 1,),
        ga_sem=(4,),
        w_send=(experts, 2),
        w_recv=(experts, 2),
        wc_send=(experts, 2),
        wc_recv=(experts, 2),
        pair_send=(5,),
        pair_recv=(5,),
        pl_send=(4, experts, 2),
        pl_recv=(4, experts, 2),
        ln_send=(4, chips // 2),
        ln_recv=(4, chips // 2),
        ag_send=(4, chips),
        ag_recv=(4, chips),
        fw_send=(4, chips),
        fw_recv=(4, chips),
    )
    names = [name + "_hbm" for name in LOADED] + ["emb_hbm", "logit_hbm", "emb_grad_hbm", "early_hbm", "middle_hbm"]
    names += ["late_hbm", "small_hbm"]
    names += [*shapes, *semaphores, "relay"]
    anywhere = pl.BlockSpec(memory_space=pl.ANY)
    return pl.pallas_call(
        functools.partial(fused_kernel, total, names),
        in_specs=[anywhere] * (len(LOADED) + 1),
        out_specs=[anywhere] * 6,
        out_shape=[
            jax.ShapeDtypeStruct((tasks, rows), F32),
            jax.ShapeDtypeStruct((width, rows), F32),
            jax.ShapeDtypeStruct((h, 2 * out), CODE),
            jax.ShapeDtypeStruct((h, out), CODE),
            jax.ShapeDtypeStruct((h, din), CODE),
            jax.ShapeDtypeStruct((h, out), CODE),
        ],
        scratch_shapes=[pltpu.VMEM(shape, kind) for shape, kind in shapes.values()]
        + [pltpu.SemaphoreType.DMA(shape) for shape in semaphores.values()]
        + [pltpu.SemaphoreType.REGULAR],
        compiler_params=pltpu.CompilerParams(
            collective_id=2, has_side_effects=True, vmem_limit_bytes=60 * MIB
        ),
    )(*arrays, emb)


def halves(value):
    high = value.astype(LOW)
    return high, (value - high.astype(F32)).astype(LOW)


def gram(value, once=False):
    high, rest = halves(value)
    if once:
        return mm_nt(high, high)
    return mm_nt(
        jnp.concatenate([high, high, rest], axis=1), jnp.concatenate([high, rest, high], axis=1)
    )


def times(left, right, once=False):
    high, rest = halves(left)
    up, down = halves(right)
    if once:
        return mm(high, up)
    return mm(jnp.concatenate([high, high, rest], axis=1), jnp.concatenate([up, down, up], axis=0))


def unit(matrix):
    return matrix / (jnp.sqrt(jnp.sum(matrix * matrix)) + 1e-07)


def sweep(current, masks, once):
    number = range(len(current))
    grams = [gram(current[i], once[i]) for i in number]
    grams = [g if m is None else g * m for g, m in zip(grams, masks)]
    squares = [times(grams[i], grams[i], once[i]) for i in number]
    polys = [NS_B * g + NS_C * s for g, s in zip(grams, squares)]
    return [NS_A * current[i] + times(polys[i], current[i], once[i]) for i in number]


MUON = ("proj", "router", "task", "e1", "s1", "e2", "s2", "tower")
CHUNKS = 4


def update_kernel(coded, moved, names, *refs):
    table = dict(zip(names, refs))
    r = types.SimpleNamespace(**table)
    din, h = r.e1.shape[1:]
    out = r.s1.shape[2]
    tasks, th, _ = r.tower.shape
    experts = r.router.shape[0]
    ready = {}
    stores = []

    def load(name, k):
        ready[name] = pltpu.make_async_copy(table[name + "_hbm"], table[name], r.load_sem.at[k])
        ready[name].start()

    def store(name):
        to = r.store_sem.at[len(stores)]
        copy = pltpu.make_async_copy(table[name + "_next"], table[name + "_next_hbm"], to)
        copy.start()
        stores.append(copy)

    for k, name in enumerate(coded):
        load(name, k)
    for k, name in enumerate(MUON):
        load(name + "_m", len(coded) + k)
    passing = []
    for name in moved:
        size = table[name].shape[0] // CHUNKS if table[name].shape[0] % (8 * CHUNKS) == 0 else table[name].shape[0]
        for at in range(0, table[name].shape[0], size):
            rows = pl.ds(at, size)
            sem = r.pass_sem.at[len(passing)]
            copy = pltpu.make_async_copy(table[name + "_hbm"].at[rows], table[name].at[rows], sem)
            copy.start()
            back = pltpu.make_async_copy(table[name].at[rows], table[name + "_next_hbm"].at[rows], sem)
            passing.append((copy, back))
    rest = (*MUON, "final", "moment", "square")
    for k, name in enumerate(rest):
        load(name, len(coded) + len(MUON) + k)

    for name in coded:
        ready[name].wait()
    for name in MUON:
        ready[name + "_m"].wait()

    if len(coded) == 1:
        grads = r.full
        late, middle = grads[:, 0:din], grads[:, din : din + out]
        early, small = grads[:, din + out : din + 3 * out], grads[:, din + 3 * out :]
    else:
        late, early, middle, small = [
            jnp.concatenate(
                [decode(table[name][j * PAD : (j + 1) * PAD, :]) for j in range(h // PAD)], axis=0
            )
            for name in coded
        ]

    def renew(name, at, gradient):
        value = 0.5 * table[name + "_m"][at] + gradient
        table[name + "_m_next"][at] = value
        return value

    def settle(name, at, ortho):
        weight = table[name][at]
        scale = 0.2 * math.sqrt(max(weight.shape))
        table[name + "_next"][at] = weight * (1.0 - 0.2 * 0.1) - 0.2 * scale * ortho

    m_e1 = renew("e1", 0, late.T)
    m_s1 = renew("s1", 0, middle)
    m_e2 = renew("e2", 0, early[:, 0:out].T)
    m_s2 = renew("s2", 0, early[:, out:])

    stacked, owner = [], []
    at = 0
    for t in range(tasks):
        stacked.append(unit(renew("tower", t, small[at : at + th, :])))
        owner += [th]
        at += th
    router_rows = []
    for k in range(din // out):
        router_rows.append(small[at : at + PAD, :])
        at += PAD
    every = slice(None)
    m_router = renew("router", every, jnp.concatenate(router_rows, axis=1)[0:experts, :])
    for t in range(tasks):
        m_task = renew("task", t, small[at + t * experts : at + (t + 1) * experts, :])
        stacked.append(pad_to(unit(m_task), 8, out))
        owner += [8]
    at += PAD
    dense, width = r.proj.shape
    m_proj = renew("proj", every, small[at : at + PAD, :][0:dense, 0:width])
    stacked.append(pad_to(unit(m_proj), PAD, out))
    owner += [PAD]
    at += PAD
    grad_final = small[at : at + PAD, :][0:tasks, 0:th]
    for name in MUON:
        store(name + "_m")

    rows = sum(owner)
    down = lax.broadcasted_iota(jnp.int32, (rows, rows), 0)
    across = lax.broadcasted_iota(jnp.int32, (rows, rows), 1)
    mask = jnp.zeros((rows, rows), F32)
    at = 0
    for length in owner:
        inside = (down >= at) & (down < at + length) & (across >= at) & (across < at + length)
        mask = jnp.where(inside, 1.0, mask)
        at += length

    current = [
        unit(m_e1).T,
        unit(m_s1).T,
        unit(m_e2),
        unit(m_s2).T,
        jnp.concatenate(stacked, axis=0),
        pad_to(unit(m_router), 8, din),
    ]
    masks = [None, None, None, None, mask, None]
    for number in range(5):
        once = [number < 2 and x.shape[0] >= out and m is None for x, m in zip(current, masks)]
        current = sweep(current, masks, once)
        if number == 0:
            for copy, back in passing:
                copy.wait()
                back.start()
    x_e1, x_s1, x_e2, x_s2, x_small, x_router = current

    for name in rest:
        ready[name].wait()
    settle("e1", 0, x_e1.T)
    store("e1")
    settle("s1", 0, x_s1.T)
    settle("e2", 0, x_e2)
    settle("s2", 0, x_s2.T)
    at = 0
    for t in range(tasks):
        settle("tower", t, x_small[at : at + th, :])
        at += th
    for t in range(tasks):
        settle("task", t, x_small[at : at + experts, :])
        at += 8
    settle("proj", every, x_small[at : at + dense, 0:width])
    settle("router", every, x_router[0:experts, :])

    moment_now = 0.9 * r.moment[...] + 0.1 * grad_final
    square_now = 0.95 * r.square[...] + 0.05 * grad_final * grad_final
    corrected = moment_now / (1.0 - 0.9**STEP)
    denom = jnp.sqrt(square_now / (1.0 - 0.95**STEP)) + 1e-08
    r.moment_next[...] = moment_now
    r.square_next[...] = square_now
    r.final_next[...] = r.final[...] * (1.0 - 0.0005) - 0.25 * corrected / denom
    for name in rest:
        if name != "e1":
            store(name)
    for copy in stores:
        copy.wait()
    for copy, back in passing:
        back.wait()


def update(sums, weights, momenta, final, passed):
    taken = dict(sums)
    taken |= {name + "_m": a for name, a in zip(MUON, momenta)}
    taken |= passed
    taken |= {name: a for name, a in zip((*MUON, "final", "moment", "square"), (*weights, *final))}
    given = [name + "_m" for name in MUON] + [*MUON, "final", "moment", "square"]
    outs = [*given, *passed]
    scratch = {name: (a.shape, a.dtype) for name, a in taken.items()}
    scratch |= {name + "_next": (taken[name].shape, F32) for name in given}
    semaphores = dict(
        load_sem=(len(taken),),
        pass_sem=(CHUNKS * len(passed) + 1,),
        store_sem=(len(given),),    )
    names = [name + "_hbm" for name in taken] + [name + "_next_hbm" for name in outs]
    names += [*scratch, *semaphores]
    anywhere = pl.BlockSpec(memory_space=pl.ANY)
    results = pl.pallas_call(
        functools.partial(update_kernel, tuple(sums), tuple(passed), names),
        in_specs=[anywhere] * len(taken),
        out_specs=[anywhere] * len(outs),
        out_shape=[jax.ShapeDtypeStruct(taken[name].shape, F32) for name in outs],
        scratch_shapes=[pltpu.VMEM(shape, kind) for shape, kind in scratch.values()]
        + [pltpu.SemaphoreType.DMA(shape) for shape in semaphores.values()],
        compiler_params=pltpu.CompilerParams(vmem_limit_bytes=60 * MIB),
    )(*taken.values())
    return dict(zip(outs, results))


def on_device(
    embedded,
    dense_features,
    labels,
    projector,
    projector_momentum,
    router,
    router_momentum,
    task_router,
    task_router_momentum,
    expand_one,
    expand_one_momentum,
    shrink_one,
    shrink_one_momentum,
    expand_two,
    expand_two_momentum,
    shrink_two,
    shrink_two_momentum,
    tower_hidden,
    tower_hidden_momentum,
    tower_final,
    tower_final_moment,
    tower_final_square,
):
    devices, blk = lax.axis_size("dp"), lax.axis_size("blk")
    total = embedded.shape[0] * devices * blk

    def turn(a):
        return jnp.swapaxes(a, -1, -2)

    router_t, task_t, tower_t = turn(router), turn(task_router), turn(tower_hidden)
    examples = (turn(embedded), turn(dense_features), turn(labels))
    matrices = (expand_one, shrink_one, expand_two, shrink_two)
    small = (projector, router_t, task_t, tower_t, tower_final)
    whole = blk <= 2 and devices // 2 * PAD == expand_one.shape[2] // 2
    if whole:
        logits, embedded_grad, early, middle, late, sums = fused(
            blk, devices, float(total), examples[0], (*matrices, *examples[1:], *small)
        )
        sums = dict(late=late, early=early, middle=middle, small=sums)
        passed = dict(emb_grad=embedded_grad, logit=logits)
    else:
        everything = gather_weights(blk, *matrices)
        logits, embedded_grad, grads = compute(float(total), *examples, *small, everything)
        sums = dict(full=reduce_gradients(blk, devices, grads))
        passed = {}
    results = update(
        sums,
        [projector, router_t, task_t, expand_one, shrink_one, expand_two, shrink_two, tower_t],
        [
            projector_momentum,
            turn(router_momentum),
            turn(task_router_momentum),
            expand_one_momentum,
            shrink_one_momentum,
            expand_two_momentum,
            shrink_two_momentum,
            turn(tower_hidden_momentum),
        ],
        [tower_final, tower_final_moment, tower_final_square],
        passed,
    )
    if whole:
        embedded_grad, logits = results["emb_grad"], results["logit"]
    pairs = []
    for name in MUON:
        for value in (results[name + "_m"], results[name]):
            pairs.append(turn(value) if name in ("router", "task", "tower") else value)
    last = [results[name] for name in ("moment", "square", "final")]
    return (turn(logits), turn(embedded_grad), *pairs, *last)


def solution(mesh):
    rows, owned, whole = P(("dp", "blk"), None), P("blk", None, None), P()
    return jax.shard_map(
        on_device,
        mesh=mesh,
        in_specs=(rows,) * 3 + (whole,) * 6 + (owned,) * 8 + (whole,) * 5,
        out_specs=(rows,) * 2 + (whole,) * 6 + (owned,) * 8 + (whole,) * 5,
        check_vma=False,
    )
```

```python
import functools
import math
import types

import jax
import jax.numpy as jnp
from jax import lax
from jax.experimental import pallas as pl
from jax.experimental.pallas import tpu as pltpu
from jax.sharding import PartitionSpec as P

STEP = 5
NS_A = 3.4445
NS_B = -4.775
NS_C = 2.0315
C0 = math.sqrt(2.0 / math.pi)
C1 = C0 * 0.044715
LOW = jnp.bfloat16
F32 = jnp.float32
CODE = jnp.int16
MESH = pl.DeviceIdType.MESH
MIB = 2**20
PAD = 16
LANES = 128


def mm(a, b):
    return lax.dot_general(a, b, (((1,), (0,)), ((), ())), preferred_element_type=F32)


def mm_nt(a, b):
    return lax.dot_general(a, b, (((1,), (1,)), ((), ())), preferred_element_type=F32)


def gelu(x):
    square = x * x
    half = 0.5 * jnp.tanh(x * (C0 + C1 * square)) + 0.5
    value = x * half
    slope = half + (value - value * half) * (2.0 * C0 + 6.0 * C1 * square)
    return value, slope


def softmax_rows(logits):
    shifted = jnp.exp(logits - jnp.max(logits, axis=0, keepdims=True))
    return shifted / jnp.sum(shifted, axis=0, keepdims=True)


def stack_rows(rows, height):
    width = rows[0].shape[1]
    index = lax.broadcasted_iota(jnp.int32, (height, width), 0)
    out = jnp.zeros((height, width), F32)
    for i, row in enumerate(rows):
        out = jnp.where(index == i, row, out)
    return out


def pad_to(value, rows, columns):
    if value.shape[1] < columns:
        fill = jnp.zeros((value.shape[0], columns - value.shape[1]), F32)
        value = jnp.concatenate([value, fill], axis=1)
    if value.shape[0] < rows:
        fill = jnp.zeros((rows - value.shape[0], columns), F32)
        value = jnp.concatenate([value, fill], axis=0)
    return value


def encode(v):
    top = jnp.max(jnp.abs(v), axis=0, keepdims=True)
    power = jnp.ceil(jnp.log2(jnp.maximum(top, 1e-30)))
    whole = jnp.round(v * (16000.0 * jnp.exp2(-power))).astype(jnp.int32)
    row = lax.broadcasted_iota(jnp.int32, v.shape, 0) & 7
    bit = ((power.astype(jnp.int32) + 128) >> row) & 1
    return (2 * whole + bit).astype(CODE)


def decode(code):
    v = code.astype(jnp.int32)
    bit = v & 1
    row = lax.broadcasted_iota(jnp.int32, v.shape, 0) & 7
    power = jnp.sum((bit << row).astype(F32)[0:8], axis=0, keepdims=True) - 128.0
    return (v - bit).astype(F32) * (jnp.exp2(power) * (1.0 / 32000.0))


def weights_kernel(e1_ref, s1_ref, e2_ref, s2_ref, all_ref, send, recv, send_core, recv_core):
    blk = lax.axis_size("blk")
    dp, me = lax.axis_index("dp"), lax.axis_index("blk")
    core = lax.rem(dp, 2)
    sibling = dp + 1 - 2 * core
    rows = all_ref.shape[1]
    half = rows // 2

    barrier = pltpu.get_barrier_semaphore()
    for step in range(1, blk):
        peer = lax.rem(me + step, blk)
        pl.semaphore_signal(barrier, inc=1, device_id=(dp, peer), device_id_type=MESH)
    pl.semaphore_signal(barrier, inc=1, device_id=(sibling, me), device_id_type=MESH)
    din, out = e1_ref.shape[1], e2_ref.shape[1]
    all_ref[me, 0:din, :] = e1_ref[0].astype(LOW)
    all_ref[me, din : din + out, :] = e2_ref[0].astype(LOW)
    all_ref[me, din + out :, 0:out] = s1_ref[0].astype(LOW)
    all_ref[me, din + out :, out : 2 * out] = s2_ref[0].astype(LOW)
    pl.semaphore_wait(barrier, blk)

    mine = pl.ds(pl.multiple_of(core * half, 16), half)
    copies = []
    for step in range(1, blk):
        peer = lax.rem(me + step, blk)
        copy = pltpu.make_async_remote_copy(
            src_ref=all_ref.at[me, mine],
            dst_ref=all_ref.at[me, mine],
            send_sem=send.at[step],
            recv_sem=recv.at[step],
            device_id=(dp, peer),
            device_id_type=MESH,
        )
        copy.start()
        copies.append(copy)
    forwards = []
    for step in range(1, blk):
        source = lax.rem(me - step + blk, blk)
        copies[step - 1].wait_recv()
        copy = pltpu.make_async_remote_copy(
            src_ref=all_ref.at[source, mine],
            dst_ref=all_ref.at[source, mine],
            send_sem=send_core.at[step],
            recv_sem=recv_core.at[step],
            device_id=(sibling, me),
            device_id_type=MESH,
        )
        copy.start()
        forwards.append(copy)
    for copy in copies:
        copy.wait_send()
    for copy in forwards:
        copy.wait()


def gather_weights(blk, e1, s1, e2, s2):
    rows = e1.shape[1] + e2.shape[1] + s1.shape[1]
    return pl.pallas_call(
        weights_kernel,
        out_shape=jax.ShapeDtypeStruct((blk, rows, e1.shape[2]), LOW),
        in_specs=[pl.BlockSpec(memory_space=pltpu.VMEM)] * 4,
        out_specs=pl.BlockSpec(memory_space=pltpu.VMEM),
        scratch_shapes=[pltpu.SemaphoreType.DMA((blk,)) for _ in range(4)],
        compiler_params=pltpu.CompilerParams(
            collective_id=0, has_side_effects=True, vmem_limit_bytes=16 * MIB
        ),
    )(e1, s1, e2, s2)


def compute_kernel(
    total,
    emb_ref,
    dense_ref,
    labels_ref,
    proj_ref,
    router_ref,
    task_ref,
    tower_ref,
    final_ref,
    all_ref,
    logit_ref,
    emb_grad_ref,
    grads_ref,
    a1,
    a2,
    b1,
    b2,
    s1t,
    s2t,
    s1n,
    s2n,
    tow,
    tow_n,
    fin,
    projt,
    col1,
    col2,
    x_ref,
    d1,
    d2,
    hid1,
    hid2,
    dtp,
    acc_r,
    acc_t,
    acc_p,
    acc_tow,
    acc_f,
):
    experts, h = all_ref.shape[0], all_ref.shape[2]
    tasks, th, out = tower_ref.shape
    emb, tile = emb_ref.shape
    din = router_ref.shape[1]
    eh = experts * h
    repeat = tile // LANES
    step = pl.program_id(0)
    side = din + 3 * out

    def wide(column):
        return jnp.concatenate([column] * repeat, axis=1)

    @pl.when(step == 0)
    def _():
        for e in range(experts):
            span = slice(e * h, (e + 1) * h)
            e1 = all_ref[e, 0:din, :]
            e2 = all_ref[e, din : din + out, :]
            s1 = all_ref[e, din + out :, 0:out]
            s2 = all_ref[e, din + out :, out : 2 * out]
            a1[span, :] = e1.T
            a2[span, :] = e2.T
            b1[:, span] = e1
            b2[:, span] = e2
            s1t[e] = s1.T
            s2t[e] = s2.T
            s1n[e] = s1
            s2n[e] = s2
        router = stack_rows([router_ref[e : e + 1, :] for e in range(experts)], PAD).astype(LOW)
        a1[eh:, :] = router
        router_t = pad_to(router.astype(F32), LANES, din).T
        pairs = [task_ref[t, e : e + 1, :] for t in range(tasks) for e in range(experts)]
        task = stack_rows(pairs, PAD).astype(LOW)
        a2[eh:, :] = task
        task_t = pad_to(task.astype(F32), LANES, out).T
        for e in range(experts):
            col1[e] = jnp.broadcast_to(router_t[:, e : e + 1], (din, LANES))
        for k in range(tasks * experts):
            col2[k] = jnp.broadcast_to(task_t[:, k : k + 1], (out, LANES))
        tow_n[...] = jnp.zeros_like(tow_n)
        final_t = stack_rows([final_ref[t : t + 1, :] for t in range(tasks)], 8).T
        for t in range(tasks):
            tow[t] = tower_ref[t].astype(LOW)
            tow_n[t * out : (t + 1) * out, t * th : (t + 1) * th] = tower_ref[t].T.astype(LOW)
            fin[t] = jnp.broadcast_to(final_t[:, t : t + 1], (th, LANES))
        projt[...] = proj_ref[...].T.astype(LOW)
        grads_ref[...] = jnp.zeros_like(grads_ref)
        acc_r[...] = jnp.zeros_like(acc_r)
        acc_t[...] = jnp.zeros_like(acc_t)
        acc_p[...] = jnp.zeros_like(acc_p)
        acc_tow[...] = jnp.zeros_like(acc_tow)
        acc_f[...] = jnp.zeros_like(acc_f)

    x_ref[0:emb, :] = emb_ref[...]
    x_ref[emb:, :] = mm(projt[...], dense_ref[...]).astype(LOW)
    x = x_ref[...]
    pre1 = mm(a1[...], x)
    gate1 = softmax_rows(pre1[eh : eh + experts, :])
    mid = jnp.zeros((out, tile), F32)
    slope1, mslope1, outs1 = [], [], []
    for e in range(experts):
        value, slope = gelu(pre1[e * h : (e + 1) * h, :])
        hid1[e] = value.astype(LOW)
        slope1.append(slope)
        mixed, mslope = gelu(mm(s1t[e], hid1[e]))
        outs1.append(mixed)
        mslope1.append(mslope)
        mid = mid + gate1[e : e + 1, :] * mixed
    mid = mid.astype(LOW)

    pre2 = mm(a2[...], mid)
    gate2 = []
    for t in range(tasks):
        first = eh + t * experts
        gate2.append(softmax_rows(pre2[first : first + experts, :]))
    slope2, mslope2, outs2 = [], [], []
    rep = [jnp.zeros((out, tile), F32) for _ in range(tasks)]
    for e in range(experts):
        value, slope = gelu(pre2[e * h : (e + 1) * h, :])
        hid2[e] = value.astype(LOW)
        slope2.append(slope)
        mixed, mslope = gelu(mm(s2t[e], hid2[e]))
        outs2.append(mixed)
        mslope2.append(mslope)
        for t in range(tasks):
            rep[t] = rep[t] + gate2[t][e : e + 1, :] * mixed

    for t in range(tasks):
        rep_low = rep[t].astype(LOW)
        act, tslope = gelu(mm(tow[t], rep_low))
        weight = wide(fin[t])
        logit = jnp.sum(act * weight, axis=0, keepdims=True)
        logit_ref[t : t + 1, :] = logit
        d_logit = (jax.nn.sigmoid(logit) - labels_ref[t : t + 1, :].astype(F32)) / total
        part = act * d_logit
        lump = part[:, 0:LANES]
        for k in range(1, repeat):
            lump = lump + part[:, k * LANES : (k + 1) * LANES]
        acc_f[t] += lump
        d_tp = (tslope * (d_logit * weight)).astype(LOW)
        dtp[t * th : (t + 1) * th, :] = d_tp
        acc_tow[t] += mm_nt(d_tp, rep_low)
    d_rep = mm(tow_n[...], dtp[...])

    d_gate2 = [[None] * experts for _ in range(tasks)]
    for e in range(experts):
        d_out = jnp.zeros((out, tile), F32)
        for t in range(tasks):
            piece = d_rep[t * out : (t + 1) * out, :]
            d_out = d_out + gate2[t][e : e + 1, :] * piece
            d_gate2[t][e] = jnp.sum(outs2[e] * piece, axis=0, keepdims=True)
        d_mixed = (mslope2[e] * d_out).astype(LOW)
        grads_ref[e, :, din + 2 * out : side] += mm_nt(hid2[e], d_mixed)
        d2[e * h : (e + 1) * h, :] = (slope2[e] * mm(s2n[e], d_mixed)).astype(LOW)
    rows = []
    for t in range(tasks):
        inner = sum(gate2[t][e : e + 1, :] * d_gate2[t][e] for e in range(experts))
        for e in range(experts):
            row = gate2[t][e : e + 1, :] * (d_gate2[t][e] - inner)
            rows.append(row.astype(LOW).astype(F32))
    d2[eh:, :] = stack_rows(rows, PAD).astype(LOW)
    g2 = mm_nt(d2[...], mid)
    for e in range(experts):
        grads_ref[e, :, din + out : din + 2 * out] += g2[e * h : (e + 1) * h, :]
    acc_t[...] += g2[eh:, :]
    d_mid = mm(b2[...], d2[0:eh, :])
    for k, row in enumerate(rows):
        d_mid = d_mid + wide(col2[k]) * row

    d_gate1 = []
    for e in range(experts):
        d_gate1.append(jnp.sum(outs1[e] * d_mid, axis=0, keepdims=True))
        d_mixed = (mslope1[e] * (gate1[e : e + 1, :] * d_mid)).astype(LOW)
        grads_ref[e, :, din : din + out] += mm_nt(hid1[e], d_mixed)
        d1[e * h : (e + 1) * h, :] = (slope1[e] * mm(s1n[e], d_mixed)).astype(LOW)
    inner = sum(gate1[e : e + 1, :] * d_gate1[e] for e in range(experts))
    rows = []
    for e in range(experts):
        row = gate1[e : e + 1, :] * (d_gate1[e] - inner)
        rows.append(row.astype(LOW).astype(F32))
    d1[eh:, :] = stack_rows(rows, PAD).astype(LOW)
    g1 = mm_nt(d1[...], x)
    for e in range(experts):
        grads_ref[e, :, 0:din] += g1[e * h : (e + 1) * h, :]
    acc_r[...] += g1[eh:, :]
    d_in = mm(b1[...], d1[0:eh, :])
    for e in range(experts):
        d_in = d_in + wide(col1[e]) * rows[e]
    emb_grad_ref[...] = d_in[:emb, :]
    tail = d_in[emb:, :]
    high = tail.astype(LOW)
    rest = (tail - high.astype(F32)).astype(LOW)
    acc_p[...] += mm_nt(dense_ref[...], high) + mm_nt(dense_ref[...], rest)

    @pl.when(step == pl.num_programs(0) - 1)
    def _():
        finals = [jnp.sum(acc_f[t].T, axis=0, keepdims=True) for t in range(tasks)]
        pieces = [acc_tow[t] for t in range(tasks)]
        pieces += [acc_r[:, k * out : (k + 1) * out] for k in range(din // out)]
        pieces += [acc_t[...], pad_to(acc_p[...], PAD, out)]
        pieces += [pad_to(stack_rows(finals, PAD), PAD, out)]
        at = 0
        for piece in pieces:
            for e in range(experts):
                grads_ref[e, at : at + piece.shape[0], side:] = piece
            at += piece.shape[0]


def compute(total, emb, dense, labels, proj, router, task, tower, final, everything):
    experts, _, h = everything.shape
    tasks, th, out = tower.shape
    width, rows = emb.shape
    din = router.shape[1]
    eh = experts * h
    tile = min(rows, max(LANES, 2048 // experts))

    def full(a):
        return pl.BlockSpec(a.shape, lambda i, n=a.ndim: (0,) * n)

    def part(height):
        return pl.BlockSpec((height, tile), lambda i: (0, i))

    scratch = [
        ((eh + PAD, din), LOW),
        ((eh + PAD, out), LOW),
        ((din, eh), LOW),
        ((out, eh), LOW),
        ((experts, out, h), LOW),
        ((experts, out, h), LOW),
        ((experts, h, out), LOW),
        ((experts, h, out), LOW),
        ((tasks, th, out), LOW),
        ((tasks * out, tasks * th), LOW),
        ((tasks, th, LANES), F32),
        ((proj.shape[1], proj.shape[0]), LOW),
        ((experts, din, LANES), F32),
        ((tasks * experts, out, LANES), F32),
        ((din, tile), LOW),
        ((eh + PAD, tile), LOW),
        ((eh + PAD, tile), LOW),
        ((experts, h, tile), LOW),
        ((experts, h, tile), LOW),
        ((tasks * th, tile), LOW),
        ((PAD, din), F32),
        ((PAD, out), F32),
        (proj.shape, F32),
        ((tasks, th, out), F32),
        ((tasks, th, LANES), F32),
    ]
    small = (proj, router, task, tower, final, everything)
    return pl.pallas_call(
        functools.partial(compute_kernel, total),
        grid=(rows // tile,),
        in_specs=[part(width), part(dense.shape[0]), part(tasks)] + [full(a) for a in small],
        out_specs=[
            part(tasks),
            part(width),
            pl.BlockSpec((experts, h, din + 4 * out), lambda i: (0, 0, 0)),
        ],
        out_shape=[
            jax.ShapeDtypeStruct((tasks, rows), F32),
            jax.ShapeDtypeStruct(emb.shape, F32),
            jax.ShapeDtypeStruct((experts, h, din + 4 * out), F32),
        ],
        scratch_shapes=[pltpu.VMEM(shape, kind) for shape, kind in scratch],
        compiler_params=pltpu.CompilerParams(vmem_limit_bytes=56 * MIB),
    )(emb, dense, labels, *small)


def reduce_kernel(
    grads_ref,
    full_ref,
    pair_out,
    pair_in,
    pieces,
    landed,
    gathered,
    pair_sem,
    send,
    recv,
    spread_send,
    spread_recv,
    core_send,
    core_recv,
):
    blk, devices = lax.axis_size("blk"), lax.axis_size("dp")
    chips = devices // 2
    dp, me = lax.axis_index("dp"), lax.axis_index("blk")
    core = lax.rem(dp, 2)
    chip = lax.div(dp, 2)
    sibling = dp + 1 - 2 * core
    height, columns = pieces.shape[1:]
    half = grads_ref.shape[1] // 2
    blocks = half // height
    slots = blk * chips
    own = me * chips + chip

    def place(k):
        return (lax.rem(k, blocks) * height, lax.div(k, blocks) * columns)

    def peer(step):
        to = lax.rem(own + step, slots)
        return to, (lax.rem(to, chips) * 2 + core, lax.div(to, chips))

    def source(step):
        return lax.rem(own - step + slots, slots)

    barrier = pltpu.get_barrier_semaphore()

    def greet(step, unused):
        pl.semaphore_signal(barrier, inc=1, device_id=peer(step)[1], device_id_type=MESH)
        return unused

    lax.fori_loop(1, slots, greet, 0)
    pl.semaphore_signal(barrier, inc=1, device_id=(sibling, me), device_id_type=MESH)

    other = (1 - core) * half
    first = core * half
    for e in range(blk):

        def code(j, unused, e=e):
            at = pl.multiple_of(other + j * PAD, PAD)
            to = pl.ds(pl.multiple_of(j * PAD, PAD), PAD)
            pair_out[e, to, :] = encode(grads_ref[e, pl.ds(at, PAD), :])
            return unused

        lax.fori_loop(0, half // PAD, code, 0)
    pl.semaphore_wait(barrier, slots)

    pair = pltpu.make_async_remote_copy(
        src_ref=pair_out,
        dst_ref=pair_in,
        send_sem=pair_sem.at[0],
        recv_sem=pair_sem.at[1],
        device_id=(sibling, me),
        device_id_type=MESH,
    )
    pair.start()
    pair.wait_recv()

    def outgoing(step):
        to, device = peer(step)
        return pltpu.make_async_remote_copy(
            src_ref=pieces.at[to],
            dst_ref=landed.at[own],
            send_sem=send.at[step],
            recv_sem=recv.at[step],
            device_id=device,
            device_id_type=MESH,
        )

    def prepare(to):
        e = lax.div(to, chips)
        row, column = place(lax.rem(to, chips))
        row = pl.multiple_of(row, height)
        span = pl.ds(pl.multiple_of(column, LANES), columns)
        mine = grads_ref[e, pl.ds(pl.multiple_of(first + row, height), height), span]
        return encode(mine + decode(pair_in[e, pl.ds(row, height), span]))

    def ship(step, unused):
        to = peer(step)[0]
        pieces[to] = prepare(to)
        outgoing(step).start()
        return unused

    lax.fori_loop(1, slots, ship, 0)
    landed[own] = prepare(own)

    def arrive(step, unused):
        outgoing(step).wait_recv()
        return unused

    lax.fori_loop(1, slots, arrive, 0)

    def add(slot, partial):
        return partial + decode(landed[slot])

    summed = lax.fori_loop(0, slots, add, jnp.zeros((height, columns), F32))

    def where(k, c):
        row, column = place(k)
        row = pl.multiple_of(c * half + row, height)
        return pl.ds(row, height), pl.ds(pl.multiple_of(column, LANES), columns)

    rows_own, columns_own = where(chip, core)
    gathered[rows_own, columns_own] = encode(summed)

    def spread(step):
        to = lax.rem(chip + step, chips)
        return pltpu.make_async_remote_copy(
            src_ref=gathered.at[rows_own, columns_own],
            dst_ref=gathered.at[rows_own, columns_own],
            send_sem=spread_send.at[step],
            recv_sem=spread_recv.at[step],
            device_id=(to * 2 + core, me),
            device_id_type=MESH,
        )

    def forward(step):
        rows, span = where(lax.rem(chip - step + chips, chips), core)
        return pltpu.make_async_remote_copy(
            src_ref=gathered.at[rows, span],
            dst_ref=gathered.at[rows, span],
            send_sem=core_send.at[step],
            recv_sem=core_recv.at[step],
            device_id=(sibling, me),
            device_id_type=MESH,
        )

    def spread_start(step, unused):
        spread(step).start()
        return unused

    lax.fori_loop(1, chips, spread_start, 0)
    forward(0).start()

    def pass_on(step, unused):
        spread(step).wait_recv()
        forward(step).start()
        return unused

    lax.fori_loop(1, chips, pass_on, 0)

    def finish(step, unused):
        forward(step).wait()
        return unused

    lax.fori_loop(0, chips, finish, 0)

    def write(j, unused):
        at = pl.ds(pl.multiple_of(j * PAD, PAD), PAD)
        full_ref[at, :] = decode(gathered[at, :])
        return unused

    lax.fori_loop(0, full_ref.shape[0] // PAD, write, 0)

    pair.wait_send()

    def drain(step, unused):
        outgoing(step).wait_send()
        return unused

    lax.fori_loop(1, slots, drain, 0)

    def drain_spread(step, unused):
        spread(step).wait_send()
        return unused

    lax.fori_loop(1, chips, drain_spread, 0)


def reduce_gradients(blk, devices, grads):
    _, h, width = grads.shape
    chips = devices // 2
    blocks = h // 2 // PAD
    columns = width * blocks // chips
    slots = blk * chips
    dma = pltpu.SemaphoreType.DMA
    return pl.pallas_call(
        reduce_kernel,
        out_shape=jax.ShapeDtypeStruct((h, width), F32),
        in_specs=[pl.BlockSpec(memory_space=pltpu.VMEM)],
        out_specs=pl.BlockSpec(memory_space=pltpu.VMEM),
        scratch_shapes=[
            pltpu.VMEM((blk, h // 2, width), CODE),
            pltpu.VMEM((blk, h // 2, width), CODE),
            pltpu.VMEM((slots, PAD, columns), CODE),
            pltpu.VMEM((slots, PAD, columns), CODE),
            pltpu.VMEM((h, width), CODE),
            dma((2,)),
            dma((slots,)),
            dma((slots,)),
            dma((chips,)),
            dma((chips,)),
            dma((chips,)),
            dma((chips,)),
        ],
        compiler_params=pltpu.CompilerParams(
            collective_id=1, has_side_effects=True, vmem_limit_bytes=32 * MIB
        ),
    )(grads)


MATRIX, VECTOR = range(2)


def drive(steps):
    live = [[one, next(one), k] for k, one in enumerate(steps)]
    while live:
        due = [item for item in live if item[2] == 0]
        for item in live:
            item[2] = max(0, item[2] - 1)
        for kind in (VECTOR, MATRIX):
            for item in [item for item in due if item[1] == kind]:
                item[1] = next(item[0], None)
                due.remove(item)
        live = [item for item in live if item[1] is not None]


def put(ref, at, value, first):
    if first:
        ref[at] = value
    else:
        ref[at] += value


EARLY, MIDDLE, LATE, SMALL = range(4)


def fused_kernel(total, names, *refs):
    table = dict(zip(names, refs))
    r = types.SimpleNamespace(**table)
    blk, devices = lax.axis_size("blk"), lax.axis_size("dp")
    chips = devices // 2
    dp, me = lax.axis_index("dp"), lax.axis_index("blk")
    core, chip = lax.rem(dp, 2), lax.div(dp, 2)
    sibling = dp + 1 - 2 * core
    experts = blk
    w1, w2 = r.w1, r.w2
    din, h = w1.shape[1:]
    tasks, th, out = r.tower.shape
    width, rows = r.emb_hbm.shape
    eh = experts * h
    tile = TILE
    count = rows // tile
    half = h // 2
    tiles = range(count)

    def owner(s):
        return lax.rem(me + s, blk)

    line, b = lax.div(chip, 2), lax.rem(chip, 2)
    lines = chips // 2
    plane_rows = half // 2
    others = [(s, bb) for s in range(blk) for bb in (1, 0) if s or bb]

    def at_chip(line, b):
        return (line * 2 + b) * 2 + core

    def order(s):
        return (s + experts - 1) % experts * h

    def remote(src, dst, send, recv, device):
        return pltpu.make_async_remote_copy(
            src_ref=src,
            dst_ref=dst,
            send_sem=send,
            recv_sem=recv,
            device_id=device,
            device_id_type=MESH,
        )

    barrier = pltpu.get_barrier_semaphore()
    met = [(sibling, me), (at_chip(line ^ 1, b), me), (at_chip(line ^ 2, b), me)]
    met += [(at_chip(line, b ^ bb), owner(s)) for s, bb in others]
    for device in met:
        pl.semaphore_signal(barrier, inc=1, device_id=device, device_id_type=MESH)

    x, d1, d2, hid2, mid, reps, dtp, dm1, dm2, hid1 = [
        [table[name + str(i)] for i in range(count * (experts if name == HID1 else 1))]
        for name in (*TILED, HID1)
    ]
    loads = {}
    for k, name in enumerate(LOADED):
        loads[name] = pltpu.make_async_copy(table[name + "_hbm"], table[name], r.load_sem.at[k])
        loads[name].start()
    emb_loads = []
    for i in range(count):
        span = slice(i * tile, (i + 1) * tile)
        copy = pltpu.make_async_copy(
            r.emb_hbm.at[:, span], x[i].at[0:width], r.emb_sem.at[i]
        )
        copy.start()
        emb_loads.append(copy)

    for name in ("e1", "s1", "e2", "s2"):
        loads[name].wait()
    w1[0] = r.e1[0].astype(LOW)
    w2[0, 0:out, :] = r.e2[0].astype(LOW)
    w2[0, out:, 0:out] = r.s1[0].astype(LOW)
    w2[0, out:, out : 2 * out] = r.s2[0].astype(LOW)

    a1, a2, b1, b2 = r.a1, r.a2, r.b1, r.b2

    def set_first(s):
        e1 = w1[s]
        a1[s * h : (s + 1) * h, :] = e1.T
        b1[:, order(s) : order(s) + h] = e1

    def set_rest(s):
        e2 = w2[s, 0:out, :]
        s1, s2 = w2[s, out:, 0:out], w2[s, out:, out : 2 * out]
        a2[s * h : (s + 1) * h, :] = e2.T
        b2[:, s * h : (s + 1) * h] = e2
        r.s1t[s], r.s2t[s] = s1.T, s2.T
        r.s1n[s], r.s2n[s] = s1, s2

    pl.semaphore_wait(barrier, len(met))
    pl.semaphore_signal(r.relay, inc=1, device_id=met[1], device_id_type=MESH)

    def weight_copy(s, part):
        ref = (w1, w2)[part]
        size = ref.shape[1] // 2
        mine = pl.ds(pl.multiple_of(core * size, PAD), size)
        return remote(
            ref.at[0, mine],
            ref.at[blk - s, mine],
            r.w_send.at[s, part],
            r.w_recv.at[s, part],
            (dp, owner(s)),
        )

    def weight_forward(s, part):
        ref = (w1, w2)[part]
        size = ref.shape[1] // 2
        mine = pl.ds(pl.multiple_of(core * size, PAD), size)
        return remote(
            ref.at[s, mine],
            ref.at[s, mine],
            r.wc_send.at[s, part],
            r.wc_recv.at[s, part],
            (sibling, me),
        )

    for part in range(2):
        for s in range(1, blk):
            weight_copy(s, part).start()

    set_first(0)
    set_rest(0)
    for name in LOADED[4:]:
        loads[name].wait()
    router = stack_rows([r.router[pl.ds(owner(s), 1), :] for s in range(experts)], PAD)
    router = router.astype(LOW)
    a1[eh:, :] = router
    router_t = pad_to(router.astype(F32), LANES, din).T
    r.gate_tail[...] = router_t[width:, 0:PAD].astype(LOW)
    pairs = [r.task[t, pl.ds(owner(s), 1), :] for t in range(tasks) for s in range(experts)]
    task = stack_rows(pairs, PAD).astype(LOW)
    a2[eh:, :] = task
    task_t = pad_to(task.astype(F32), LANES, out).T
    for s in range(experts):
        r.col1[s] = jnp.broadcast_to(router_t[0:width, s : s + 1], (width, LANES))
    for k in range(tasks * experts):
        r.col2[k] = jnp.broadcast_to(task_t[:, k : k + 1], (out, LANES))
    r.tow_n[...] = jnp.zeros_like(r.tow_n)
    final_t = stack_rows([r.final[t : t + 1, :] for t in range(tasks)], 8).T
    for t in range(tasks):
        r.tow[t] = r.tower[t].astype(LOW)
        r.tow_n[t * out : (t + 1) * out, t * th : (t + 1) * th] = r.tower[t].T.astype(LOW)
        r.fin[t] = jnp.broadcast_to(final_t[:, t : t + 1], (th, LANES))
    r.projt[...] = r.proj[...].T.astype(LOW)

    sl1, out1, msl1, dmid, gate1_ref = r.sl1, r.out1, r.msl1, r.dmid, r.gate1
    p2, q2, ms2, gate2, tp, dr, dh = r.p2, r.q2, r.ms2, r.gate2, r.tp, r.dr, r.dh
    eg, lines1, lines2 = r.eg, r.lines1, r.lines2
    g_late, g_middle, g_early, g_small = r.g_late, r.g_middle, r.g_early, r.g_small
    stores = []

    def chunked(height, w, step, body):
        for left in range(w.start, w.stop, step):
            columns = slice(left, left + step)
            for top in range(0, height, PAD):
                body(slice(top, top + PAD), columns)

    def local(columns):
        left = columns.start % tile
        return slice(left, left + columns.stop - columns.start)

    def narrow(column, step):
        return jnp.concatenate([column] * (step // LANES), axis=1)

    def layer_one(i, s):
        w = slice(i * tile, (i + 1) * tile)
        yield MATRIX
        if s == 0:
            emb_loads[i].wait()
            x[i][width:, :] = mm(r.projt[...], r.dense[:, w]).astype(LOW)
            sl1[s, :, w] = mm(a1[0:h, :], x[i][...])
            gate1_ref[:, w] = softmax_rows(mm(a1[eh:, :], x[i][...])[0:experts, :])
        else:
            sl1[s, :, w] = mm(a1[s * h : (s + 1) * h, :], x[i][...])
        yield VECTOR

        def hidden(rows, columns):
            value, slope = gelu(sl1[s, rows, columns])
            hid1[s * count + i][rows, local(columns)] = value.astype(LOW)
            sl1[s, rows, columns] = slope

        chunked(h, w, STEP_COLUMNS, hidden)

    def layer_one_out(i, s):
        w = slice(i * tile, (i + 1) * tile)
        yield MATRIX
        out1[s, :, w] = mm(r.s1t[s], hid1[s * count + i][...])
        yield VECTOR

        def mixed(rows, columns):
            value, slope = gelu(out1[s, rows, columns])
            out1[s, rows, columns] = value
            msl1[s, rows, columns] = slope
            if s == experts - 1:
                total_out = gate1_ref[s : s + 1, columns] * value
                for other in range(experts - 1):
                    gate = gate1_ref[other : other + 1, columns]
                    total_out = total_out + gate * out1[other, rows, columns]
                mid[i][rows, local(columns)] = total_out.astype(LOW)

        chunked(out, w, STEP_COLUMNS, mixed)

    def layer_two(i):
        w = slice(i * tile, (i + 1) * tile)
        first = i == 0
        pairs_of = [(t, s) for t in range(tasks) for s in range(experts)]
        yield MATRIX
        p2[:, w] = mm(a2[...], mid[i][...])
        yield VECTOR
        for t in range(tasks):
            at = eh + t * experts
            gate2[t * experts : (t + 1) * experts, w] = softmax_rows(p2[at : at + experts, w])

        def hidden(rows, columns):
            value, slope = gelu(p2[rows, columns])
            hid2[i][rows, local(columns)] = value.astype(LOW)
            p2[rows, columns] = slope

        chunked(eh, w, STEP_COLUMNS, hidden)
        yield MATRIX
        for s in range(experts):
            q2[s, :, w] = mm(r.s2t[s], hid2[i][s * h : (s + 1) * h, :])
        yield VECTOR

        def mixed(rows, columns):
            rep = [None] * tasks
            for s in range(experts):
                value, slope = gelu(q2[s, rows, columns])
                q2[s, rows, columns] = value
                ms2[s, rows, columns] = slope
                for t in range(tasks):
                    k = t * experts + s
                    term = gate2[k : k + 1, columns] * value
                    rep[t] = term if s == 0 else rep[t] + term
            for t in range(tasks):
                reps[i][t, rows, local(columns)] = rep[t].astype(LOW)

        chunked(out, w, STEP_COLUMNS, mixed)
        yield MATRIX
        for t in range(tasks):
            tp[t * th : (t + 1) * th, w] = mm(r.tow[t], reps[i][t])
        yield VECTOR
        lumps = [None] * tasks
        for left in range(w.start, w.stop, STEP_COLUMNS):
            columns = slice(left, left + STEP_COLUMNS)
            for t in range(tasks):
                at = slice(t * th, (t + 1) * th)
                weight = narrow(r.fin[t], STEP_COLUMNS)
                act, slope = gelu(tp[at, columns])
                logit = jnp.sum(act * weight, axis=0, keepdims=True)
                r.logit[t : t + 1, columns] = logit
                label = r.labels[t : t + 1, columns].astype(F32)
                d_logit = (jax.nn.sigmoid(logit) - label) / total
                dtp[i][at, local(columns)] = (slope * weight * d_logit).astype(LOW)
                part = act * d_logit
                for k in range(0, STEP_COLUMNS, LANES):
                    piece = part[:, k : k + LANES]
                    lumps[t] = piece if lumps[t] is None else lumps[t] + piece
        for t in range(tasks):
            put(r.acc_f, t, lumps[t], first)
        yield MATRIX
        dr[:, w] = mm(r.tow_n[...], dtp[i][...])
        for t in range(tasks):
            span = slice(t * th, (t + 1) * th)
            put(g_small, span, mm_nt(dtp[i][span, :], reps[i][t]), first)
        yield VECTOR
        for left in range(w.start, w.stop, STEP_COLUMNS):
            columns = slice(left, left + STEP_COLUMNS)
            sums = [None] * (tasks * experts)
            for top in range(0, out, PAD):
                rows = slice(top, top + PAD)
                piece = [dr[t * out + top : t * out + top + PAD, columns] for t in range(tasks)]
                for s in range(experts):
                    value = q2[s, rows, columns]
                    d_out = None
                    for t in range(tasks):
                        k = t * experts + s
                        term = gate2[k : k + 1, columns] * piece[t]
                        d_out = term if t == 0 else d_out + term
                        part = value * piece[t]
                        sums[k] = part if top == 0 else sums[k] + part
                    slope = ms2[s, rows, columns]
                    dm2[i][s, rows, local(columns)] = (slope * d_out).astype(LOW)
            d_gate = [jnp.sum(part, axis=0, keepdims=True) for part in sums]
            lines = []
            for t in range(tasks):
                gates = [
                    gate2[t * experts + s : t * experts + s + 1, columns] for s in range(experts)
                ]
                inner = sum(gates[s] * d_gate[t * experts + s] for s in range(experts))
                for s in range(experts):
                    lines.append(gates[s] * (d_gate[t * experts + s] - inner))
            lines = stack_rows(lines, PAD).astype(LOW)
            d2[i][eh:, local(columns)] = lines
            lines2[:, columns] = lines.astype(F32)
        yield MATRIX
        for s in range(experts):
            dh[s, :, w] = mm(r.s2n[s], dm2[i][s])
        yield VECTOR

        def before(rows, columns):
            s, top = divmod(rows.start, h)
            d_hidden = dh[s, top : top + PAD, columns]
            d2[i][rows, local(columns)] = (p2[rows, columns] * d_hidden).astype(LOW)

        chunked(eh, w, STEP_COLUMNS, before)
        yield MATRIX
        for s in range(experts):
            at = (s, slice(None), slice(out, 2 * out))
            put(g_early, at, mm_nt(hid2[i][s * h : (s + 1) * h, :], dm2[i][s]), first)
        both = mm_nt(d2[i][...], mid[i][...])
        for s in range(experts):
            put(g_early, (s, slice(None), slice(0, out)), both[s * h : (s + 1) * h, :], first)
        put(r.acc_t, Ellipsis, both[eh:, :], first)
        dmid[:, w] = mm(b2[...], d2[i][0:eh, :])
        yield VECTOR

        def gates_too(rows, columns):
            value = dmid[rows, columns]
            for k in range(tasks * experts):
                line = lines2[k : k + 1, columns]
                value = value + narrow(r.col2[k, rows, :], STEP_COLUMNS) * line
            dmid[rows, columns] = value

        chunked(out, w, STEP_COLUMNS, gates_too)

    def matrix_grad(first, last):
        left = jnp.concatenate([d1[i][first:last, :] for i in tiles], axis=1)
        return mm_nt(left, jnp.concatenate([x[i][...] for i in tiles], axis=1))

    def back_one(i, s):
        w = slice(i * tile, (i + 1) * tile)
        yield VECTOR
        for left in range(w.start, w.stop, STEP_COLUMNS):
            columns = slice(left, left + STEP_COLUMNS)
            gate = gate1_ref[s : s + 1, columns]
            sums = None
            for top in range(0, out, PAD):
                rows = slice(top, top + PAD)
                d_out = dmid[rows, columns]
                part = out1[s, rows, columns] * d_out
                sums = part if top == 0 else sums + part
                slope = msl1[s, rows, columns]
                dm1[i][rows, local(columns)] = (slope * (gate * d_out)).astype(LOW)
            r.dgate1[s : s + 1, columns] = jnp.sum(sums, axis=0, keepdims=True)
            if s == 0:
                gates, d_gates = gate1_ref[:, columns], r.dgate1[:, columns]
                inner = jnp.sum(gates * d_gates, axis=0, keepdims=True)
                lines = pad_to(gates * (d_gates - inner), PAD, STEP_COLUMNS).astype(LOW)
                d1[i][eh:, local(columns)] = lines
                lines1[:, columns] = lines.astype(F32)
        yield MATRIX
        dh[s, :, w] = mm(r.s1n[s], dm1[i][...])
        put(g_middle, s, mm_nt(hid1[s * count + i][...], dm1[i][...]), i == 0)
        yield VECTOR

        def before(rows, columns):
            at = order(s) + rows.start
            d_hidden = dh[s, rows, columns]
            d_pre = (sl1[s, rows, columns] * d_hidden).astype(LOW)
            d1[i][at : at + PAD, local(columns)] = d_pre

        chunked(h, w, STEP_COLUMNS, before)

    def input_grad(i):
        w = slice(i * tile, (i + 1) * tile)
        yield MATRIX
        eg[:, w] = mm(b1[0:width, :], d1[i][0:eh, :])
        yield VECTOR

        def gates_too(rows, columns):
            value = eg[rows, columns]
            for s in range(experts):
                gate = lines1[s : s + 1, columns]
                value = value + narrow(r.col1[s, rows, :], STEP_COLUMNS) * gate
            eg[rows, columns] = value

        chunked(width, w, STEP_COLUMNS, gates_too)
        copy = pltpu.make_async_copy(eg.at[:, w], r.emb_grad_hbm.at[:, w], r.eg_sem.at[i])
        copy.start()
        stores.append(copy)

    def projector_grad():
        left = jnp.concatenate([d1[i][...] for i in tiles], axis=1)
        summed = mm_nt(r.dense[...], left)
        high = summed.astype(LOW)
        rest = (summed - high.astype(F32)).astype(LOW)
        value = jnp.zeros(r.proj.shape, F32)
        for piece in (high, rest):
            value = value + mm_nt(piece[:, 0:eh], b1[width:, :])
            value = value + mm_nt(piece[:, eh:], r.gate_tail[...])
        return value


    mine = pl.multiple_of(core * half, half)
    other = pl.multiple_of((1 - core) * half, half)
    staged = (r.st_early, r.st_middle, r.st_late, r.st_small)
    plane_in = (r.pi_early, r.pi_middle, r.pi_late, r.pi_small)
    line_out = (r.lo_early, r.lo_middle, r.lo_late, r.lo_small)
    line_in = (r.li_early, r.li_middle, r.li_late, r.li_small)
    gathered = (r.ga_early, r.ga_middle, r.ga_late, r.ga_small)

    def pair(k):
        src, dst = (
            (g_early.at[:, pl.ds(other, half)], r.in_early),
            (g_middle.at[:, pl.ds(other, half)], r.in_middle),
            (g_late.at[pl.ds(1, blk - 1), pl.ds(other, half)], r.in_late.at[pl.ds(1, blk - 1)]),
            (g_late.at[0, pl.ds(other, half)], r.in_late.at[0]),
            (g_small.at[pl.ds(other, half)], r.in_small),
        )[k]
        return remote(src, dst, r.pair_send.at[k], r.pair_recv.at[k], (sibling, me))

    def stage(kind, s):
        for top in range(0, half, PAD):
            at = slice(top, top + PAD)
            here = pl.ds(pl.multiple_of(mine + top, PAD), PAD)
            if kind == SMALL:
                staged[kind][at, :] = encode(g_small[here, :] + r.in_small[at, :])
            else:
                sums, come = ((g_early, r.in_early), (g_middle, r.in_middle), (g_late, r.in_late))[kind]
                staged[kind][s, at, :] = encode(sums[s, here, :] + come[s, at, :])

    def plane(kind, s, bb):
        at = pl.ds(pl.multiple_of((b ^ bb) * plane_rows, PAD), plane_rows)
        src = staged[kind].at[at] if kind == SMALL else staged[kind].at[s, at]
        return remote(
            src,
            plane_in[kind].at[me * 2 + b],
            r.pl_send.at[kind, s, bb],
            r.pl_recv.at[kind, s, bb],
            (at_chip(line, b ^ bb), owner(s)),
        )

    def plane_start(kind, s):
        for slot, bb in others:
            if slot == s:
                plane(kind, s, bb).start()

    def along(kind, j):
        to = lax.rem(line + j, lines)
        at = pl.ds(pl.multiple_of(to * PAD, PAD), PAD)
        return remote(
            line_out[kind].at[at],
            line_in[kind].at[line],
            r.ln_send.at[kind, j],
            r.ln_recv.at[kind, j],
            (at_chip(to, b), me),
        )

    def line_start(kind):
        for s, bb in others:
            plane(kind, s, bb).wait_recv()
        at = pl.ds(pl.multiple_of(b * plane_rows, PAD), plane_rows)
        plane_in[kind][me * 2 + b] = staged[kind][at, :] if kind == SMALL else staged[kind][0, at, :]

        for top in range(0, plane_rows, PAD):
            here = slice(top, top + PAD)
            summed = decode(plane_in[kind][0, here, :])
            for k in range(1, 2 * blk):
                summed = summed + decode(plane_in[kind][k, here, :])
            line_out[kind][here, :] = encode(summed)
        for j in range(1, lines):
            along(kind, j).start()

    def collect(kind):
        for j in range(1, lines):
            along(kind, j).wait_recv()
        line_in[kind][line] = line_out[kind][pl.ds(pl.multiple_of(line * PAD, PAD), PAD), :]
        summed = decode(line_in[kind][0])
        for k in range(1, lines):
            summed = summed + decode(line_in[kind][k])
        gathered[kind][rows_of(chip), :] = encode(summed)

    def rows_of(k):
        at = mine + lax.rem(k, 2) * plane_rows + lax.div(k, 2) * PAD
        return pl.ds(pl.multiple_of(at, PAD), PAD)

    def piece(kind, k):
        return gathered[kind].at[rows_of(k)]

    def spread(kind, j):
        to = lax.rem(chip + j, chips)
        return remote(
            piece(kind, chip),
            piece(kind, chip),
            r.ag_send.at[kind, j],
            r.ag_recv.at[kind, j],
            (to * 2 + core, me),
        )

    def forward(kind, j):
        ref = piece(kind, lax.rem(chip - j + chips, chips))
        return remote(
            ref, ref, r.fw_send.at[kind, j], r.fw_recv.at[kind, j], (sibling, me)
        )

    def spread_start(kind):
        def one(j, unused):
            spread(kind, j).start()
            return unused

        lax.fori_loop(1, chips, one, 0)
        forward(kind, 0).start()

    def pass_on(kind):
        def one(j, unused):
            spread(kind, j).wait_recv()
            forward(kind, j).start()
            return unused

        lax.fori_loop(1, chips, one, 0)

    def finish(kind):
        def one(j, unused):
            forward(kind, j).wait_recv()
            return unused

        lax.fori_loop(0, chips, one, 0)
        out_ref = (r.early_hbm, r.middle_hbm, r.late_hbm, r.small_hbm)[kind]
        copy = pltpu.make_async_copy(gathered[kind], out_ref, r.ga_sem.at[kind])
        copy.start()
        stores.append(copy)


    drive([layer_one(i, 0) for i in tiles])
    drive([layer_one_out(i, 0) for i in tiles])
    for s in range(1, experts):
        weight_copy(blk - s, 0).wait_recv()
        weight_forward(s, 0).start()
    for s in range(1, experts):
        weight_forward(s, 0).wait_recv()
        set_first(s)
        drive([layer_one(i, s) for i in tiles[: 1]])
    for s in range(1, experts):
        weight_copy(blk - s, 1).wait_recv()
        weight_forward(s, 1).start()
    for s in range(1, experts):
        drive([layer_one(i, s) for i in tiles[1:]])
    for s in range(1, experts):
        weight_forward(s, 1).wait_recv()
        set_rest(s)
        drive([layer_one_out(i, s) for i in tiles])
    drive([layer_two(i) for i in tiles])
    pair(0).start()
    copy = pltpu.make_async_copy(r.logit, r.logit_hbm, r.eg_sem.at[count])
    copy.start()
    stores.append(copy)

    for s in range(1, experts):
        drive([back_one(i, s) for i in tiles])
    pair(0).wait_recv()
    for s in range(experts):
        stage(EARLY, s)
        plane_start(EARLY, s)
    for s in range(1, experts):
        g_late[s] = matrix_grad(order(s), order(s) + h)
    pair(2).start()
    drive([back_one(i, 0) for i in tiles])
    pair(1).start()
    pair(2).wait_recv()
    for s in range(1, experts):
        stage(LATE, s)
        plane_start(LATE, s)
    both = matrix_grad(order(0), eh + PAD)
    g_late[0] = both[0:h, :]
    pair(3).start()
    pair(1).wait_recv()
    for s in range(experts):
        stage(MIDDLE, s)
        plane_start(MIDDLE, s)
    at = tasks * th
    for k in range(din // out):
        value = both[h:, k * out : (k + 1) * out]
        parts = [value[s : s + 1, :] for s in range(experts)]
        g_small[at : at + PAD, :] = stack_at(parts, [owner(s) for s in range(experts)], PAD)
        at += PAD
    parts = [r.acc_t[k : k + 1, :] for k in range(tasks * experts)]
    to = [t * experts + owner(s) for t in range(tasks) for s in range(experts)]
    g_small[at : at + PAD, :] = stack_at(parts, to, PAD)
    at += PAD
    finals = [jnp.sum(r.acc_f[t].T, axis=0, keepdims=True) for t in range(tasks)]
    g_small[at + PAD : at + 2 * PAD, :] = pad_to(stack_rows(finals, PAD), PAD, out)
    g_small[at + 2 * PAD :, :] = jnp.zeros((h - at - 2 * PAD, out), F32)
    g_small[at : at + PAD, :] = pad_to(projector_grad(), PAD, out)
    pair(4).start()
    pair(3).wait_recv()
    stage(LATE, 0)
    plane_start(LATE, 0)
    pair(4).wait_recv()
    stage(SMALL, 0)
    for s in range(experts):
        plane_start(SMALL, s)
    pl.semaphore_wait(r.relay, 1)
    line_start(EARLY)
    drive([input_grad(i) for i in tiles])
    line_start(MIDDLE)
    line_start(LATE)
    line_start(SMALL)
    collect(EARLY)
    spread_start(EARLY)
    collect(MIDDLE)
    spread_start(MIDDLE)
    collect(LATE)
    spread_start(LATE)
    collect(SMALL)
    spread_start(SMALL)
    pass_on(EARLY)
    finish(EARLY)
    pass_on(MIDDLE)
    finish(MIDDLE)
    pass_on(LATE)
    pass_on(SMALL)
    finish(LATE)
    finish(SMALL)

    for s in range(1, experts):
        for part in range(2):
            weight_copy(s, part).wait_send()
            weight_forward(s, part).wait_send()
    for k in range(5):
        pair(k).wait_send()
    for kind in range(4):
        for s, bb in others:
            plane(kind, s, bb).wait_send()
        for j in range(1, lines):
            along(kind, j).wait_send()

        def gone(j, unused, kind=kind):
            spread(kind, j).wait_send()
            return unused

        lax.fori_loop(1, chips, gone, 0)

        def passed(j, unused, kind=kind):
            forward(kind, j).wait_send()
            return unused

        lax.fori_loop(0, chips, passed, 0)
    for copy in stores:
        copy.wait()


def stack_at(lines, places, height):
    width = lines[0].shape[1]
    index = lax.broadcasted_iota(jnp.int32, (height, width), 0)
    value = jnp.zeros((height, width), F32)
    for line, place in zip(lines, places):
        value = jnp.where(index == place, line, value)
    return value


TILE = 512
STEP_COLUMNS = 256
HID1 = "hid1"
TILED = ("x", "d1", "d2", "hid2", "mid", "reps", "dtp", "dm1", "dm2")
LOADED = ("e1", "s1", "e2", "s2", "dense", "labels", "proj", "router", "task", "tower", "final")


def fused(blk, devices, total, emb, arrays):
    table = dict(zip(LOADED, arrays))
    by = types.SimpleNamespace(**table)
    experts, chips = blk, devices // 2
    din, h = by.e1.shape[1:]
    tasks, th, out = by.tower.shape
    width, rows = emb.shape
    eh = experts * h
    half = h // 2
    shapes = {name: (a.shape, a.dtype) for name, a in table.items()}
    shapes |= dict(
        w1=((experts, din, h), LOW),
        w2=((experts, out + h, 2 * out), LOW),
        a1=((eh + PAD, din), LOW),
        a2=((eh + PAD, out), LOW),
        b1=((din, eh), LOW),
        b2=((out, eh), LOW),
        s1t=((experts, out, h), LOW),
        s2t=((experts, out, h), LOW),
        s1n=((experts, h, out), LOW),
        s2n=((experts, h, out), LOW),
        tow=((tasks, th, out), LOW),
        tow_n=((tasks * out, tasks * th), LOW),
        fin=((tasks, th, LANES), F32),
        projt=(by.proj.shape[::-1], LOW),
        col1=((experts, width, LANES), F32),
        gate_tail=((din - width, PAD), LOW),
        col2=((tasks * experts, out, LANES), F32),
        sl1=((experts, h, rows), F32),
        out1=((experts, out, rows), F32),
        msl1=((experts, out, rows), F32),
        dmid=((out, rows), F32),
        gate1=((experts, rows), F32),
        dgate1=((experts, rows), F32),
        logit=((tasks, rows), F32),
        eg=((width, rows), F32),
        lines1=((PAD, rows), F32),
        lines2=((PAD, rows), F32),
        p2=((eh + PAD, rows), F32),
        q2=((experts, out, rows), F32),
        ms2=((experts, out, rows), F32),
        gate2=((tasks * experts, rows), F32),
        tp=((tasks * th, rows), F32),
        dr=((tasks * out, rows), F32),
        dh=((experts, h, rows), F32),
        acc_t=((PAD, out), F32),
        acc_f=((tasks, th, LANES), F32),
        g_early=((experts, h, 2 * out), F32),
        g_middle=((experts, h, out), F32),
        g_late=((experts, h, din), F32),
        g_small=((h, out), F32),
        in_early=((experts, half, 2 * out), F32),
        in_middle=((experts, half, out), F32),
        in_late=((experts, half, din), F32),
        in_small=((half, out), F32),
        st_early=((experts, half, 2 * out), CODE),
        st_middle=((experts, half, out), CODE),
        st_late=((experts, half, din), CODE),
        st_small=((half, out), CODE),
        pi_early=((2 * blk, half // 2, 2 * out), CODE),
        pi_middle=((2 * blk, half // 2, out), CODE),
        pi_late=((2 * blk, half // 2, din), CODE),
        pi_small=((2 * blk, half // 2, out), CODE),
        lo_early=((half // 2, 2 * out), CODE),
        lo_middle=((half // 2, out), CODE),
        lo_late=((half // 2, din), CODE),
        lo_small=((half // 2, out), CODE),
        li_early=((chips // 2, PAD, 2 * out), CODE),
        li_middle=((chips // 2, PAD, out), CODE),
        li_late=((chips // 2, PAD, din), CODE),
        li_small=((chips // 2, PAD, out), CODE),
        ga_early=((h, 2 * out), CODE),
        ga_middle=((h, out), CODE),
        ga_late=((h, din), CODE),
        ga_small=((h, out), CODE),
    )
    count = rows // TILE
    for name, shape in zip(
        TILED,
        (
            (din,),
            (eh + PAD,),
            (eh + PAD,),
            (eh,),
            (out,),
            (tasks, out),
            (tasks * th,),
            (out,),
            (experts, out),
        ),
    ):
        shapes |= {name + str(i): ((*shape, TILE), LOW) for i in range(count)}
    shapes |= {HID1 + str(i): ((h, TILE), LOW) for i in range(count * experts)}
    semaphores = dict(
        load_sem=(len(LOADED),),
        emb_sem=(count,),
        eg_sem=(count + 1,),
        ga_sem=(4,),
        w_send=(experts, 2),
        w_recv=(experts, 2),
        wc_send=(experts, 2),
        wc_recv=(experts, 2),
        pair_send=(5,),
        pair_recv=(5,),
        pl_send=(4, experts, 2),
        pl_recv=(4, experts, 2),
        ln_send=(4, chips // 2),
        ln_recv=(4, chips // 2),
        ag_send=(4, chips),
        ag_recv=(4, chips),
        fw_send=(4, chips),
        fw_recv=(4, chips),
    )
    names = [name + "_hbm" for name in LOADED] + ["emb_hbm", "logit_hbm", "emb_grad_hbm", "early_hbm", "middle_hbm"]
    names += ["late_hbm", "small_hbm"]
    names += [*shapes, *semaphores, "relay"]
    anywhere = pl.BlockSpec(memory_space=pl.ANY)
    return pl.pallas_call(
        functools.partial(fused_kernel, total, names),
        in_specs=[anywhere] * (len(LOADED) + 1),
        out_specs=[anywhere] * 6,
        out_shape=[
            jax.ShapeDtypeStruct((tasks, rows), F32),
            jax.ShapeDtypeStruct((width, rows), F32),
            jax.ShapeDtypeStruct((h, 2 * out), CODE),
            jax.ShapeDtypeStruct((h, out), CODE),
            jax.ShapeDtypeStruct((h, din), CODE),
            jax.ShapeDtypeStruct((h, out), CODE),
        ],
        scratch_shapes=[pltpu.VMEM(shape, kind) for shape, kind in shapes.values()]
        + [pltpu.SemaphoreType.DMA(shape) for shape in semaphores.values()]
        + [pltpu.SemaphoreType.REGULAR],
        compiler_params=pltpu.CompilerParams(
            collective_id=2, has_side_effects=True, vmem_limit_bytes=60 * MIB
        ),
    )(*arrays, emb)


def halves(value):
    high = value.astype(LOW)
    return high, (value - high.astype(F32)).astype(LOW)


def gram(value, once=False):
    high, rest = halves(value)
    if once:
        return mm_nt(high, high)
    return mm_nt(
        jnp.concatenate([high, high, rest], axis=1), jnp.concatenate([high, rest, high], axis=1)
    )


def times(left, right, once=False):
    high, rest = halves(left)
    up, down = halves(right)
    if once:
        return mm(high, up)
    return mm(jnp.concatenate([high, high, rest], axis=1), jnp.concatenate([up, down, up], axis=0))


def unit(matrix):
    return matrix / (jnp.sqrt(jnp.sum(matrix * matrix)) + 1e-07)


def sweep(current, masks, once):
    number = range(len(current))
    grams = [gram(current[i], once[i]) for i in number]
    grams = [g if m is None else g * m for g, m in zip(grams, masks)]
    squares = [times(grams[i], grams[i], once[i]) for i in number]
    polys = [NS_B * g + NS_C * s for g, s in zip(grams, squares)]
    return [NS_A * current[i] + times(polys[i], current[i], once[i]) for i in number]


MUON = ("proj", "router", "task", "e1", "s1", "e2", "s2", "tower")
CHUNKS = 4


def update_kernel(coded, moved, names, *refs):
    table = dict(zip(names, refs))
    r = types.SimpleNamespace(**table)
    din, h = r.e1.shape[1:]
    out = r.s1.shape[2]
    tasks, th, _ = r.tower.shape
    experts = r.router.shape[0]
    ready = {}
    stores = []

    def load(name, k):
        ready[name] = pltpu.make_async_copy(table[name + "_hbm"], table[name], r.load_sem.at[k])
        ready[name].start()

    def store(name):
        to = r.store_sem.at[len(stores)]
        copy = pltpu.make_async_copy(table[name + "_next"], table[name + "_next_hbm"], to)
        copy.start()
        stores.append(copy)

    for k, name in enumerate(coded):
        load(name, k)
    for k, name in enumerate(MUON):
        load(name + "_m", len(coded) + k)
    passing = []
    for name in moved:
        size = table[name].shape[0] // CHUNKS if table[name].shape[0] % (8 * CHUNKS) == 0 else table[name].shape[0]
        for at in range(0, table[name].shape[0], size):
            rows = pl.ds(at, size)
            sem = r.pass_sem.at[len(passing)]
            copy = pltpu.make_async_copy(table[name + "_hbm"].at[rows], table[name].at[rows], sem)
            copy.start()
            back = pltpu.make_async_copy(table[name].at[rows], table[name + "_next_hbm"].at[rows], sem)
            passing.append((copy, back))
    rest = (*MUON, "final", "moment", "square")
    for k, name in enumerate(rest):
        load(name, len(coded) + len(MUON) + k)

    for name in coded:
        ready[name].wait()
    for name in MUON:
        ready[name + "_m"].wait()

    if len(coded) == 1:
        grads = r.full
        late, middle = grads[:, 0:din], grads[:, din : din + out]
        early, small = grads[:, din + out : din + 3 * out], grads[:, din + 3 * out :]
    else:
        late, early, middle, small = [
            jnp.concatenate(
                [decode(table[name][j * PAD : (j + 1) * PAD, :]) for j in range(h // PAD)], axis=0
            )
            for name in coded
        ]

    def renew(name, at, gradient):
        value = 0.5 * table[name + "_m"][at] + gradient
        table[name + "_m_next"][at] = value
        return value

    def settle(name, at, ortho):
        weight = table[name][at]
        scale = 0.2 * math.sqrt(max(weight.shape))
        table[name + "_next"][at] = weight * (1.0 - 0.2 * 0.1) - 0.2 * scale * ortho

    m_e1 = renew("e1", 0, late.T)
    m_s1 = renew("s1", 0, middle)
    m_e2 = renew("e2", 0, early[:, 0:out].T)
    m_s2 = renew("s2", 0, early[:, out:])

    stacked, owner = [], []
    at = 0
    for t in range(tasks):
        stacked.append(unit(renew("tower", t, small[at : at + th, :])))
        owner += [th]
        at += th
    router_rows = []
    for k in range(din // out):
        router_rows.append(small[at : at + PAD, :])
        at += PAD
    every = slice(None)
    m_router = renew("router", every, jnp.concatenate(router_rows, axis=1)[0:experts, :])
    for t in range(tasks):
        m_task = renew("task", t, small[at + t * experts : at + (t + 1) * experts, :])
        stacked.append(pad_to(unit(m_task), 8, out))
        owner += [8]
    at += PAD
    dense, width = r.proj.shape
    m_proj = renew("proj", every, small[at : at + PAD, :][0:dense, 0:width])
    stacked.append(pad_to(unit(m_proj), PAD, out))
    owner += [PAD]
    at += PAD
    grad_final = small[at : at + PAD, :][0:tasks, 0:th]
    for name in MUON:
        store(name + "_m")

    rows = sum(owner)
    down = lax.broadcasted_iota(jnp.int32, (rows, rows), 0)
    across = lax.broadcasted_iota(jnp.int32, (rows, rows), 1)
    mask = jnp.zeros((rows, rows), F32)
    at = 0
    for length in owner:
        inside = (down >= at) & (down < at + length) & (across >= at) & (across < at + length)
        mask = jnp.where(inside, 1.0, mask)
        at += length

    current = [
        unit(m_e1).T,
        unit(m_s1).T,
        unit(m_e2),
        unit(m_s2).T,
        jnp.concatenate(stacked, axis=0),
        pad_to(unit(m_router), 8, din),
    ]
    masks = [None, None, None, None, mask, None]
    for number in range(5):
        once = [number < 2 and x.shape[0] >= out and m is None for x, m in zip(current, masks)]
        current = sweep(current, masks, once)
        if number == 0:
            for copy, back in passing:
                copy.wait()
                back.start()
    x_e1, x_s1, x_e2, x_s2, x_small, x_router = current

    for name in rest:
        ready[name].wait()
    settle("e1", 0, x_e1.T)
    store("e1")
    settle("s1", 0, x_s1.T)
    settle("e2", 0, x_e2)
    settle("s2", 0, x_s2.T)
    at = 0
    for t in range(tasks):
        settle("tower", t, x_small[at : at + th, :])
        at += th
    for t in range(tasks):
        settle("task", t, x_small[at : at + experts, :])
        at += 8
    settle("proj", every, x_small[at : at + dense, 0:width])
    settle("router", every, x_router[0:experts, :])

    moment_now = 0.9 * r.moment[...] + 0.1 * grad_final
    square_now = 0.95 * r.square[...] + 0.05 * grad_final * grad_final
    corrected = moment_now / (1.0 - 0.9**STEP)
    denom = jnp.sqrt(square_now / (1.0 - 0.95**STEP)) + 1e-08
    r.moment_next[...] = moment_now
    r.square_next[...] = square_now
    r.final_next[...] = r.final[...] * (1.0 - 0.0005) - 0.25 * corrected / denom
    for name in rest:
        if name != "e1":
            store(name)
    for copy in stores:
        copy.wait()
    for copy, back in passing:
        back.wait()


def update(sums, weights, momenta, final, passed):
    taken = dict(sums)
    taken |= {name + "_m": a for name, a in zip(MUON, momenta)}
    taken |= passed
    taken |= {name: a for name, a in zip((*MUON, "final", "moment", "square"), (*weights, *final))}
    given = [name + "_m" for name in MUON] + [*MUON, "final", "moment", "square"]
    outs = [*given, *passed]
    scratch = {name: (a.shape, a.dtype) for name, a in taken.items()}
    scratch |= {name + "_next": (taken[name].shape, F32) for name in given}
    semaphores = dict(
        load_sem=(len(taken),),
        pass_sem=(CHUNKS * len(passed) + 1,),
        store_sem=(len(given),),
    )
    names = [name + "_hbm" for name in taken] + [name + "_next_hbm" for name in outs]
    names += [*scratch, *semaphores]
    anywhere = pl.BlockSpec(memory_space=pl.ANY)
    results = pl.pallas_call(
        functools.partial(update_kernel, tuple(sums), tuple(passed), names),
        in_specs=[anywhere] * len(taken),
        out_specs=[anywhere] * len(outs),
        out_shape=[jax.ShapeDtypeStruct(taken[name].shape, F32) for name in outs],
        scratch_shapes=[pltpu.VMEM(shape, kind) for shape, kind in scratch.values()]
        + [pltpu.SemaphoreType.DMA(shape) for shape in semaphores.values()],
        compiler_params=pltpu.CompilerParams(vmem_limit_bytes=60 * MIB),
    )(*taken.values())
    return dict(zip(outs, results))


def on_device(
    embedded,
    dense_features,
    labels,
    projector,
    projector_momentum,
    router,
    router_momentum,
    task_router,
    task_router_momentum,
    expand_one,
    expand_one_momentum,
    shrink_one,
    shrink_one_momentum,
    expand_two,
    expand_two_momentum,
    shrink_two,
    shrink_two_momentum,
    tower_hidden,
    tower_hidden_momentum,
    tower_final,
    tower_final_moment,
    tower_final_square,
):
    devices, blk = lax.axis_size("dp"), lax.axis_size("blk")
    total = embedded.shape[0] * devices * blk

    def turn(a):
        return jnp.swapaxes(a, -1, -2)

    router_t, task_t, tower_t = turn(router), turn(task_router), turn(tower_hidden)
    examples = (turn(embedded), turn(dense_features), turn(labels))
    matrices = (expand_one, shrink_one, expand_two, shrink_two)
    small = (projector, router_t, task_t, tower_t, tower_final)
    whole = blk <= 2 and devices // 2 * PAD == expand_one.shape[2] // 2
    if whole:
        logits, embedded_grad, early, middle, late, sums = fused(
            blk, devices, float(total), examples[0], (*matrices, *examples[1:], *small)
        )
        sums = dict(late=late, early=early, middle=middle, small=sums)
        passed = dict(emb_grad=embedded_grad, logit=logits)
    else:
        everything = gather_weights(blk, *matrices)
        logits, embedded_grad, grads = compute(float(total), *examples, *small, everything)
        sums = dict(full=reduce_gradients(blk, devices, grads))
        passed = {}
    results = update(
        sums,
        [projector, router_t, task_t, expand_one, shrink_one, expand_two, shrink_two, tower_t],
        [
            projector_momentum,
            turn(router_momentum),
            turn(task_router_momentum),
            expand_one_momentum,
            shrink_one_momentum,
            expand_two_momentum,
            shrink_two_momentum,
            turn(tower_hidden_momentum),
        ],
        [tower_final, tower_final_moment, tower_final_square],
        passed,
    )
    if whole:
        embedded_grad, logits = results["emb_grad"], results["logit"]
    pairs = []
    for name in MUON:
        for value in (results[name + "_m"], results[name]):
            pairs.append(turn(value) if name in ("router", "task", "tower") else value)
    last = [results[name] for name in ("moment", "square", "final")]
    return (turn(logits), turn(embedded_grad), *pairs, *last)


def solution(mesh):
    rows, owned, whole = P(("dp", "blk"), None), P("blk", None, None), P()
    return jax.shard_map(
        on_device,
        mesh=mesh,
        in_specs=(rows,) * 3 + (whole,) * 6 + (owned,) * 8 + (whole,) * 5,
        out_specs=(rows,) * 2 + (whole,) * 6 + (owned,) * 8 + (whole,) * 5,
        check_vma=False,
    )
```
